32 devices in a mesh: expert: 8 (over z, x), fsdp: 4 (over y, core).
Axes of the slice: x: 2, y: 2, z: 4, core: 2. Of those that a mesh axis runs over, the one named last changes fastest.
Arguments:
- tokens_in: bfloat16 [8192, 768], P(('expert', 'fsdp')), may hold values from -6 to 6
- seg_ids: int32 [8192], P(('expert', 'fsdp')), may hold values from 0 to 2, as said below
- routes: int32 [8192, 2], P(('expert', 'fsdp')), may hold values from 0 to 7, all different within a row; in each aligned block of 256 rows (0 to 255, 256 to 511, ...) at most 96 rows name the same one
- buckets: int32 [1024], replicated, may hold values from 0 to 31, as said below
- attn_gain: bfloat16 [768], P('fsdp'), may hold values from 0.5 to 1.5
- w_query: bfloat16 [768, 768], P('fsdp'), may hold values from -0.3125 to 0.3125
- w_key: bfloat16 [768, 768], P('fsdp'), may hold values from -0.3125 to 0.3125
- w_value: bfloat16 [768, 768], P('fsdp'), may hold values from -0.21875 to 0.21875
- w_output: bfloat16 [768, 768], P('fsdp'), may hold values from -0.875 to 0.875
- bias_table: bfloat16 [32, 12], P('fsdp'), may hold values from -4 to 4
- ffn_gain: bfloat16 [768], P('fsdp'), may hold values from 0.5 to 1.5
- w_router: bfloat16 [768, 8], P('fsdp'), may hold values from -0.15625 to 0.15625
- w_in: bfloat16 [8, 768, 3072], P('expert'), may hold values from -0.21875 to 0.21875
- w_out: bfloat16 [8, 3072, 768], P('expert'), may hold values from -0.109375 to 0.109375
- cotangent: bfloat16 [8192, 768], P(('expert', 'fsdp')), may hold values from -6 to 6
Outputs:
- block_out: bfloat16 [8192, 768], P(('expert', 'fsdp'))
- grad_tokens: float32 [8192, 768], P(('expert', 'fsdp'))
- grad_attn_gain: float32 [768], P('fsdp')
- grad_query: float32 [768, 768], P('fsdp')
- grad_key: float32 [768, 768], P('fsdp')
- grad_value: float32 [768, 768], P('fsdp')
- grad_output: float32 [768, 768], P('fsdp')
- grad_bias_table: float32 [32, 12], P('fsdp')
- grad_ffn_gain: float32 [768], P('fsdp')
- grad_router: float32 [768, 8], P('fsdp')
- grad_w_in: float32 [8, 768, 3072], P('expert', 'fsdp')
- grad_w_out: float32 [8, 3072, 768], P('expert', 'fsdp')
The draws below stay inside these ranges and needn't reach their ends.
Inputs may be any that keep to these rules, and one draw needn't show every extreme that they name: `seg_ids`: each sequence of 1024 tokens holds three documents in order: document 0 from position 0, document 1 beginning among the first 128 positions, document 2 beginning among the last 128 positions; each has at least one token. `routes`: each row names 2 different experts; among the tokens of one device no expert is named more than 96 times. `buckets`: never falls as the distance grows; distance d has bucket d for d < 16; the largest distance has bucket 32 - 1.
All inputs are finite; a program needn't handle non-finite values.
Results may differ from the reference program's by a relative error of at most 0.023.
Values may be sent and summed in bfloat16 or wider, within the bound.
No kernel may reach another device: no remote copies, remote signals or barrier semaphores. Data moves between devices by JAX's collectives and lax.ppermute only.
A program may use at most 192 MiB of HBM per device.

```python
import math
import jax
import jax.numpy as jnp
import numpy as np
from jax import lax

D = 768
HEADS = 12
HEAD_DIM = 64
FF = 3072
BUCKETS = 32
TOP = 2
TOK_DEV = 256
SEQ = 1024
SEQS = 8
TOKENS = 8192
EXPERTS = 8
CAP = 96


def draw_seg_ids(key, part):
    key = jax.random.fold_in(key, 11)
    first_key, last_key = jax.random.split(key, 2)
    half_block = max(TOK_DEV // 2, 2)
    opening = jax.random.randint(first_key, (SEQS, 1), 1, half_block)
    closing = jax.random.randint(last_key, (SEQS, 1), SEQ - half_block, SEQ - 1)
    position = jnp.arange(SEQ, dtype=jnp.int32)[None, :]
    documents = (position >= opening).astype(jnp.int32) + (position > closing).astype(jnp.int32)
    return documents.reshape(-1).astype(jnp.int32)


def draw_buckets(key, part):
    key = jax.random.fold_in(key, 23)
    distance = jnp.arange(SEQ, dtype=jnp.int32)
    near_count = BUCKETS // 2
    stepped = (jax.random.randint(key, (SEQ,), 0, jnp.maximum(distance, 1)) < 3) & (distance >= near_count)
    farther = near_count - 1 + jnp.cumsum(stepped.astype(jnp.int32))
    result = jnp.where(distance < near_count, distance, jnp.minimum(farther, BUCKETS - 1))
    return jnp.where(distance == SEQ - 1, BUCKETS - 1, result).astype(jnp.int32)


def steps_of(stream_key, dims, shards, least, high):
    def one(axis_at, parts):
        steps = jax.random.uniform(jax.random.fold_in(jax.random.fold_in(stream_key, 6), axis_at), (parts,), jnp.float32, least / len(shards), high / len(shards))
        return jnp.repeat(jnp.exp(steps), dims[axis_at] // parts).reshape((-1,) + (1,) * (len(dims) - axis_at - 1))

    loudness = one(*shards[0])
    for cut in shards[1:]:
        loudness = loudness * one(*cut)
    return loudness


def deal_out(own_key, own, number, rows, number_of, top, most, slope):
    ranking = jax.random.permutation(own_key, number_of)
    crowded, usual = shares(number_of, rows * top, most, slope, True), shares(number_of, rows * top, most, slope, False)
    places = jnp.arange(number_of)

    def named(tallies, rotation):
        used = int((tallies > 0).sum())
        fixed = max(1, used // 4)
        passed = fixed + (places - fixed + rotation * (used - fixed)) % max(1, number_of - fixed)
        return jnp.zeros((number_of,), jnp.int32).at[ranking[jnp.where(places < fixed, places, passed)]].set(jnp.asarray(tallies, jnp.int32))

    tallies = jnp.where(number % 4 == 0, named(crowded, number // 4), named(usual, number - number // 4 - 1))
    mixed = jax.random.permutation(jax.random.fold_in(own, 3), number_of)
    giver, receiver = mixed[0:number_of // 2 * 2:2], mixed[1:number_of // 2 * 2:2]
    slack = jnp.minimum(tallies[giver] - 1, most - tallies[receiver]) // 2
    slack = jnp.where((giver == ranking[0]) | (receiver == ranking[0]) | (tallies[receiver] == 0), 0, jnp.maximum(slack, 0))
    passed = jax.random.randint(jax.random.fold_in(own, 4), (number_of // 2,), 0, 1 << 20) % (slack + 1)
    tallies = tallies.at[giver].add(-passed).at[receiver].add(passed)
    items = jnp.searchsorted(jnp.cumsum(tallies), jnp.arange(rows * top), side="right").astype(jnp.int32)
    grid = items.reshape(top, rows).T
    grid = grid[jax.random.permutation(jax.random.fold_in(own, 1), rows)]
    rotation = jax.random.randint(jax.random.fold_in(own, 2), (rows, 1), 0, top)
    return jnp.take_along_axis(grid, (jnp.arange(top)[None, :] + rotation) % top, axis=1)


def shares(number_of, total, bound, slope, full):
    loads = [(1 << 20) // math.isqrt(standing ** slope) + 1 for standing in range(1, number_of + 1)]
    largest = bound if full else min(bound, max(-(-total // number_of), total * loads[0] // sum(loads)))
    least = 1 if total - largest >= number_of - 1 else 0
    given, spare = [largest] + [least] * (number_of - 1), total - largest - least * (number_of - 1)
    while spare > 0:
        free = [i for i in range(1, number_of) if given[i] < largest] or [i for i in range(1, number_of) if given[i] < bound]
        pool, budget = sum([loads[i] for i in free]), spare
        for i in free:
            extra = min(bound - given[i], max(1, budget * loads[i] // pool), spare)
            given[i] = given[i] + extra
            spare = spare - extra
    return np.array(given)


def noise(own_key, shape, spread, reach, shards=(), held_as=jnp.bfloat16):
    array = spread * jax.random.normal(own_key, shape, jnp.float32)
    if shards:
        array = array * steps_of(own_key, shape, shards, -0.22, 0.18)
    return jnp.clip(array, -reach, reach).astype(held_as)


def setup_inputs(seed: int = 0) -> dict:
    splits = jax.random.split(jax.random.key(seed), 16)
    tokens_in = noise(splits[0], (TOKENS, D), 1.0, 6.0, ((0, 32),))
    seg_ids = draw_seg_ids(jax.random.fold_in(splits[15], 71), 0)
    routes_keys = jax.random.split(jax.random.fold_in(splits[2], 1), TOKENS // TOK_DEV)
    routes_turns = jax.random.permutation(jax.random.fold_in(splits[2], 3), TOKENS // TOK_DEV)
    routes = jax.vmap(lambda own, number: deal_out(jax.random.fold_in(splits[2], 2), own, number, TOK_DEV, EXPERTS, TOP, CAP, 1))(routes_keys, routes_turns).reshape((TOKENS, TOP))
    buckets = draw_buckets(jax.random.fold_in(splits[15], 71), 0)
    attn_gain = jnp.clip(1.0 + 0.1 * jax.random.normal(splits[4], (D,), jnp.float32), 0.5, 1.5).astype(jnp.bfloat16)
    w_query = noise(splits[5], (D, D), (D // 2) ** -0.5, 0.3125, ((0, 4),))
    w_key = noise(splits[6], (D, D), (D // 2) ** -0.5, 0.3125, ((0, 4),))
    w_value = noise(splits[7], (D, D), D ** -0.5, 0.21875, ((0, 4),))
    w_output = noise(splits[8], (D, D), (D // 16) ** -0.5, 0.875, ((0, 4),))
    bias_table = noise(splits[9], (BUCKETS, HEADS), 1.0, 4.0, ((0, 4),))
    ffn_gain = jnp.clip(1.0 + 0.1 * jax.random.normal(splits[10], (D,), jnp.float32), 0.5, 1.5).astype(jnp.bfloat16)
    w_router = noise(splits[11], (D, EXPERTS), (2 * D) ** -0.5, 0.15625, ((0, 4),))
    w_in = noise(splits[12], (EXPERTS, D, FF), D ** -0.5, 0.21875, ((0, 8),))
    w_out = noise(splits[13], (EXPERTS, FF, D), FF ** -0.5, 0.109375, ((0, 8),))
    cotangent = noise(splits[14], (TOKENS, D), 1.0, 6.0, ((0, 32),))
    return dict(tokens_in=tokens_in, seg_ids=seg_ids, routes=routes, buckets=buckets, attn_gain=attn_gain, w_query=w_query, w_key=w_key, w_value=w_value, w_output=w_output, bias_table=bias_table, ffn_gain=ffn_gain, w_router=w_router, w_in=w_in, w_out=w_out, cotangent=cotangent)


@jax.custom_vjp
def low(v):
    return lax.optimization_barrier(v.astype(jnp.bfloat16)).astype(jnp.float32)

@jax.custom_vjp
def low_back(v):
    return v

def low_keep(v):
    return (low(v), None)

def low_pass(kept, grad):
    return (grad,)

def back_keep(v):
    return (v, None)

def back_low(kept, grad):
    return (low(grad),)
low.defvjp(low_keep, low_pass)
low_back.defvjp(back_keep, back_low)
eps = 1e-06
highest = lax.Precision.HIGHEST

def product(left_side, right_side):
    return jnp.dot(left_side, right_side, precision=highest, preferred_element_type=jnp.float32)

def rms_scale(values, scales):
    return values * lax.rsqrt(lax.optimization_barrier(jnp.mean(values * values, axis=-1, keepdims=True)) + eps) * scales

def query_block(block_item, key_heads, value_heads, segments, by_distance):
    query_heads, block_start, query_segments = block_item
    row_count = query_heads.shape[0]
    scores = jnp.einsum('qhd,khd->hqk', query_heads, key_heads, precision=highest, preferred_element_type=jnp.float32) * HEAD_DIM ** (-0.5)
    distance = block_start + jnp.arange(row_count, dtype=jnp.int32)[:, None] - jnp.arange(SEQ, dtype=jnp.int32)[None, :]
    scores = low_back(scores + by_distance[:, jnp.clip(distance, 0, SEQ - 1)])
    allowed = (distance >= 0) & (query_segments[:, None] == segments[None, :])
    scores = jnp.where(allowed[None], scores, -1e+30)
    probabilities = jax.nn.softmax(scores, axis=-1)
    return jnp.einsum('hqk,khd->qhd', low(probabilities), value_heads, precision=highest, preferred_element_type=jnp.float32)

def sequence_attention(sequence_item, query_w, key_w, value_w, by_distance):
    normed, segments = sequence_item
    head_shape = (SEQ, HEADS, HEAD_DIM)
    query_heads = low_back(low(product(normed, query_w))).reshape(head_shape)
    key_heads = low_back(low(product(normed, key_w))).reshape(head_shape)
    value_heads = low_back(low(product(normed, value_w))).reshape(head_shape)
    block_rows = min(SEQ, 512)
    block_count = SEQ // block_rows
    starts = jnp.arange(block_count, dtype=jnp.int32) * block_rows
    blocks = (query_heads.reshape(block_count, block_rows, HEADS, HEAD_DIM), starts, segments.reshape(block_count, block_rows))
    attend = jax.checkpoint(query_block)
    context = lax.map(lambda block_item: attend(block_item, key_heads, value_heads, segments, by_distance), blocks)
    return context.reshape(SEQ, D)

def expert_rows(expert_item):
    buffer_rows, weight_in, weight_out = expert_item
    hidden = low_back(product(buffer_rows, weight_in))
    active = low(jax.nn.gelu(hidden, approximate=False))
    return low_back(low(product(active, weight_out)))

def reference(tokens_in, seg_ids, routes, buckets, attn_gain, w_query, w_key, w_value, w_output, bias_table, ffn_gain, w_router, w_in, w_out, cotangent):
    source_count = TOKENS // TOK_DEV
    flat_routes = routes.reshape(source_count, TOK_DEV * TOP)
    expert_hot = (flat_routes[:, :, None] == jnp.arange(EXPERTS, dtype=jnp.int32)[None, None, :]).astype(jnp.int32)
    earlier = jnp.cumsum(expert_hot, axis=1) - expert_hot
    slot_index = lax.optimization_barrier(jnp.sum(earlier * expert_hot, axis=2))
    sources = jnp.arange(source_count, dtype=jnp.int32)[:, None]
    destination = ((flat_routes * source_count + sources) * CAP + slot_index).reshape(-1).astype(jnp.int32)
    bucket_hot = (buckets[:, None] == jnp.arange(BUCKETS, dtype=jnp.int32)[None, :]).astype(jnp.float32)

    def forward(inputs, gain_attn, query_w, key_w, value_w, output_w, bias_rows, gain_ffn, router_w, expert_in, expert_out):
        normed = low(rms_scale(inputs, gain_attn))
        by_distance = product(bucket_hot, bias_rows).T
        sequences = (normed.reshape(SEQS, SEQ, D), seg_ids.reshape(SEQS, SEQ))
        context = lax.map(lambda sequence_item: sequence_attention(sequence_item, query_w, key_w, value_w, by_distance), sequences)
        context = low_back(low(context.reshape(TOKENS, D)))
        residual = inputs + low_back(product(context, output_w))
        ffn_in = low(rms_scale(residual, gain_ffn))
        logits = low_back(product(ffn_in, router_w))
        gate_weights = jax.nn.softmax(jnp.take_along_axis(logits, routes, axis=1), axis=1)
        buffer = jnp.zeros((EXPERTS * source_count * CAP, D), jnp.float32).at[destination].set(jnp.repeat(ffn_in, TOP, axis=0))
        buffer = low_back(buffer)
        produced = lax.map(jax.checkpoint(expert_rows), (buffer.reshape(EXPERTS, source_count * CAP, D), expert_in, expert_out))
        picked = produced.reshape(EXPERTS * source_count * CAP, D)[destination].reshape(TOKENS, TOP, D)
        return residual + lax.optimization_barrier(jnp.sum(gate_weights[:, :, None] * picked, axis=1))
    primals = tuple((argument.astype(jnp.float32) for argument in (tokens_in, attn_gain, w_query, w_key, w_value, w_output, bias_table, ffn_gain, w_router, w_in, w_out)))
    result, pullback = jax.vjp(forward, primals[0], primals[1], primals[2], primals[3], primals[4], primals[5], primals[6], primals[7], primals[8], primals[9], primals[10])
    gradients = pullback(cotangent.astype(jnp.float32))
    return (result.astype(jnp.bfloat16), gradients[0], gradients[1], gradients[2], gradients[3], gradients[4], gradients[5], gradients[6], gradients[7], gradients[8], gradients[9], gradients[10])
```

```python
import math

import jax
import jax.numpy as jnp
from jax import lax
from jax.experimental import pallas as pl
from jax.experimental.pallas import tpu as pltpu
from jax.sharding import PartitionSpec as P

eps = 1e-06
log2e = math.log2(math.e)
masked_score = -1e30
f32 = jnp.float32
bf16 = jnp.bfloat16
tile = 128
extra_rows = 16


def mm(left_side, right_side):
    return lax.dot_general(
        left_side, right_side, (((1,), (0,)), ((), ())), preferred_element_type=f32
    )


def mm_t(left_side, right_side):
    return lax.dot_general(
        left_side, right_side, (((1,), (1,)), ((), ())), preferred_element_type=f32
    )


def t_mm(left_side, right_side):
    return lax.dot_general(
        left_side, right_side, (((0,), (0,)), ((), ())), preferred_element_type=f32
    )


def swap(value, axis_name, axis_size, bit):
    return lax.ppermute(value, axis_name, [(i, i ^ bit) for i in range(axis_size)])


def params(megabytes=56):
    return pltpu.CompilerParams(vmem_limit_bytes=megabytes << 20)


def cost(flops, moved):
    return pl.CostEstimate(flops=int(flops) >> 8, bytes_accessed=int(moved) >> 8, transcendentals=0)


def shape_of(dims, dtype):
    return jax.ShapeDtypeStruct(dims, dtype)


def whole_spec(dims):
    return pl.BlockSpec(dims, lambda *unused: (0,) * len(dims))


def to_column(row):
    return jnp.broadcast_to(row, (tile, row.shape[1])).T


def route_kernel(capacity, routes_ref, cot_ref, map_ref, back0_ref, back1_ref, out_ref, slot_ref):
    tokens = routes_ref.shape[0]
    slots = map_ref.shape[0]
    experts = slots // capacity
    routes = routes_ref[...]
    first, second = routes[:, 0:1], routes[:, 1:2]
    numbers = lax.broadcasted_iota(jnp.int32, (tokens, experts), 1)
    hot0 = (first == numbers).astype(f32)
    hot1 = (second == numbers).astype(f32)
    rows = lax.broadcasted_iota(jnp.int32, (tokens, tokens), 0)
    cols = lax.broadcasted_iota(jnp.int32, (tokens, tokens), 1)
    before = (cols < rows).astype(f32).astype(bf16)
    earlier = mm(before, (hot0 + hot1).astype(bf16))
    slot0 = jnp.sum(hot0 * earlier, axis=1, keepdims=True)
    slot1 = jnp.sum(hot1 * (earlier + hot0), axis=1, keepdims=True)
    slot_ref[...] = jnp.concatenate([slot0, slot1], axis=1)
    dest0 = first.astype(f32) * capacity + slot0
    dest1 = second.astype(f32) * capacity + slot1
    lane_slot = lax.broadcasted_iota(jnp.int32, (tokens, slots), 1).astype(f32)
    back0_ref[...] = (lane_slot == dest0).astype(f32).astype(bf16)
    back1_ref[...] = (lane_slot == dest1).astype(f32).astype(bf16)
    row0 = jnp.broadcast_to(dest0, (tokens, tile)).T[0:1, :]
    row1 = jnp.broadcast_to(dest1, (tokens, tile)).T[0:1, :]
    row_slot = lax.broadcasted_iota(jnp.int32, (slots, tokens), 0).astype(f32)
    hot = ((row_slot == row0).astype(f32) + (row_slot == row1).astype(f32)).astype(bf16)
    map_ref[...] = hot
    rows = mm(hot, cot_ref[...]).astype(bf16)
    others = back0_ref[...].astype(f32) * second.astype(f32) + back1_ref[...].astype(f32) * first.astype(f32)
    others = jnp.broadcast_to(jnp.sum(others, axis=0, keepdims=True), (extra_rows, slots))
    width = rows.shape[1]
    for expert in range(experts):
        at = expert * capacity
        lanes = pltpu.roll(others, (slots - at) % slots, 1)[:, :tile]
        lanes = jnp.concatenate([lanes, jnp.zeros((extra_rows, width - tile), f32)], axis=1)
        out_ref[expert, :capacity, :] = rows[at : at + capacity, :]
        out_ref[expert, capacity:, :] = lanes.astype(bf16)


def route_call(routes, cotangent, capacity, experts):
    tokens, width = cotangent.shape
    slots = experts * capacity
    return pl.pallas_call(
        lambda *refs: route_kernel(capacity, *refs),
        out_shape=(
            shape_of((slots, tokens), bf16),
            shape_of((tokens, slots), bf16),
            shape_of((tokens, slots), bf16),
            shape_of((experts, capacity + extra_rows, width), bf16),
            shape_of((tokens, 2), f32),
        ),
        compiler_params=params(),
        cost_estimate=cost(2 * slots * tokens * width, 4 * slots * width),
        name="route",
    )(routes, cotangent)


def pack_call(me, weights, tokens_in, seg_row, gains, table, router, small, width):
    shards = weights[0].shape[0]
    tokens = tokens_in.shape[0]
    experts, heads = router.shape[0], table.shape[1]
    used = experts + heads + 3

    def placed(me_ref, rows):
        at = lax.broadcasted_iota(jnp.int32, (rows, width), 1)
        own = lax.broadcasted_iota(jnp.int32, (rows, width), 0) + me_ref[0] * rows
        return (at == own).astype(f32).astype(bf16)

    def kernel(me_ref, wq_ref, wk_ref, wv_ref, x_ref, seg_ref, gain_ref, table_ref, router_ref, out_ref):
        for at, ref in enumerate((wq_ref, wk_ref, wv_ref)):
            out_ref[at * shards : (at + 1) * shards, :] = ref[...]
        out_ref[3 * shards : 3 * shards + tokens, :] = x_ref[...]
        columns = placed(me_ref, shards)
        rows = [
            mm(router_ref[...], columns),
            t_mm(table_ref[...], placed(me_ref, table_ref.shape[0])),
            mm(gain_ref[...], columns),
            jnp.zeros((small - used, width), f32),
            jnp.concatenate([seg_ref[...].astype(f32), jnp.zeros((1, width - tokens), f32)], axis=1),
        ]
        out_ref[3 * shards + tokens :, :] = jnp.concatenate(rows, axis=0).astype(bf16)

    vmem = pl.BlockSpec(memory_space=pltpu.VMEM)
    return pl.pallas_call(
        kernel,
        in_specs=[pl.BlockSpec(memory_space=pltpu.SMEM)] + [vmem] * 8,
        out_shape=shape_of((3 * shards + tokens + small, width), bf16),
        compiler_params=params(),
        cost_estimate=cost(1, 4 * shards * width),
        name="pack",
    )(me, *weights, tokens_in, seg_row, gains, table, router)


def project_call(me, blocks, shards, small, bucket_window, heads, buckets, experts):
    count = len(blocks)
    rows, width = blocks[0].shape
    tokens = rows - 3 * shards - small
    seq = count * tokens
    window = bucket_window.shape[1]

    def kernel(me_ref, *refs):
        block_refs = refs[:count]
        (bucket_ref, q_ref, k_ref, v_ref, normed_ref, tok_ref, wq_ref, wk_ref, wv_ref, small_ref, bias_ref, mask_ref) = refs[count:]
        me_index = me_ref[0]
        totals = jnp.zeros((small, width), f32)
        own_docs = block_refs[0][rows - small :, :].astype(f32)[small - 1 :, :tokens]
        for offset in range(count):
            place = lax.bitwise_xor(me_index, offset)
            row = pl.multiple_of(place * shards, shards)
            for part, full_ref in enumerate((wq_ref, wk_ref, wv_ref)):
                full_ref[pl.ds(row, shards), :] = block_refs[offset][part * shards : (part + 1) * shards, :]
            token_row = pl.multiple_of(place * tokens, tokens)
            tok_ref[pl.ds(token_row, tokens), :] = block_refs[offset][3 * shards : rows - small, :]
            extra = block_refs[offset][rows - small :, :].astype(f32)
            totals = totals + extra
            docs = to_column(extra[small - 1 :, :tokens])
            docs = jnp.concatenate([docs] * (tokens // tile), axis=1)
            mask_ref[pl.ds(token_row, tokens), :] = jnp.where(docs == own_docs, 0.0, masked_score)
        small_ref[...] = totals
        gain = totals[experts + heads : experts + heads + 1, :]
        table = totals[experts : experts + heads, :buckets].astype(bf16)
        numbers = lax.broadcasted_iota(jnp.int32, (buckets, window), 0)
        hot = (numbers == bucket_ref[...]).astype(f32).astype(bf16)
        by_distance = mm(table, hot) * log2e
        by_distance = jnp.where(bucket_ref[...] < 0, masked_score, by_distance)
        for head in range(heads):
            bias_ref[head] = by_distance[head : head + 1, :]

        @pl.loop(0, count)
        def chunk(index):
            rows = pl.ds(pl.multiple_of(index * tokens, tokens), tokens)
            values = tok_ref[rows, :].astype(f32)
            inverse = lax.rsqrt(jnp.mean(values * values, axis=-1, keepdims=True) + eps)
            normed = (values * inverse * gain).astype(bf16)
            normed_ref[rows, :] = normed
            k_ref[rows, :] = mm(normed, wk_ref[...]).astype(bf16)
            v_ref[rows, :] = mm(normed, wv_ref[...]).astype(bf16)

        own = normed_ref[pl.ds(pl.multiple_of(me_index * tokens, tokens), tokens), :]
        q_ref[...] = mm(own, wq_ref[...]).astype(bf16)

    vmem = pl.BlockSpec(memory_space=pltpu.VMEM)
    return pl.pallas_call(
        kernel,
        in_specs=[pl.BlockSpec(memory_space=pltpu.SMEM)] + [vmem] * (count + 1),
        out_shape=(
            shape_of((tokens, width), bf16),
            shape_of((seq, width), bf16),
            shape_of((seq, width), bf16),
            shape_of((seq, width), bf16),
            shape_of((seq, width), bf16),
            shape_of((width, width), bf16),
            shape_of((width, width), bf16),
            shape_of((width, width), bf16),
            shape_of((small, width), f32),
            shape_of((heads, 1, window), f32),
            shape_of((seq, tokens), f32),
        ),
        compiler_params=params(),
        cost_estimate=cost(2 * width * width * (2 * seq + tokens), 20 * seq * width),
        name="project",
    )(me, *blocks, bucket_window)


def skewed(bias_row, window):
    spread = jnp.broadcast_to(bias_row, (tile, window))
    return pltpu.roll(spread, 0, 1, stride=1, stride_axis=0)


def attend_call(queries, keys, values, bias, mask, head_dim):
    tokens, width = queries.shape
    seq = keys.shape[0]
    heads, _, window = bias.shape
    pairs = width // tile
    per_step = heads // pairs
    key_blocks = seq // tile
    scale = head_dim**-0.5 * log2e

    def kernel(q_ref, k_ref, v_ref, bias_ref, mask_ref, ctx_ref, lse_ref, score_ref, prob_ref, skew_ref):
        lane = lax.broadcasted_iota(jnp.int32, (tokens, tile), 1)
        row = lax.broadcasted_iota(jnp.int32, (tile, tokens), 0)
        query = q_ref[...]
        values_t = v_ref[...].T
        result = jnp.zeros((tile, tokens), f32)
        for half in range(per_step):
            mine = jnp.where(lane // head_dim == half, query, jnp.zeros_like(query))
            skew_ref[...] = skewed(bias_ref[half], window)
            top = jnp.full((8, tokens), -3e38, f32)
            for block in range(key_blocks):
                rows = pl.ds(block * tile, tile)
                begin = tile * (key_blocks - block)
                scores = mm_t(k_ref[rows, :], mine) * scale
                scores = scores + (skew_ref[:, begin : begin + tokens] + mask_ref[rows, :])
                score_ref[rows, :] = scores
                top = jnp.maximum(top, jnp.max(scores.reshape(tile // 8, 8, tokens), axis=0))
            top = jnp.max(top, axis=0, keepdims=True)
            total = jnp.zeros((8, tokens), f32)
            for block in range(key_blocks):
                rows = pl.ds(block * tile, tile)
                probs = jnp.exp2(score_ref[rows, :] - top)
                prob_ref[rows, :] = probs.astype(bf16)
                total = total + jnp.sum(probs.reshape(tile // 8, 8, tokens), axis=0)
            total = jnp.sum(total, axis=0, keepdims=True)
            lse_ref[half] = top + jnp.log2(total)
            mixed = mm(values_t, prob_ref[...]) * (1.0 / total)
            result = jnp.where(row // head_dim == half, mixed, result)
        ctx_ref[...] = result.T

    return pl.pallas_call(
        kernel,
        grid=(pairs,),
        in_specs=[
            pl.BlockSpec((tokens, tile), lambda p: (0, p)),
            pl.BlockSpec((seq, tile), lambda p: (0, p)),
            pl.BlockSpec((seq, tile), lambda p: (0, p)),
            pl.BlockSpec((per_step, 1, window), lambda p: (p, 0, 0)),
            pl.BlockSpec((seq, tokens), lambda p: (0, 0)),
        ],
        out_specs=(
            pl.BlockSpec((tokens, tile), lambda p: (0, p)),
            pl.BlockSpec((per_step, 1, tokens), lambda p: (p, 0, 0)),
        ),
        out_shape=(shape_of((tokens, width), f32), shape_of((heads, 1, tokens), f32)),
        scratch_shapes=[
            pltpu.VMEM((seq, tokens), f32),
            pltpu.VMEM((seq, tokens), bf16),
            pltpu.VMEM((tile, window), f32),
        ],
        compiler_params=params(),
        cost_estimate=cost(16 * heads * tokens * seq * tile, 4 * seq * width),
        name="attend",
    )(queries, keys, values, bias, mask)


def unskewed(total):
    window = total.shape[1]
    rows = total.shape[0]
    while rows > 8:
        rows = rows // 2
        total = total[:rows, :] + pltpu.roll(total[rows:, :], window - rows, 1)
    step = 4
    while step:
        moved = pltpu.roll(pltpu.roll(total, 8 - step, 0), window - step, 1)
        total = total + moved
        step = step // 2
    return total[0:1, :]


def attend_back_call(queries, keys, values, bias, mask, lse, context, grad_context, bucket_window, buckets, head_dim, first, pairs):
    tokens, width = queries.shape
    seq = keys.shape[0]
    heads, _, window = bias.shape
    per_step = heads // (width // tile)
    key_blocks = seq // tile
    scale = head_dim**-0.5

    def kernel(
        q_ref, k_ref, v_ref, bias_ref, mask_ref, lse_ref, ctx_ref, grad_ref, bucket_ref,
        dq_ref, dk_ref, dv_ref, table_ref, prob_ref, ds_ref, skew_ref, sum_ref,
    ):
        lane = lax.broadcasted_iota(jnp.int32, (tokens, tile), 1)
        row = lax.broadcasted_iota(jnp.int32, (tile, tokens), 0)
        query = q_ref[...]
        grad = grad_ref[...]
        keys_t = k_ref[...].T
        products = (grad.astype(f32) * ctx_ref[...]).T
        result = jnp.zeros((tile, tokens), f32)
        numbers = lax.broadcasted_iota(jnp.int32, (buckets, window), 0)
        hot = (numbers == bucket_ref[...]).astype(f32)
        mine_q, mine_g = [], []
        for half in range(per_step):
            mine_q.append(jnp.where(lane // head_dim == half, query, jnp.zeros_like(query)))
            mine_g.append(jnp.where(lane // head_dim == half, grad, jnp.zeros_like(grad)))
        for half in range(per_step):
            delta = jnp.sum(
                products[half * head_dim : (half + 1) * head_dim, :], axis=0, keepdims=True
            )
            lse_row = lse_ref[half]
            skew_ref[...] = skewed(bias_ref[half], window)
            sum_ref[...] = jnp.zeros((tile, window), f32)
            cols = slice(half * tokens, (half + 1) * tokens)
            for block in range(key_blocks):
                rows = pl.ds(block * tile, tile)
                begin = tile * (key_blocks - block)
                scores = mm_t(k_ref[rows, :], mine_q[half]) * (scale * log2e)
                scores = scores + (skew_ref[:, begin : begin + tokens] + mask_ref[rows, :])
                probs = jnp.exp2(scores - lse_row)
                grad_probs = mm_t(v_ref[rows, :], mine_g[half])
                grad_scores = (probs * (grad_probs - delta)).astype(bf16)
                prob_ref[rows, cols] = probs.astype(bf16)
                ds_ref[rows, cols] = grad_scores
                sum_ref[:, begin : begin + tokens] += grad_scores.astype(f32)
            grad_q = mm(keys_t, ds_ref[:, cols])
            result = jnp.where(row // head_dim == half, grad_q, result)
            by_distance = unskewed(sum_ref[...])
            table_ref[half] = jnp.sum(hot * by_distance, axis=1, keepdims=True)
        dq_ref[...] = (result * scale).T.astype(bf16)
        dk_ref[...] = (mm(ds_ref[...], jnp.concatenate(mine_q, axis=0)) * scale).astype(bf16)
        dv_ref[...] = mm(prob_ref[...], jnp.concatenate(mine_g, axis=0)).astype(bf16)

    narrow = pl.BlockSpec((tokens, tile), lambda p: (0, p + first))
    tall = pl.BlockSpec((seq, tile), lambda p: (0, p + first))
    narrow_out = pl.BlockSpec((tokens, tile), lambda p: (0, p))
    tall_out = pl.BlockSpec((seq, tile), lambda p: (0, p))
    return pl.pallas_call(
        kernel,
        grid=(pairs,),
        in_specs=[
            narrow,
            tall,
            tall,
            pl.BlockSpec((per_step, 1, window), lambda p: (p + first, 0, 0)),
            pl.BlockSpec((seq, tokens), lambda p: (0, 0)),
            pl.BlockSpec((per_step, 1, tokens), lambda p: (p + first, 0, 0)),
            narrow,
            narrow,
            pl.BlockSpec((1, window), lambda p: (0, 0)),
        ],
        out_specs=(
            narrow_out,
            tall_out,
            tall_out,
            pl.BlockSpec((per_step, buckets, 1), lambda p: (p, 0, 0)),
        ),
        out_shape=(
            shape_of((tokens, pairs * tile), bf16),
            shape_of((seq, pairs * tile), bf16),
            shape_of((seq, pairs * tile), bf16),
            shape_of((pairs * per_step, buckets, 1), f32),
        ),
        scratch_shapes=[
            pltpu.VMEM((seq, per_step * tokens), bf16),
            pltpu.VMEM((seq, per_step * tokens), bf16),
            pltpu.VMEM((tile, window), f32),
            pltpu.VMEM((tile, window), f32),
        ],
        compiler_params=params(),
        cost_estimate=cost(40 * pairs * per_step * tokens * seq * tile, 8 * seq * pairs * tile),
        name="attend_back",
    )(queries, keys, values, bias, mask, lse, context, grad_context, bucket_window)


def chosen_logits(routes, logits):
    numbers = lax.broadcasted_iota(jnp.int32, logits.shape, 1)
    hot0 = routes[:, 0:1] == numbers
    hot1 = routes[:, 1:2] == numbers
    return hot0, hot1


def dispatch_call(me, context, out_blocks, tokens_in, smalls, routes, slot_map, heads):
    tokens, width = tokens_in.shape
    count = len(out_blocks)
    shards = out_blocks[0].shape[0]
    slots = slot_map.shape[0]

    def make(experts):
        def kernel(me_ref, ctx_ref, *refs):
            block_refs = refs[:count]
            (x_ref, small_ref, routes_ref, map_ref, wo_ref, low_ref, res_ref, ffn_ref, gate_ref, rows_ref) = refs[count:]
            for offset in range(count):
                place = lax.bitwise_xor(me_ref[0], offset)
                wo_ref[pl.ds(pl.multiple_of(place * shards, shards), shards), :] = block_refs[offset][...]
            context_low = ctx_ref[...].astype(bf16)
            low_ref[...] = context_low
            residual = x_ref[...].astype(f32) + mm(context_low, wo_ref[...])
            res_ref[...] = residual
            gain = small_ref[experts + heads + 1 : experts + heads + 2, :]
            inverse = lax.rsqrt(jnp.mean(residual * residual, axis=-1, keepdims=True) + eps)
            ffn_low = (residual * inverse * gain).astype(bf16)
            ffn_ref[...] = ffn_low
            rows_ref[...] = mm(map_ref[...], ffn_low).astype(bf16)
            logits = mm_t(ffn_low, small_ref[0:experts, :].astype(bf16))
            hot0, hot1 = chosen_logits(routes_ref[...], logits)
            first = jnp.sum(jnp.where(hot0, logits, 0.0), axis=1, keepdims=True)
            second = jnp.sum(jnp.where(hot1, logits, 0.0), axis=1, keepdims=True)
            top = jnp.maximum(first, second)
            weight0 = jnp.exp(first - top)
            weight1 = jnp.exp(second - top)
            whole = weight0 + weight1
            gate0 = weight0 / whole
            gate1 = weight1 / whole
            gate_ref[...] = jnp.concatenate([gate0, gate1], axis=1)

        return kernel

    def run(experts):
        vmem = pl.BlockSpec(memory_space=pltpu.VMEM)
        return pl.pallas_call(
            make(experts),
            in_specs=[pl.BlockSpec(memory_space=pltpu.SMEM)] + [vmem] * (count + 5),
            out_shape=(
                shape_of((width, width), bf16),
                shape_of((tokens, width), bf16),
                shape_of((tokens, width), f32),
                shape_of((tokens, width), bf16),
                shape_of((tokens, 2), f32),
                shape_of((slots, width), bf16),
            ),
            compiler_params=params(),
            cost_estimate=cost(4 * tokens * width * width, 8 * width * width),
            name="dispatch",
        )(me, context, *out_blocks, tokens_in, smalls, routes, slot_map)

    return run


def expert_call(rows, grads, expert_in, expert_out, experts):
    count, width = rows.shape
    capacity = count // experts
    stride = capacity + extra_rows
    hidden_width = expert_in.shape[1]
    step_width = 512
    chunk_rows = 256
    steps = hidden_width // step_width
    half_root = math.sqrt(0.5)
    density = 1.0 / math.sqrt(2.0 * math.pi)

    def kernel(x_ref, g_ref, in_ref, out_ref, active_ref, gh_ref, made_ref, back_ref, made_sum, back_sum):
        step = pl.program_id(0)

        @pl.when(step == 0)
        def start():
            made_sum[...] = jnp.zeros((count, width), f32)
            back_sum[...] = jnp.zeros((count, width), f32)

        @pl.loop(0, count // chunk_rows)
        def chunk(index):
            at = pl.ds(pl.multiple_of(index * chunk_rows, chunk_rows), chunk_rows)
            hidden = mm(x_ref[at, :], in_ref[...])
            upstream = mm_t(g_ref[at, :], out_ref[...])
            share = 0.5 + 0.5 * lax.erf(hidden * half_root)
            active = (hidden * share).astype(bf16)
            slope = share + hidden * (jnp.exp(hidden * hidden * -0.5) * density)
            grad_hidden = (upstream * slope).astype(bf16)
            active_ref[at, :] = active
            gh_ref[at, :] = grad_hidden
            made_sum[at, :] += mm(active, out_ref[...])
            back_sum[at, :] += mm_t(grad_hidden, in_ref[...])

        @pl.when(step == steps - 1)
        def finish():
            made = made_sum[...].astype(bf16)
            made_ref[...] = made
            products = made.astype(f32) * g_ref[...].astype(f32)
            folded = products[:, :tile]
            for at in range(tile, width, tile):
                folded = folded + products[:, at : at + tile]
            dots = jnp.broadcast_to(jnp.sum(folded.T, axis=0, keepdims=True), (8, count))
            coarse = dots.astype(bf16).astype(f32)
            fine = dots - coarse
            for expert in range(experts):
                at = expert * capacity
                shift = (count - at) % count
                lanes = [pltpu.roll(half, shift, 1)[:, :tile] for half in (coarse, fine)]
                lanes = jnp.concatenate(lanes, axis=0)
                lanes = jnp.concatenate([lanes, jnp.zeros((extra_rows, width - tile), f32)], axis=1)
                back_ref[expert, :capacity, :] = back_sum[at : at + capacity, :].astype(bf16)
                back_ref[expert, capacity:, :] = lanes.astype(bf16)

    full = whole_spec((count, width))
    return pl.pallas_call(
        kernel,
        grid=(steps,),
        in_specs=[
            full,
            full,
            pl.BlockSpec((width, step_width), lambda s: (0, s)),
            pl.BlockSpec((step_width, width), lambda s: (s, 0)),
        ],
        out_specs=(
            pl.BlockSpec((count, step_width), lambda s: (0, s)),
            pl.BlockSpec((count, step_width), lambda s: (0, s)),
            full,
            whole_spec((experts, stride, width)),
        ),
        out_shape=(
            shape_of((count, hidden_width), bf16),
            shape_of((count, hidden_width), bf16),
            shape_of((count, width), bf16),
            shape_of((experts, stride, width), bf16),
        ),
        scratch_shapes=[pltpu.VMEM((count, width), f32), pltpu.VMEM((count, width), f32)],
        compiler_params=params(),
        cost_estimate=cost(8 * count * width * hidden_width, 8 * width * hidden_width),
        name="experts",
    )(rows, grads, expert_in, expert_out)


def offset_place(offsets, step, me_ref):
    offset = offsets[0]
    for at in range(1, len(offsets)):
        offset = jnp.where(step == at, offsets[at], offset)
    return lax.bitwise_xor(me_ref[0], offset)


def gate_column(me_ref, rows_ref, router_ref, others_ref):
    logits = mm_t(router_ref[...].astype(bf16), rows_ref[...])
    numbers = lax.broadcasted_iota(jnp.int32, logits.shape, 0).astype(f32)
    mine = jnp.sum(jnp.where(numbers == me_ref[1].astype(f32), logits, 0.0), axis=0, keepdims=True)
    other = jnp.sum(
        jnp.where(numbers == others_ref[...].astype(f32), logits, 0.0), axis=0, keepdims=True
    )
    return to_column(1.0 / (1.0 + jnp.exp(other - mine)))[:, 0:1]


def expert_grads_call(me, rows_t, rows_in, grads, active, grad_hidden, router, others, offsets):
    width, rows = rows_t.shape
    hidden_width = grad_hidden.shape[1]
    count = len(offsets)
    half = count // 2
    in_rows, out_rows = width // count, hidden_width // count

    def kernel(
        me_ref, xt_ref, rows_ref, g_ref, active_ref, gh_ref, router_ref, others_ref,
        in_give_ref, in_keep_ref, out_give_ref, out_keep_ref, gh_scr, g_scr,
    ):
        step = pl.program_id(0)

        @pl.when(step == 0)
        def start():
            column = gate_column(me_ref, rows_ref, router_ref, others_ref)
            g_scr[...] = (g_ref[...].astype(f32) * column).astype(bf16)
            for at in range(0, hidden_width, width):
                gh_scr[:, at : at + width] = (gh_ref[:, at : at + width].astype(f32) * column).astype(bf16)

        def shard(in_ref, out_ref):
            for at in range(0, hidden_width, width):
                in_ref[0, :, at : at + width] = mm(xt_ref[...], gh_scr[:, at : at + width]).astype(bf16)
            out_ref[0] = t_mm(active_ref[...], g_scr[...]).astype(bf16)

        @pl.when(step < half)
        def first():
            shard(in_give_ref, out_give_ref)

        @pl.when(step >= half)
        def second():
            shard(in_keep_ref, out_keep_ref)

    def give_at(s, me_ref):
        return (jnp.minimum(s, half - 1), 0, 0)

    def keep_at(s, me_ref):
        return (jnp.maximum(s - half, 0), 0, 0)

    return pl.pallas_call(
        kernel,
        grid_spec=pltpu.PrefetchScalarGridSpec(
            num_scalar_prefetch=1,
            grid=(count,),
            in_specs=[
                pl.BlockSpec((in_rows, rows), lambda s, me_ref: (offset_place(offsets, s, me_ref), 0)),
                whole_spec((rows, width)),
                whole_spec((rows, width)),
                pl.BlockSpec((rows, out_rows), lambda s, me_ref: (0, offset_place(offsets, s, me_ref))),
                whole_spec((rows, hidden_width)),
                whole_spec(router.shape),
                whole_spec((1, rows)),
            ],
            out_specs=(
                pl.BlockSpec((1, in_rows, hidden_width), give_at),
                pl.BlockSpec((1, in_rows, hidden_width), keep_at),
                pl.BlockSpec((1, out_rows, width), give_at),
                pl.BlockSpec((1, out_rows, width), keep_at),
            ),
            scratch_shapes=[pltpu.VMEM((rows, hidden_width), bf16), pltpu.VMEM((rows, width), bf16)],
        ),
        out_shape=(
            shape_of((half, in_rows, hidden_width), bf16),
            shape_of((half, in_rows, hidden_width), bf16),
            shape_of((half, out_rows, width), bf16),
            shape_of((half, out_rows, width), bf16),
        ),
        compiler_params=params(),
        cost_estimate=cost(4 * rows * width * hidden_width, 8 * width * hidden_width),
        name="expert_grads",
    )(me, rows_t, rows_in, grads, active, grad_hidden, router, others)


def combine_call(experts, heads, rows, places, gates, routes, cotangent, residual, ffn_low, smalls, w_output):
    tokens, width = cotangent.shape
    stride = rows.shape[0] // experts
    capacity = stride - extra_rows

    def kernel(
        rows_ref, place_ref, gate_ref, routes_ref, cot_ref, res_ref, ffn_ref, small_ref, wo_ref,
        grad_res_ref, branch_ref, ctx_ref, router_ref, gain_ref,
    ):
        gate0, gate1 = gate_ref[:, 0:1], gate_ref[:, 1:2]
        lane_row = lax.broadcasted_iota(jnp.int32, (tokens, stride * experts), 1).astype(f32)
        lane_slot = lax.broadcasted_iota(jnp.int32, (tokens, tile), 1).astype(f32)
        grad_ffn = jnp.zeros((tokens, width), f32)
        grad_gate = []
        for k, gate in enumerate((gate0, gate1)):
            first_row = routes_ref[:, k : k + 1].astype(f32) * stride
            place = place_ref[:, k : k + 1]
            back = (lane_row == first_row + place).astype(f32).astype(bf16)
            grad_ffn = grad_ffn + mm(back, rows_ref[...]) * gate
            coarse = (lane_row == first_row + capacity).astype(f32)
            fine = (lane_row == first_row + (capacity + 8)).astype(f32)
            dots = mm((coarse + fine).astype(bf16), rows_ref[:, :tile])
            grad_gate.append(jnp.sum(jnp.where(lane_slot == place, dots, 0.0), axis=1, keepdims=True))
        grad_gate0, grad_gate1 = grad_gate
        mean_grad = gate0 * grad_gate0 + gate1 * grad_gate1
        chosen0 = gate0 * (grad_gate0 - mean_grad)
        chosen1 = gate1 * (grad_gate1 - mean_grad)
        numbers = lax.broadcasted_iota(jnp.int32, (tokens, experts), 1)
        hot0 = routes_ref[:, 0:1] == numbers
        hot1 = routes_ref[:, 1:2] == numbers
        grad_logits = jnp.where(hot0, chosen0, 0.0) + jnp.where(hot1, chosen1, 0.0)
        grad_logits = grad_logits.astype(bf16)
        router_ref[...] = t_mm(grad_logits, ffn_ref[...])
        grad_ffn = grad_ffn + mm(grad_logits, small_ref[0:experts, :].astype(bf16))
        gain = small_ref[experts + heads + 1 : experts + heads + 2, :]
        residual = res_ref[...]
        inverse = lax.rsqrt(jnp.mean(residual * residual, axis=-1, keepdims=True) + eps)
        scaled = grad_ffn * gain
        inner = jnp.mean(scaled * residual, axis=-1, keepdims=True)
        gain_ref[...] = jnp.sum(grad_ffn * residual * inverse, axis=0, keepdims=True)
        grad_res = cot_ref[...].astype(f32) + inverse * scaled - residual * (inverse * inverse * inverse * inner)
        grad_res_ref[...] = grad_res
        branch = grad_res.astype(bf16)
        branch_ref[...] = branch
        ctx_ref[...] = mm_t(branch, wo_ref[...]).astype(bf16)

    return pl.pallas_call(
        kernel,
        out_shape=(
            shape_of((tokens, width), f32),
            shape_of((tokens, width), bf16),
            shape_of((tokens, width), bf16),
            shape_of((experts, width), f32),
            shape_of((1, width), f32),
        ),
        compiler_params=params(),
        cost_estimate=cost(6 * tokens * width * width, 8 * width * width),
        name="combine",
    )(rows, places, gates, routes, cotangent, residual, ffn_low, smalls, w_output)


def split_rows(full_ref, me_index, count, shards, give_ref, keep_ref):
    for offset in range(count):
        place = lax.bitwise_xor(me_index, offset)
        target = give_ref if offset & 1 else keep_ref
        target[offset // 2, :shards, :] = full_ref[
            pl.ds(pl.multiple_of(place * shards, shards), shards), :
        ].astype(bf16)


def output_grad_call(me, context_low, branch, count):
    tokens, width = branch.shape
    shards = width // count

    def kernel(me_ref, ctx_ref, branch_ref, give_ref, keep_ref, full_ref):
        full_ref[...] = t_mm(ctx_ref[...], branch_ref[...])
        split_rows(full_ref, me_ref[0], count, shards, give_ref, keep_ref)

    vmem = pl.BlockSpec(memory_space=pltpu.VMEM)
    return pl.pallas_call(
        kernel,
        in_specs=[pl.BlockSpec(memory_space=pltpu.SMEM), vmem, vmem],
        out_shape=(shape_of((count // 2, shards, width), bf16),) * 2,
        scratch_shapes=[pltpu.VMEM((width, width), f32)],
        compiler_params=params(),
        cost_estimate=cost(2 * tokens * width * width, 4 * width * width),
        name="output_grad",
    )(me, context_low, branch)


def projection_grad_call(me, dq, dk, dv, normed_t, count):
    tokens, part = dq.shape
    width, seq = normed_t.shape
    shards = width // count

    def kernel(me_ref, dq_ref, dk_ref, dv_ref, normed_ref, give_ref, keep_ref, full_ref):
        own = pl.ds(pl.multiple_of(me_ref[0] * tokens, tokens), tokens)
        full_ref[:, :part] = mm(normed_ref[:, own], dq_ref[...])
        full_ref[:, part : 2 * part] = mm(normed_ref[...], dk_ref[...])
        full_ref[:, 2 * part :] = mm(normed_ref[...], dv_ref[...])
        split_rows(full_ref, me_ref[0], count, shards, give_ref, keep_ref)

    vmem = pl.BlockSpec(memory_space=pltpu.VMEM)
    return pl.pallas_call(
        kernel,
        in_specs=[pl.BlockSpec(memory_space=pltpu.SMEM)] + [vmem] * 4,
        out_shape=(shape_of((count // 2, shards, 3 * part), bf16),) * 2,
        scratch_shapes=[pltpu.VMEM((width, 3 * part), f32)],
        compiler_params=params(),
        cost_estimate=cost(5 * seq * width * part, 10 * seq * width),
        name="projection_grad",
    )(me, dq, dk, dv, normed_t)


def project_back_call(me, first, second, normed_t, sequence, weights, tables, grad_router, grad_gain_ffn, count, small):
    tokens, part = second[0].shape
    width, seq = normed_t.shape
    shards = width // count
    experts = grad_router.shape[0]
    heads, buckets = 2 * tables[0].shape[0], tables[0].shape[1]

    def kernel(
        me_ref, dq1_ref, dk1_ref, dv1_ref, dq2_ref, dk2_ref, dv2_ref, normed_ref, tok_ref, wq_ref, wk_ref, wv_ref,
        table1_ref, table2_ref, router_ref, gain_ffn_ref, give_ref, keep_ref, rows_give_ref, rows_keep_ref, full_ref,
    ):
        own = pl.ds(pl.multiple_of(me_ref[0] * tokens, tokens), tokens)
        full_ref[:, :part] = mm(normed_ref[:, own], dq2_ref[...])
        full_ref[:, part : 2 * part] = mm(normed_ref[...], dk2_ref[...])
        full_ref[:, 2 * part :] = mm(normed_ref[...], dv2_ref[...])
        split_rows(full_ref, me_ref[0], count, shards, give_ref, keep_ref)
        gain = jnp.zeros((1, width), f32)
        for offset in range(count):
            place = lax.bitwise_xor(me_ref[0], offset)
            at = pl.ds(pl.multiple_of(place * tokens, tokens), tokens)
            total = mm_t(dk1_ref[at, :], wk_ref[:, :part]) + mm_t(dk2_ref[at, :], wk_ref[:, part:])
            total = total + mm_t(dv1_ref[at, :], wv_ref[:, :part]) + mm_t(dv2_ref[at, :], wv_ref[:, part:])
            if offset == 0:
                total = total + mm_t(dq1_ref[...], wq_ref[:, :part]) + mm_t(dq2_ref[...], wq_ref[:, part:])
            target = rows_give_ref if offset & 1 else rows_keep_ref
            target[offset // 2] = total.astype(bf16)
            values = tok_ref[at, :].astype(f32)
            inverse = lax.rsqrt(jnp.mean(values * values, axis=-1, keepdims=True) + eps)
            gain = gain + jnp.sum(total * values * inverse, axis=0, keepdims=True)
        wide = jnp.concatenate(
            [router_ref[...], gain, gain_ffn_ref[...], jnp.zeros((small - experts - 2, width), f32)],
            axis=0,
        )
        table = jnp.concatenate([table1_ref[...], table2_ref[...]], axis=0)
        table = jnp.concatenate([table, jnp.zeros((small - heads, buckets), f32)], axis=0)
        extra = jnp.concatenate([table, jnp.zeros((small, 3 * part - width - buckets), f32)], axis=1)
        extra = jnp.concatenate([wide, extra], axis=1).astype(bf16)
        for at in range(count // 2):
            give_ref[at, shards:, :] = extra
            keep_ref[at, shards:, :] = extra

    vmem = pl.BlockSpec(memory_space=pltpu.VMEM)
    return pl.pallas_call(
        kernel,
        in_specs=[pl.BlockSpec(memory_space=pltpu.SMEM)] + [vmem] * 15,
        out_shape=(
            shape_of((count // 2, shards + small, 3 * part), bf16),
            shape_of((count // 2, shards + small, 3 * part), bf16),
            shape_of((count // 2, tokens, width), bf16),
            shape_of((count // 2, tokens, width), bf16),
        ),
        scratch_shapes=[pltpu.VMEM((width, 3 * part), f32)],
        compiler_params=params(),
        cost_estimate=cost(10 * seq * width * width, 10 * seq * width),
        name="project_back",
    )(me, *first, *second, normed_t, sequence, *weights, *tables, grad_router, grad_gain_ffn)


def gather_blocks(value, axis_size):
    blocks = {0: value}
    bit = 2
    while bit < axis_size:
        for offset in sorted(blocks):
            blocks[offset | bit] = swap(blocks[offset], "fsdp", axis_size, bit)
        bit *= 2
    for offset in sorted(blocks):
        blocks[offset | 1] = swap(blocks[offset], "fsdp", axis_size, 1)
    return [blocks[offset] for offset in range(axis_size)]


def scatter_bits(axis_size):
    bits, bit = [1], axis_size // 2
    while bit > 1:
        bits.append(bit)
        bit //= 2
    return [bit for bit in bits if bit < axis_size]


def added(left_side, right_side):
    return left_side.astype(f32) + right_side.astype(f32)


def scatter_sum(given, kept, axis_size, after_cores=None):
    total = added(kept, swap(given, "fsdp", axis_size, 1))
    pieces = {2 * at: total[at] for at in range(axis_size // 2)}
    for bit in scatter_bits(axis_size):
        if bit == 1:
            continue
        left = {}
        for offset in sorted(pieces):
            if offset & bit:
                continue
            leaving = pieces[offset | bit].astype(bf16)
            if after_cores is not None:
                leaving = after_cores(leaving)
            left[offset] = added(pieces[offset], swap(leaving, "fsdp", axis_size, bit))
        pieces = left
    return pieces[0]


def all_sum_expert(value, axis_size, index):
    rows = value.shape[0]
    parts = jnp.pad(value.astype(bf16), ((0, -rows % (axis_size // 2)), (0, 0)))
    bit, bits = 1, []
    while bit < axis_size:
        bits.append(bit)
        bit *= 2
    inner = bits.pop()
    for bit in bits:
        low_half, high_half = jnp.split(parts, 2, axis=0)
        upper = (index & bit) != 0
        keep = jnp.where(upper, high_half, low_half)
        give = jnp.where(upper, low_half, high_half)
        parts = added(keep, swap(give, "expert", axis_size, bit)).astype(bf16)
    parts = added(parts, swap(parts, "expert", axis_size, inner)).astype(bf16)
    for bit in reversed(bits):
        other = swap(parts, "expert", axis_size, bit)
        upper = (index & bit) != 0
        parts = jnp.concatenate(
            [jnp.where(upper, other, parts), jnp.where(upper, parts, other)], axis=0
        )
    return parts[:rows]


def ordered(*values):
    return lax.optimization_barrier(values)


def build(count, expert_ranks):
    def per_device(
        tokens_in,
        seg_ids,
        routes,
        buckets,
        attn_gain,
        w_query,
        w_key,
        w_value,
        w_output,
        bias_table,
        ffn_gain,
        w_router,
        w_in,
        w_out,
        cotangent,
    ):
        tokens, width = tokens_in.shape
        shards, experts = w_router.shape
        bucket_rows, heads = bias_table.shape
        bucket_count = bucket_rows * count
        head_dim = width // heads
        seq = buckets.shape[0]
        top_count = routes.shape[1]
        capacity = 3 * top_count * tokens // (2 * experts)
        slots = experts * capacity
        fsdp_index = lax.axis_index("fsdp")
        expert_index = lax.axis_index("expert")
        me = jnp.stack([fsdp_index, expert_index]).astype(jnp.int32)

        used = experts + heads + 3
        small_rows = -(-used // 16) * 16
        packed = pack_call(
            me, (w_query, w_key, w_value), tokens_in, seg_ids[None, :],
            jnp.stack([attn_gain, ffn_gain]), bias_table, w_router.T, small_rows, width,
        )
        blocks = gather_blocks(packed, count)
        out_blocks = gather_blocks(ordered(w_output, blocks[-2])[0], count)
        routes, blocks[1] = ordered(routes, blocks[1])
        padded_buckets = jnp.concatenate([jnp.full((seq,), -1, jnp.int32), buckets])
        bucket_window = lax.dynamic_slice_in_dim(
            padded_buckets, fsdp_index * tokens, seq + tokens, 0
        )[None, :]

        slot_map, back0, back1, grad_rows_out, places = route_call(routes, cotangent, capacity, experts)
        grad_rows_in = lax.all_to_all(
            grad_rows_out, "expert", split_axis=0, concat_axis=0, tiled=True
        )
        others = grad_rows_in[:, capacity, :capacity].reshape(1, slots)
        grad_rows_in = grad_rows_in[:, :capacity, :].reshape(slots, width)

        (queries, keys, values, normed, sequence, wq, wk, wv, smalls, bias, mask) = project_call(
            me, blocks, shards, small_rows, bucket_window, heads, bucket_count, experts
        )
        queries, grad_rows_in, others = ordered(queries, grad_rows_in, others)
        context, lse = attend_call(queries, keys, values, bias, mask, head_dim)
        wo, context_low, residual, ffn_low, gates, rows_out = dispatch_call(
            me, context, out_blocks, tokens_in, smalls, routes, slot_map, heads
        )(experts)
        rows_in = lax.all_to_all(
            rows_out.reshape(experts, capacity, width),
            "expert",
            split_axis=0,
            concat_axis=0,
            tiled=True,
        ).reshape(slots, width)
        active, grad_hidden, made, row_grads = expert_call(
            rows_in, grad_rows_in, w_in[0], w_out[0], experts
        )
        row_grads_back = lax.all_to_all(
            row_grads, "expert", split_axis=0, concat_axis=0, tiled=True
        ).reshape(-1, width)

        rows_t = rows_in.T
        normed_t = normed.T
        give = [offset for offset in range(count) if offset & 1]
        keep = [offset for offset in range(count) if not offset & 1]
        router = smalls[:experts]
        in_give, in_keep, out_give, out_keep = expert_grads_call(
            me, rows_t, rows_in, grad_rows_in, active, grad_hidden, router, others, give + keep
        )
        in_total = added(in_keep, swap(in_give, "fsdp", count, 1)).astype(bf16)
        out_total = added(out_keep, swap(out_give, "fsdp", count, 1)).astype(bf16)
        row_grads_back, in_total = ordered(row_grads_back, in_total)

        grad_residual, branch, grad_context, grad_router, grad_gain_ffn = combine_call(
            experts, heads, row_grads_back, places, gates, routes, cotangent,
            residual, ffn_low, smalls, wo,
        )
        made_back = lax.all_to_all(
            made.reshape(experts, capacity, width),
            "expert",
            split_axis=0,
            concat_axis=0,
            tiled=True,
        ).reshape(slots, width)
        wo_give, wo_keep = output_grad_call(me, context_low, branch, count)
        grad_context, wo_give, wo_keep = ordered(grad_context, wo_give, wo_keep)

        def far_sum(total, early, late):
            pieces = {2 * at: total[at] for at in range(count // 2)}
            for bit in scatter_bits(count):
                if bit == 1:
                    continue
                left = {}
                for offset in sorted(pieces):
                    if offset & bit:
                        continue
                    leaving = pieces[offset | bit].astype(bf16)
                    if early is not None:
                        leaving = ordered(leaving, early)[0]
                    arrived = swap(leaving, "fsdp", count, bit)
                    if late is not None:
                        arrived = ordered(arrived, late)[0]
                    left[offset] = added(pieces[offset], arrived)
                pieces = left
            return pieces[0]

        pairs = width // tile
        near = pairs // 2
        part1 = attend_back_call(
            queries, keys, values, bias, mask, lse, context, grad_context, bucket_window,
            bucket_count, head_dim, 0, near,
        )
        part2 = attend_back_call(
            queries, keys, values, bias, mask, lse, context, grad_context, bucket_window,
            bucket_count, head_dim, near, pairs - near,
        )
        parts = [part1, part2]
        in_sum = far_sum(in_total, None, part1[0])
        small_grad_rows = -(-max(experts + 2, heads) // 32) * 32
        give1, keep1 = projection_grad_call(me, *parts[0][:3], normed_t, count)
        normed_last, in_sum, give1 = ordered(normed_t, in_sum, give1)
        give2, keep2, rows_give, rows_keep = project_back_call(
            me, parts[0][:3], parts[1][:3], normed_last, sequence, (wq, wk, wv),
            (parts[0][3][:, :, 0], parts[1][3][:, :, 0]), grad_router, grad_gain_ffn, count, small_grad_rows,
        )

        wo_sum = scatter_sum(wo_give, wo_keep, count)
        sum1 = scatter_sum(give1, keep1, count)
        sum2 = scatter_sum(give2, keep2, count)
        grad_shards = [in_sum, far_sum(out_total, sum2, None)]
        chain1 = all_sum_expert(jnp.concatenate([wo_sum, sum1], axis=1), expert_ranks, expert_index)
        chain2 = all_sum_expert(sum2, expert_ranks, expert_index)
        chain1 = chain1.astype(f32)
        chain2 = chain2.astype(f32)
        half_cols = near * tile

        grad_normed = scatter_sum(rows_give, rows_keep, count, lambda value: ordered(value, sum2)[0])
        inputs = tokens_in.astype(f32)
        inverse = lax.rsqrt(jnp.mean(inputs * inputs, axis=-1, keepdims=True) + eps)
        gain_attn = smalls[experts + heads]
        scaled = grad_normed * gain_attn
        inner = jnp.mean(scaled * inputs, axis=-1, keepdims=True)
        grad_tokens = grad_residual + inverse * scaled - inputs * inverse**3 * inner

        made_back = ordered(made_back, part2[0])[0]
        picked0 = mm(back0, made_back)
        picked1 = mm(back1, made_back)
        block_out = (residual + gates[:, 0:1] * picked0 + gates[:, 1:2] * picked1).astype(bf16)

        shards_out = []
        for part in range(3):
            left = chain1[:, width + part * half_cols : width + (part + 1) * half_cols]
            rest = width - half_cols
            right = chain2[:shards, part * rest : (part + 1) * rest]
            shards_out.append(jnp.concatenate([left, right], axis=1))
        shards_out.append(chain1[:, :width])
        small_out = chain2[shards:]
        cols = lax.dynamic_slice_in_dim(small_out[:, :width], fsdp_index * shards, shards, 1)
        table_cols = lax.dynamic_slice_in_dim(
            small_out[:heads, width:], fsdp_index * bucket_rows, bucket_rows, 1
        )
        return (
            block_out,
            grad_tokens,
            cols[experts],
            shards_out[0],
            shards_out[1],
            shards_out[2],
            shards_out[3],
            table_cols.T,
            cols[experts + 1],
            cols[:experts].T,
            grad_shards[0][None],
            grad_shards[1][None],
        )

    return per_device


def solution(mesh):
    return jax.shard_map(
        build(mesh.shape["fsdp"], mesh.shape["expert"]),
        mesh=mesh,
        in_specs=(
            P(("expert", "fsdp"), None),
            P(("expert", "fsdp")),
            P(("expert", "fsdp"), None),
            P(),
            P("fsdp"),
            P("fsdp", None),
            P("fsdp", None),
            P("fsdp", None),
            P("fsdp", None),
            P("fsdp", None),
            P("fsdp"),
            P("fsdp", None),
            P("expert", None, None),
            P("expert", None, None),
            P(("expert", "fsdp"), None),
        ),
        out_specs=(
            P(("expert", "fsdp"), None),
            P(("expert", "fsdp"), None),
            P("fsdp"),
            P("fsdp", None),
            P("fsdp", None),
            P("fsdp", None),
            P("fsdp", None),
            P("fsdp", None),
            P("fsdp"),
            P("fsdp", None),
            P("expert", "fsdp", None),
            P("expert", "fsdp", None),
        ),
        check_vma=False,
    )
```

```python
import math

import jax
import jax.numpy as jnp
from jax import lax
from jax.experimental import pallas as pl
from jax.experimental.pallas import tpu as pltpu
from jax.sharding import PartitionSpec as P

eps = 1e-06
log2e = math.log2(math.e)
masked_score = -1e30
f32 = jnp.float32
bf16 = jnp.bfloat16
tile = 128
extra_rows = 16


def mm(left_side, right_side):
    return lax.dot_general(
        left_side, right_side, (((1,), (0,)), ((), ())), preferred_element_type=f32
    )


def mm_t(left_side, right_side):
    return lax.dot_general(
        left_side, right_side, (((1,), (1,)), ((), ())), preferred_element_type=f32
    )


def t_mm(left_side, right_side):
    return lax.dot_general(
        left_side, right_side, (((0,), (0,)), ((), ())), preferred_element_type=f32
    )


def swap(value, axis_name, axis_size, bit):
    return lax.ppermute(value, axis_name, [(i, i ^ bit) for i in range(axis_size)])


def params(megabytes=56):
    return pltpu.CompilerParams(vmem_limit_bytes=megabytes << 20)


def cost(flops, moved):
    return pl.CostEstimate(flops=int(flops) >> 8, bytes_accessed=int(moved) >> 8, transcendentals=0)


def shape_of(dims, dtype):
    return jax.ShapeDtypeStruct(dims, dtype)


def whole_spec(dims):
    return pl.BlockSpec(dims, lambda *unused: (0,) * len(dims))


def to_column(row):
    return jnp.broadcast_to(row, (tile, row.shape[1])).T


def route_kernel(capacity, routes_ref, cot_ref, map_ref, back0_ref, back1_ref, out_ref, slot_ref):
    tokens = routes_ref.shape[0]
    slots = map_ref.shape[0]
    experts = slots // capacity
    routes = routes_ref[...]
    first, second = routes[:, 0:1], routes[:, 1:2]
    numbers = lax.broadcasted_iota(jnp.int32, (tokens, experts), 1)
    hot0 = (first == numbers).astype(f32)
    hot1 = (second == numbers).astype(f32)
    rows = lax.broadcasted_iota(jnp.int32, (tokens, tokens), 0)
    cols = lax.broadcasted_iota(jnp.int32, (tokens, tokens), 1)
    before = (cols < rows).astype(f32).astype(bf16)
    earlier = mm(before, (hot0 + hot1).astype(bf16))
    slot0 = jnp.sum(hot0 * earlier, axis=1, keepdims=True)
    slot1 = jnp.sum(hot1 * (earlier + hot0), axis=1, keepdims=True)
    slot_ref[...] = jnp.concatenate([slot0, slot1], axis=1)
    dest0 = first.astype(f32) * capacity + slot0
    dest1 = second.astype(f32) * capacity + slot1
    lane_slot = lax.broadcasted_iota(jnp.int32, (tokens, slots), 1).astype(f32)
    back0_ref[...] = (lane_slot == dest0).astype(f32).astype(bf16)
    back1_ref[...] = (lane_slot == dest1).astype(f32).astype(bf16)
    row0 = jnp.broadcast_to(dest0, (tokens, tile)).T[0:1, :]
    row1 = jnp.broadcast_to(dest1, (tokens, tile)).T[0:1, :]
    row_slot = lax.broadcasted_iota(jnp.int32, (slots, tokens), 0).astype(f32)
    hot = ((row_slot == row0).astype(f32) + (row_slot == row1).astype(f32)).astype(bf16)
    map_ref[...] = hot
    rows = mm(hot, cot_ref[...]).astype(bf16)
    others = back0_ref[...].astype(f32) * second.astype(f32) + back1_ref[...].astype(f32) * first.astype(f32)
    others = jnp.broadcast_to(jnp.sum(others, axis=0, keepdims=True), (extra_rows, slots))
    width = rows.shape[1]
    for expert in range(experts):
        at = expert * capacity
        lanes = pltpu.roll(others, (slots - at) % slots, 1)[:, :tile]
        lanes = jnp.concatenate([lanes, jnp.zeros((extra_rows, width - tile), f32)], axis=1)
        out_ref[expert, :capacity, :] = rows[at : at + capacity, :]
        out_ref[expert, capacity:, :] = lanes.astype(bf16)


def route_call(routes, cotangent, capacity, experts):
    tokens, width = cotangent.shape
    slots = experts * capacity
    return pl.pallas_call(
        lambda *refs: route_kernel(capacity, *refs),
        out_shape=(
            shape_of((slots, tokens), bf16),
            shape_of((tokens, slots), bf16),
            shape_of((tokens, slots), bf16),
            shape_of((experts, capacity + extra_rows, width), bf16),
            shape_of((tokens, 2), f32),
        ),
        compiler_params=params(),
        cost_estimate=cost(2 * slots * tokens * width, 4 * slots * width),
        name="route",
    )(routes, cotangent)


def pack_call(me, weights, tokens_in, seg_row, gains, table, router, small, width):
    shards = weights[0].shape[0]
    tokens = tokens_in.shape[0]
    experts, heads = router.shape[0], table.shape[1]
    used = experts + heads + 3

    def placed(me_ref, rows):
        at = lax.broadcasted_iota(jnp.int32, (rows, width), 1)
        own = lax.broadcasted_iota(jnp.int32, (rows, width), 0) + me_ref[0] * rows
        return (at == own).astype(f32).astype(bf16)

    def kernel(me_ref, wq_ref, wk_ref, wv_ref, x_ref, seg_ref, gain_ref, table_ref, router_ref, out_ref):
        for at, ref in enumerate((wq_ref, wk_ref, wv_ref)):
            out_ref[at * shards : (at + 1) * shards, :] = ref[...]
        out_ref[3 * shards : 3 * shards + tokens, :] = x_ref[...]
        columns = placed(me_ref, shards)
        rows = [
            mm(router_ref[...], columns),
            t_mm(table_ref[...], placed(me_ref, table_ref.shape[0])),
            mm(gain_ref[...], columns),
            jnp.zeros((small - used, width), f32),
            jnp.concatenate([seg_ref[...].astype(f32), jnp.zeros((1, width - tokens), f32)], axis=1),
        ]
        out_ref[3 * shards + tokens :, :] = jnp.concatenate(rows, axis=0).astype(bf16)

    vmem = pl.BlockSpec(memory_space=pltpu.VMEM)
    return pl.pallas_call(
        kernel,
        in_specs=[pl.BlockSpec(memory_space=pltpu.SMEM)] + [vmem] * 8,
        out_shape=shape_of((3 * shards + tokens + small, width), bf16),
        compiler_params=params(),
        cost_estimate=cost(1, 4 * shards * width),
        name="pack",
    )(me, *weights, tokens_in, seg_row, gains, table, router)


def project_call(me, blocks, shards, small, bucket_window, heads, buckets, experts):
    count = len(blocks)
    rows, width = blocks[0].shape
    tokens = rows - 3 * shards - small
    seq = count * tokens
    window = bucket_window.shape[1]

    def kernel(me_ref, *refs):
        block_refs = refs[:count]
        (bucket_ref, q_ref, k_ref, v_ref, normed_ref, tok_ref, wq_ref, wk_ref, wv_ref, small_ref, bias_ref, mask_ref) = refs[count:]
        me_index = me_ref[0]
        totals = jnp.zeros((small, width), f32)
        own_docs = block_refs[0][rows - small :, :].astype(f32)[small - 1 :, :tokens]
        for offset in range(count):
            place = lax.bitwise_xor(me_index, offset)
            row = pl.multiple_of(place * shards, shards)
            for part, full_ref in enumerate((wq_ref, wk_ref, wv_ref)):
                full_ref[pl.ds(row, shards), :] = block_refs[offset][part * shards : (part + 1) * shards, :]
            token_row = pl.multiple_of(place * tokens, tokens)
            tok_ref[pl.ds(token_row, tokens), :] = block_refs[offset][3 * shards : rows - small, :]
            extra = block_refs[offset][rows - small :, :].astype(f32)
            totals = totals + extra
            docs = to_column(extra[small - 1 :, :tokens])
            docs = jnp.concatenate([docs] * (tokens // tile), axis=1)
            mask_ref[pl.ds(token_row, tokens), :] = jnp.where(docs == own_docs, 0.0, masked_score)
        small_ref[...] = totals
        gain = totals[experts + heads : experts + heads + 1, :]
        table = totals[experts : experts + heads, :buckets].astype(bf16)
        numbers = lax.broadcasted_iota(jnp.int32, (buckets, window), 0)
        hot = (numbers == bucket_ref[...]).astype(f32).astype(bf16)
        by_distance = mm(table, hot) * log2e
        by_distance = jnp.where(bucket_ref[...] < 0, masked_score, by_distance)
        for head in range(heads):
            bias_ref[head] = by_distance[head : head + 1, :]

        @pl.loop(0, count)
        def chunk(index):
            rows = pl.ds(pl.multiple_of(index * tokens, tokens), tokens)
            values = tok_ref[rows, :].astype(f32)
            inverse = lax.rsqrt(jnp.mean(values * values, axis=-1, keepdims=True) + eps)
            normed = (values * inverse * gain).astype(bf16)
            normed_ref[rows, :] = normed
            k_ref[rows, :] = mm(normed, wk_ref[...]).astype(bf16)
            v_ref[rows, :] = mm(normed, wv_ref[...]).astype(bf16)

        own = normed_ref[pl.ds(pl.multiple_of(me_index * tokens, tokens), tokens), :]
        q_ref[...] = mm(own, wq_ref[...]).astype(bf16)

    vmem = pl.BlockSpec(memory_space=pltpu.VMEM)
    return pl.pallas_call(
        kernel,
        in_specs=[pl.BlockSpec(memory_space=pltpu.SMEM)] + [vmem] * (count + 1),
        out_shape=(
            shape_of((tokens, width), bf16),
            shape_of((seq, width), bf16),
            shape_of((seq, width), bf16),
            shape_of((seq, width), bf16),
            shape_of((seq, width), bf16),
            shape_of((width, width), bf16),
            shape_of((width, width), bf16),
            shape_of((width, width), bf16),
            shape_of((small, width), f32),
            shape_of((heads, 1, window), f32),
            shape_of((seq, tokens), f32),
        ),
        compiler_params=params(),
        cost_estimate=cost(2 * width * width * (2 * seq + tokens), 20 * seq * width),
        name="project",
    )(me, *blocks, bucket_window)


def skewed(bias_row, window):
    spread = jnp.broadcast_to(bias_row, (tile, window))
    return pltpu.roll(spread, 0, 1, stride=1, stride_axis=0)


def attend_call(queries, keys, values, bias, mask, head_dim):
    tokens, width = queries.shape
    seq = keys.shape[0]
    heads, _, window = bias.shape
    pairs = width // tile
    per_step = heads // pairs
    key_blocks = seq // tile
    scale = head_dim**-0.5 * log2e

    def kernel(q_ref, k_ref, v_ref, bias_ref, mask_ref, ctx_ref, lse_ref, score_ref, prob_ref, skew_ref):
        lane = lax.broadcasted_iota(jnp.int32, (tokens, tile), 1)
        row = lax.broadcasted_iota(jnp.int32, (tile, tokens), 0)
        query = q_ref[...]
        values_t = v_ref[...].T
        result = jnp.zeros((tile, tokens), f32)
        for half in range(per_step):
            mine = jnp.where(lane // head_dim == half, query, jnp.zeros_like(query))
            skew_ref[...] = skewed(bias_ref[half], window)
            top = jnp.full((8, tokens), -3e38, f32)
            for block in range(key_blocks):
                rows = pl.ds(block * tile, tile)
                begin = tile * (key_blocks - block)
                scores = mm_t(k_ref[rows, :], mine) * scale
                scores = scores + (skew_ref[:, begin : begin + tokens] + mask_ref[rows, :])
                score_ref[rows, :] = scores
                top = jnp.maximum(top, jnp.max(scores.reshape(tile // 8, 8, tokens), axis=0))
            top = jnp.max(top, axis=0, keepdims=True)
            total = jnp.zeros((8, tokens), f32)
            for block in range(key_blocks):
                rows = pl.ds(block * tile, tile)
                probs = jnp.exp2(score_ref[rows, :] - top)
                prob_ref[rows, :] = probs.astype(bf16)
                total = total + jnp.sum(probs.reshape(tile // 8, 8, tokens), axis=0)
            total = jnp.sum(total, axis=0, keepdims=True)
            lse_ref[half] = top + jnp.log2(total)
            mixed = mm(values_t, prob_ref[...]) * (1.0 / total)
            result = jnp.where(row // head_dim == half, mixed, result)
        ctx_ref[...] = result.T

    return pl.pallas_call(
        kernel,
        grid=(pairs,),
        in_specs=[
            pl.BlockSpec((tokens, tile), lambda p: (0, p)),
            pl.BlockSpec((seq, tile), lambda p: (0, p)),
            pl.BlockSpec((seq, tile), lambda p: (0, p)),
            pl.BlockSpec((per_step, 1, window), lambda p: (p, 0, 0)),
            pl.BlockSpec((seq, tokens), lambda p: (0, 0)),
        ],
        out_specs=(
            pl.BlockSpec((tokens, tile), lambda p: (0, p)),
            pl.BlockSpec((per_step, 1, tokens), lambda p: (p, 0, 0)),
        ),
        out_shape=(shape_of((tokens, width), f32), shape_of((heads, 1, tokens), f32)),
        scratch_shapes=[
            pltpu.VMEM((seq, tokens), f32),
            pltpu.VMEM((seq, tokens), bf16),
            pltpu.VMEM((tile, window), f32),
        ],
        compiler_params=params(),
        cost_estimate=cost(16 * heads * tokens * seq * tile, 4 * seq * width),
        name="attend",
    )(queries, keys, values, bias, mask)


def unskewed(total):
    window = total.shape[1]
    rows = total.shape[0]
    while rows > 8:
        rows = rows // 2
        total = total[:rows, :] + pltpu.roll(total[rows:, :], window - rows, 1)
    step = 4
    while step:
        moved = pltpu.roll(pltpu.roll(total, 8 - step, 0), window - step, 1)
        total = total + moved
        step = step // 2
    return total[0:1, :]


def attend_back_call(queries, keys, values, bias, mask, lse, context, grad_context, bucket_window, buckets, head_dim, first, pairs):
    tokens, width = queries.shape
    seq = keys.shape[0]
    heads, _, window = bias.shape
    per_step = heads // (width // tile)
    key_blocks = seq // tile
    scale = head_dim**-0.5

    def kernel(
        q_ref, k_ref, v_ref, bias_ref, mask_ref, lse_ref, ctx_ref, grad_ref, bucket_ref,
        dq_ref, dk_ref, dv_ref, table_ref, prob_ref, ds_ref, skew_ref, sum_ref,
    ):
        lane = lax.broadcasted_iota(jnp.int32, (tokens, tile), 1)
        row = lax.broadcasted_iota(jnp.int32, (tile, tokens), 0)
        query = q_ref[...]
        grad = grad_ref[...]
        keys_t = k_ref[...].T
        products = (grad.astype(f32) * ctx_ref[...]).T
        result = jnp.zeros((tile, tokens), f32)
        numbers = lax.broadcasted_iota(jnp.int32, (buckets, window), 0)
        hot = (numbers == bucket_ref[...]).astype(f32)
        mine_q, mine_g = [], []
        for half in range(per_step):
            mine_q.append(jnp.where(lane // head_dim == half, query, jnp.zeros_like(query)))
            mine_g.append(jnp.where(lane // head_dim == half, grad, jnp.zeros_like(grad)))
        for half in range(per_step):
            delta = jnp.sum(
                products[half * head_dim : (half + 1) * head_dim, :], axis=0, keepdims=True
            )
            lse_row = lse_ref[half]
            skew_ref[...] = skewed(bias_ref[half], window)
            sum_ref[...] = jnp.zeros((tile, window), f32)
            cols = slice(half * tokens, (half + 1) * tokens)
            for block in range(key_blocks):
                rows = pl.ds(block * tile, tile)
                begin = tile * (key_blocks - block)
                scores = mm_t(k_ref[rows, :], mine_q[half]) * (scale * log2e)
                scores = scores + (skew_ref[:, begin : begin + tokens] + mask_ref[rows, :])
                probs = jnp.exp2(scores - lse_row)
                grad_probs = mm_t(v_ref[rows, :], mine_g[half])
                grad_scores = (probs * (grad_probs - delta)).astype(bf16)
                prob_ref[rows, cols] = probs.astype(bf16)
                ds_ref[rows, cols] = grad_scores
                sum_ref[:, begin : begin + tokens] += grad_scores.astype(f32)
            grad_q = mm(keys_t, ds_ref[:, cols])
            result = jnp.where(row // head_dim == half, grad_q, result)
            by_distance = unskewed(sum_ref[...])
            column = jnp.sum(hot * by_distance, axis=1, keepdims=True)
            table_ref[half] = jnp.broadcast_to(column, (buckets, tile)).T[0:1, :]
        dq_ref[...] = (result * scale).T.astype(bf16)
        dk_ref[...] = (mm(ds_ref[...], jnp.concatenate(mine_q, axis=0)) * scale).astype(bf16)
        dv_ref[...] = mm(prob_ref[...], jnp.concatenate(mine_g, axis=0)).astype(bf16)

    narrow = pl.BlockSpec((tokens, tile), lambda p: (0, p + first))
    tall = pl.BlockSpec((seq, tile), lambda p: (0, p + first))
    narrow_out = pl.BlockSpec((tokens, tile), lambda p: (0, p))
    tall_out = pl.BlockSpec((seq, tile), lambda p: (0, p))
    return pl.pallas_call(
        kernel,
        grid=(pairs,),
        in_specs=[
            narrow,
            tall,
            tall,
            pl.BlockSpec((per_step, 1, window), lambda p: (p + first, 0, 0)),
            pl.BlockSpec((seq, tokens), lambda p: (0, 0)),
            pl.BlockSpec((per_step, 1, tokens), lambda p: (p + first, 0, 0)),
            narrow,
            narrow,
            pl.BlockSpec((1, window), lambda p: (0, 0)),
        ],
        out_specs=(
            narrow_out,
            tall_out,
            tall_out,
            pl.BlockSpec((per_step, 1, buckets), lambda p: (p, 0, 0)),
        ),
        out_shape=(
            shape_of((tokens, pairs * tile), bf16),
            shape_of((seq, pairs * tile), bf16),
            shape_of((seq, pairs * tile), bf16),
            shape_of((pairs * per_step, 1, buckets), f32),
        ),
        scratch_shapes=[
            pltpu.VMEM((seq, per_step * tokens), bf16),
            pltpu.VMEM((seq, per_step * tokens), bf16),
            pltpu.VMEM((tile, window), f32),
            pltpu.VMEM((tile, window), f32),
        ],
        compiler_params=params(),
        cost_estimate=cost(40 * pairs * per_step * tokens * seq * tile, 8 * seq * pairs * tile),
        name="attend_back",
    )(queries, keys, values, bias, mask, lse, context, grad_context, bucket_window)


def chosen_logits(routes, logits):
    numbers = lax.broadcasted_iota(jnp.int32, logits.shape, 1)
    hot0 = routes[:, 0:1] == numbers
    hot1 = routes[:, 1:2] == numbers
    return hot0, hot1


def dispatch_call(me, context, out_blocks, tokens_in, smalls, routes, slot_map, heads):
    tokens, width = tokens_in.shape
    count = len(out_blocks)
    shards = out_blocks[0].shape[0]
    slots = slot_map.shape[0]

    def make(experts):
        def kernel(me_ref, ctx_ref, *refs):
            block_refs = refs[:count]
            (x_ref, small_ref, routes_ref, map_ref, wo_ref, low_ref, res_ref, ffn_ref, gate_ref, rows_ref) = refs[count:]
            for offset in range(count):
                place = lax.bitwise_xor(me_ref[0], offset)
                wo_ref[pl.ds(pl.multiple_of(place * shards, shards), shards), :] = block_refs[offset][...]
            context_low = ctx_ref[...].astype(bf16)
            low_ref[...] = context_low
            residual = x_ref[...].astype(f32) + mm(context_low, wo_ref[...])
            res_ref[...] = residual
            gain = small_ref[experts + heads + 1 : experts + heads + 2, :]
            inverse = lax.rsqrt(jnp.mean(residual * residual, axis=-1, keepdims=True) + eps)
            ffn_low = (residual * inverse * gain).astype(bf16)
            ffn_ref[...] = ffn_low
            rows_ref[...] = mm(map_ref[...], ffn_low).astype(bf16)
            logits = mm_t(ffn_low, small_ref[0:experts, :].astype(bf16))
            hot0, hot1 = chosen_logits(routes_ref[...], logits)
            first = jnp.sum(jnp.where(hot0, logits, 0.0), axis=1, keepdims=True)
            second = jnp.sum(jnp.where(hot1, logits, 0.0), axis=1, keepdims=True)
            top = jnp.maximum(first, second)
            weight0 = jnp.exp(first - top)
            weight1 = jnp.exp(second - top)
            whole = weight0 + weight1
            gate0 = weight0 / whole
            gate1 = weight1 / whole
            gate_ref[...] = jnp.concatenate([gate0, gate1], axis=1)

        return kernel

    def run(experts):
        vmem = pl.BlockSpec(memory_space=pltpu.VMEM)
        return pl.pallas_call(
            make(experts),
            in_specs=[pl.BlockSpec(memory_space=pltpu.SMEM)] + [vmem] * (count + 5),
            out_shape=(
                shape_of((width, width), bf16),
                shape_of((tokens, width), bf16),
                shape_of((tokens, width), f32),
                shape_of((tokens, width), bf16),
                shape_of((tokens, 2), f32),
                shape_of((slots, width), bf16),
            ),
            compiler_params=params(),
            cost_estimate=cost(4 * tokens * width * width, 8 * width * width),
            name="dispatch",
        )(me, context, *out_blocks, tokens_in, smalls, routes, slot_map)

    return run


def expert_call(rows, grads, expert_in, expert_out, experts):
    count, width = rows.shape
    capacity = count // experts
    stride = capacity + extra_rows
    hidden_width = expert_in.shape[1]
    step_width = 512
    chunk_rows = 256
    steps = hidden_width // step_width
    half_root = math.sqrt(0.5)
    density = 1.0 / math.sqrt(2.0 * math.pi)

    def kernel(x_ref, g_ref, in_ref, out_ref, active_ref, gh_ref, made_ref, back_ref, made_sum, back_sum):
        step = pl.program_id(0)

        @pl.when(step == 0)
        def start():
            made_sum[...] = jnp.zeros((count, width), f32)
            back_sum[...] = jnp.zeros((count, width), f32)

        @pl.loop(0, count // chunk_rows)
        def chunk(index):
            at = pl.ds(pl.multiple_of(index * chunk_rows, chunk_rows), chunk_rows)
            hidden = mm(x_ref[at, :], in_ref[...])
            upstream = mm_t(g_ref[at, :], out_ref[...])
            share = 0.5 + 0.5 * lax.erf(hidden * half_root)
            active = (hidden * share).astype(bf16)
            slope = share + hidden * (jnp.exp(hidden * hidden * -0.5) * density)
            grad_hidden = (upstream * slope).astype(bf16)
            active_ref[at, :] = active
            gh_ref[at, :] = grad_hidden
            made_sum[at, :] += mm(active, out_ref[...])
            back_sum[at, :] += mm_t(grad_hidden, in_ref[...])

        @pl.when(step == steps - 1)
        def finish():
            made = made_sum[...].astype(bf16)
            made_ref[...] = made
            products = made.astype(f32) * g_ref[...].astype(f32)
            folded = products[:, :tile]
            for at in range(tile, width, tile):
                folded = folded + products[:, at : at + tile]
            dots = jnp.broadcast_to(jnp.sum(folded.T, axis=0, keepdims=True), (8, count))
            coarse = dots.astype(bf16).astype(f32)
            fine = dots - coarse
            for expert in range(experts):
                at = expert * capacity
                shift = (count - at) % count
                lanes = [pltpu.roll(half, shift, 1)[:, :tile] for half in (coarse, fine)]
                lanes = jnp.concatenate(lanes, axis=0)
                lanes = jnp.concatenate([lanes, jnp.zeros((extra_rows, width - tile), f32)], axis=1)
                back_ref[expert, :capacity, :] = back_sum[at : at + capacity, :].astype(bf16)
                back_ref[expert, capacity:, :] = lanes.astype(bf16)

    full = whole_spec((count, width))
    return pl.pallas_call(
        kernel,
        grid=(steps,),
        in_specs=[
            full,
            full,
            pl.BlockSpec((width, step_width), lambda s: (0, s)),
            pl.BlockSpec((step_width, width), lambda s: (s, 0)),
        ],
        out_specs=(
            pl.BlockSpec((count, step_width), lambda s: (0, s)),
            pl.BlockSpec((count, step_width), lambda s: (0, s)),
            full,
            whole_spec((experts, stride, width)),
        ),
        out_shape=(
            shape_of((count, hidden_width), bf16),
            shape_of((count, hidden_width), bf16),
            shape_of((count, width), bf16),
            shape_of((experts, stride, width), bf16),
        ),
        scratch_shapes=[pltpu.VMEM((count, width), f32), pltpu.VMEM((count, width), f32)],
        compiler_params=params(),
        cost_estimate=cost(8 * count * width * hidden_width, 8 * width * hidden_width),
        name="experts",
    )(rows, grads, expert_in, expert_out)


def offset_place(offsets, step, me_ref):
    offset = offsets[0]
    for at in range(1, len(offsets)):
        offset = jnp.where(step == at, offsets[at], offset)
    return lax.bitwise_xor(me_ref[0], offset)


def gate_column(me_ref, rows_ref, router_ref, others_ref):
    logits = mm_t(router_ref[...].astype(bf16), rows_ref[...])
    numbers = lax.broadcasted_iota(jnp.int32, logits.shape, 0).astype(f32)
    mine = jnp.sum(jnp.where(numbers == me_ref[1].astype(f32), logits, 0.0), axis=0, keepdims=True)
    other = jnp.sum(
        jnp.where(numbers == others_ref[...].astype(f32), logits, 0.0), axis=0, keepdims=True
    )
    return to_column(1.0 / (1.0 + jnp.exp(other - mine)))[:, 0:1]


def expert_grads_call(me, rows_t, rows_in, grads, active, grad_hidden, router, others, offsets):
    width, rows = rows_t.shape
    hidden_width = grad_hidden.shape[1]
    count = len(offsets)
    half = count // 2
    in_rows, out_rows = width // count, hidden_width // count

    def kernel(
        me_ref, xt_ref, rows_ref, g_ref, active_ref, gh_ref, router_ref, others_ref,
        in_give_ref, in_keep_ref, out_give_ref, out_keep_ref, gh_scr, g_scr,
    ):
        step = pl.program_id(0)

        @pl.when(step == 0)
        def start():
            column = gate_column(me_ref, rows_ref, router_ref, others_ref)
            g_scr[...] = (g_ref[...].astype(f32) * column).astype(bf16)
            for at in range(0, hidden_width, width):
                gh_scr[:, at : at + width] = (gh_ref[:, at : at + width].astype(f32) * column).astype(bf16)

        def shard(in_ref, out_ref):
            for at in range(0, hidden_width, width):
                in_ref[0, :, at : at + width] = mm(xt_ref[...], gh_scr[:, at : at + width]).astype(bf16)
            out_ref[0] = t_mm(active_ref[...], g_scr[...]).astype(bf16)

        @pl.when(step < half)
        def first():
            shard(in_give_ref, out_give_ref)

        @pl.when(step >= half)
        def second():
            shard(in_keep_ref, out_keep_ref)

    def give_at(s, me_ref):
        return (jnp.minimum(s, half - 1), 0, 0)

    def keep_at(s, me_ref):
        return (jnp.maximum(s - half, 0), 0, 0)

    return pl.pallas_call(
        kernel,
        grid_spec=pltpu.PrefetchScalarGridSpec(
            num_scalar_prefetch=1,
            grid=(count,),
            in_specs=[
                pl.BlockSpec((in_rows, rows), lambda s, me_ref: (offset_place(offsets, s, me_ref), 0)),
                whole_spec((rows, width)),
                whole_spec((rows, width)),
                pl.BlockSpec((rows, out_rows), lambda s, me_ref: (0, offset_place(offsets, s, me_ref))),
                whole_spec((rows, hidden_width)),
                whole_spec(router.shape),
                whole_spec((1, rows)),
            ],
            out_specs=(
                pl.BlockSpec((1, in_rows, hidden_width), give_at),
                pl.BlockSpec((1, in_rows, hidden_width), keep_at),
                pl.BlockSpec((1, out_rows, width), give_at),
                pl.BlockSpec((1, out_rows, width), keep_at),
            ),
            scratch_shapes=[pltpu.VMEM((rows, hidden_width), bf16), pltpu.VMEM((rows, width), bf16)],
        ),
        out_shape=(
            shape_of((half, in_rows, hidden_width), bf16),
            shape_of((half, in_rows, hidden_width), bf16),
            shape_of((half, out_rows, width), bf16),
            shape_of((half, out_rows, width), bf16),
        ),
        compiler_params=params(),
        cost_estimate=cost(4 * rows * width * hidden_width, 8 * width * hidden_width),
        name="expert_grads",
    )(me, rows_t, rows_in, grads, active, grad_hidden, router, others)


def combine_call(experts, heads, rows, places, gates, routes, cotangent, residual, ffn_low, smalls, w_output):
    tokens, width = cotangent.shape
    stride = rows.shape[1]
    capacity = stride - extra_rows

    def kernel(
        rows_ref, place_ref, gate_ref, routes_ref, cot_ref, res_ref, ffn_ref, small_ref, wo_ref,
        grad_res_ref, branch_ref, ctx_ref, router_ref, gain_ref,
    ):
        gate0, gate1 = gate_ref[:, 0:1], gate_ref[:, 1:2]
        lane_row = lax.broadcasted_iota(jnp.int32, (tokens, stride * experts), 1).astype(f32)
        rows = rows_ref[...].reshape(stride * experts, width)
        lane_slot = lax.broadcasted_iota(jnp.int32, (tokens, tile), 1).astype(f32)
        grad_ffn = jnp.zeros((tokens, width), f32)
        grad_gate = []
        for k, gate in enumerate((gate0, gate1)):
            first_row = routes_ref[:, k : k + 1].astype(f32) * stride
            place = place_ref[:, k : k + 1]
            back = (lane_row == first_row + place).astype(f32).astype(bf16)
            grad_ffn = grad_ffn + mm(back, rows) * gate
            coarse = (lane_row == first_row + capacity).astype(f32)
            fine = (lane_row == first_row + (capacity + 8)).astype(f32)
            dots = mm((coarse + fine).astype(bf16), rows[:, :tile])
            grad_gate.append(jnp.sum(jnp.where(lane_slot == place, dots, 0.0), axis=1, keepdims=True))
        grad_gate0, grad_gate1 = grad_gate
        mean_grad = gate0 * grad_gate0 + gate1 * grad_gate1
        chosen0 = gate0 * (grad_gate0 - mean_grad)
        chosen1 = gate1 * (grad_gate1 - mean_grad)
        numbers = lax.broadcasted_iota(jnp.int32, (tokens, experts), 1)
        hot0 = routes_ref[:, 0:1] == numbers
        hot1 = routes_ref[:, 1:2] == numbers
        grad_logits = jnp.where(hot0, chosen0, 0.0) + jnp.where(hot1, chosen1, 0.0)
        grad_logits = grad_logits.astype(bf16)
        router_ref[...] = t_mm(grad_logits, ffn_ref[...])
        grad_ffn = grad_ffn + mm(grad_logits, small_ref[0:experts, :].astype(bf16))
        gain = small_ref[experts + heads + 1 : experts + heads + 2, :]
        residual = res_ref[...]
        inverse = lax.rsqrt(jnp.mean(residual * residual, axis=-1, keepdims=True) + eps)
        scaled = grad_ffn * gain
        inner = jnp.mean(scaled * residual, axis=-1, keepdims=True)
        gain_ref[...] = jnp.sum(grad_ffn * residual * inverse, axis=0, keepdims=True)
        grad_res = cot_ref[...].astype(f32) + inverse * scaled - residual * (inverse * inverse * inverse * inner)
        grad_res_ref[...] = grad_res
        branch = grad_res.astype(bf16)
        branch_ref[...] = branch
        ctx_ref[...] = mm_t(branch, wo_ref[...]).astype(bf16)

    return pl.pallas_call(
        kernel,
        out_shape=(
            shape_of((tokens, width), f32),
            shape_of((tokens, width), bf16),
            shape_of((tokens, width), bf16),
            shape_of((experts, width), f32),
            shape_of((1, width), f32),
        ),
        compiler_params=params(),
        cost_estimate=cost(6 * tokens * width * width, 8 * width * width),
        name="combine",
    )(rows, places, gates, routes, cotangent, residual, ffn_low, smalls, w_output)


def split_rows(full_ref, me_index, count, shards, main, give_ref, keep_ref):
    for offset in range(count):
        place = lax.bitwise_xor(me_index, offset)
        target = give_ref if offset & 1 else keep_ref
        target[offset // 2, :, :main] = full_ref[
            pl.ds(pl.multiple_of(place * shards, shards), shards), :
        ].astype(bf16)


def small_tiles(pieces, rows, shards):
    per_tile = shards // rows
    return -(-pieces // per_tile), per_tile


def first_grads_call(me, dq, dk, dv, normed_t, context_low, branch, grad_router, grad_gain, table, count):
    tokens, part = dq.shape
    width, seq = normed_t.shape
    shards = width // count
    experts = grad_router.shape[0]
    heads, _, buckets = table.shape
    piece_rows = -(-(experts + 1) // 16) * 16
    pieces = width // tile + 1
    tiles, per_tile = small_tiles(pieces, piece_rows, shards)
    main = width + 3 * part

    def kernel(
        me_ref, dq_ref, dk_ref, dv_ref, normed_ref, ctx_ref, branch_ref, router_ref, gain_ref, table_ref,
        give_ref, keep_ref, full_ref,
    ):
        own = pl.ds(pl.multiple_of(me_ref[0] * tokens, tokens), tokens)
        full_ref[:, :width] = t_mm(ctx_ref[...], branch_ref[...])
        full_ref[:, width : width + part] = mm(normed_ref[:, own], dq_ref[...])
        full_ref[:, width + part : width + 2 * part] = mm(normed_ref[...], dk_ref[...])
        full_ref[:, width + 2 * part :] = mm(normed_ref[...], dv_ref[...])
        split_rows(full_ref, me_ref[0], count, shards, main, give_ref, keep_ref)
        small = jnp.concatenate(
            [router_ref[...], gain_ref[...], jnp.zeros((piece_rows - experts - 1, width), f32)], axis=0
        )
        rows = [table_ref[head] for head in range(heads)]
        rows = jnp.concatenate(rows + [jnp.zeros((piece_rows - heads, buckets), f32)], axis=0)
        rows = jnp.concatenate([rows, jnp.zeros((piece_rows, tile - buckets), f32)], axis=1)
        blocks = [small[:, at : at + tile] for at in range(0, width, tile)] + [rows]
        blocks = [block.astype(bf16) for block in blocks]
        for target in (give_ref, keep_ref):
            for at in range(count // 2):
                target[at, :, main:] = jnp.zeros((shards, tiles * tile), bf16)
                for index, block in enumerate(blocks):
                    row = index % per_tile * piece_rows
                    col = main + index // per_tile * tile
                    target[at, row : row + piece_rows, col : col + tile] = block

    vmem = pl.BlockSpec(memory_space=pltpu.VMEM)
    return pl.pallas_call(
        kernel,
        in_specs=[pl.BlockSpec(memory_space=pltpu.SMEM)] + [vmem] * 9,
        out_shape=(shape_of((count // 2, shards, main + tiles * tile), bf16),) * 2,
        scratch_shapes=[pltpu.VMEM((width, main), f32)],
        compiler_params=params(),
        cost_estimate=cost(5 * seq * width * part, 10 * seq * width),
        name="first_grads",
    )(me, dq, dk, dv, normed_t, context_low, branch, grad_router, grad_gain, table)


def first_smalls(columns, experts, heads, buckets, width, shards):
    piece_rows = -(-(experts + 1) // 16) * 16
    pieces = width // tile + 1
    _, per_tile = small_tiles(pieces, piece_rows, shards)
    found = []
    for index in range(pieces):
        row, col = index % per_tile * piece_rows, index // per_tile * tile
        found.append(columns[row : row + piece_rows, col : col + tile])
    wide = jnp.concatenate(found[:-1], axis=1)
    return wide[:experts], wide[experts], found[-1][:heads, :buckets]


def second_grads_call(me, dq, dk, dv, normed_t, table, count):
    tokens, part = dq.shape
    width, seq = normed_t.shape
    shards = width // count
    heads, _, buckets = table.shape
    main = 3 * part

    def kernel(me_ref, dq_ref, dk_ref, dv_ref, normed_ref, table_ref, give_ref, keep_ref, full_ref):
        own = pl.ds(pl.multiple_of(me_ref[0] * tokens, tokens), tokens)
        full_ref[:, :part] = mm(normed_ref[:, own], dq_ref[...])
        full_ref[:, part : 2 * part] = mm(normed_ref[...], dk_ref[...])
        full_ref[:, 2 * part :] = mm(normed_ref[...], dv_ref[...])
        split_rows(full_ref, me_ref[0], count, shards, main, give_ref, keep_ref)
        rows = [table_ref[head] for head in range(heads)]
        rows = jnp.concatenate(rows + [jnp.zeros((16 - heads, buckets), f32)], axis=0)
        rows = jnp.concatenate([rows, jnp.zeros((16, tile - buckets), f32)], axis=1).astype(bf16)
        for target in (give_ref, keep_ref):
            for at in range(count // 2):
                target[at, :, main:] = jnp.zeros((shards, tile), bf16)
                target[at, :16, main:] = rows

    vmem = pl.BlockSpec(memory_space=pltpu.VMEM)
    return pl.pallas_call(
        kernel,
        in_specs=[pl.BlockSpec(memory_space=pltpu.SMEM)] + [vmem] * 5,
        out_shape=(shape_of((count // 2, shards, main + tile), bf16),) * 2,
        scratch_shapes=[pltpu.VMEM((width, main), f32)],
        compiler_params=params(),
        cost_estimate=cost(5 * seq * width * part, 10 * seq * width),
        name="second_grads",
    )(me, dq, dk, dv, normed_t, table)


def rows_back_call(me, first, second, weights, count):
    tokens, part = first[0].shape
    width = weights[0].shape[0]

    def kernel(
        me_ref, dq1_ref, dk1_ref, dv1_ref, dq2_ref, dk2_ref, dv2_ref, wq_ref, wk_ref, wv_ref, give_ref, keep_ref,
    ):
        for offset in range(count):
            place = lax.bitwise_xor(me_ref[0], offset)
            at = pl.ds(pl.multiple_of(place * tokens, tokens), tokens)
            total = mm_t(dk1_ref[at, :], wk_ref[:, :part]) + mm_t(dk2_ref[at, :], wk_ref[:, part:])
            total = total + mm_t(dv1_ref[at, :], wv_ref[:, :part]) + mm_t(dv2_ref[at, :], wv_ref[:, part:])
            if offset == 0:
                total = total + mm_t(dq1_ref[...], wq_ref[:, :part]) + mm_t(dq2_ref[...], wq_ref[:, part:])
            target = give_ref if offset & 1 else keep_ref
            target[offset // 2] = total.astype(bf16)

    vmem = pl.BlockSpec(memory_space=pltpu.VMEM)
    return pl.pallas_call(
        kernel,
        in_specs=[pl.BlockSpec(memory_space=pltpu.SMEM)] + [vmem] * 9,
        out_shape=(shape_of((count // 2, tokens, width), bf16),) * 2,
        compiler_params=params(),
        cost_estimate=cost(10 * count * tokens * width * width, 10 * count * tokens * width),
        name="rows_back",
    )(me, *first, *second, *weights)


def finish_call(chain1, chain2, weights, gain, half_cols):
    shards, width = weights[0].shape
    rest = width - half_cols

    def kernel(c1_ref, c2_ref, wq_ref, wk_ref, wv_ref, gain_ref, gq_ref, gk_ref, gv_ref, go_ref, out_ref):
        total = jnp.zeros((shards, 1), f32)
        go_ref[...] = c1_ref[:, :width].astype(f32)
        for part, (weight_ref, grad_ref) in enumerate(((wq_ref, gq_ref), (wk_ref, gk_ref), (wv_ref, gv_ref))):
            left = c1_ref[:, width + part * half_cols : width + (part + 1) * half_cols].astype(f32)
            right = c2_ref[:, part * rest : (part + 1) * rest].astype(f32)
            grad_ref[:, :half_cols] = left
            grad_ref[:, half_cols:] = right
            weight = weight_ref[...].astype(f32)
            total = total + jnp.sum(left * weight[:, :half_cols], axis=1, keepdims=True)
            total = total + jnp.sum(right * weight[:, half_cols:], axis=1, keepdims=True)
        out_ref[...] = jnp.broadcast_to(total, (shards, tile)).T[0:1, :] / gain_ref[...].astype(f32)

    return pl.pallas_call(
        kernel,
        out_shape=(shape_of((shards, width), f32),) * 4 + (shape_of((1, shards), f32),),
        compiler_params=params(),
        cost_estimate=cost(6 * shards * width, 30 * shards * width),
        name="finish",
    )(chain1, chain2, *weights, gain[None, :])


def gather_blocks(value, axis_size):
    blocks = {0: value}
    bit = 2
    while bit < axis_size:
        for offset in sorted(blocks):
            blocks[offset | bit] = swap(blocks[offset], "fsdp", axis_size, bit)
        bit *= 2
    for offset in sorted(blocks):
        blocks[offset | 1] = swap(blocks[offset], "fsdp", axis_size, 1)
    return [blocks[offset] for offset in range(axis_size)]


def scatter_bits(axis_size):
    bits, bit = [1], axis_size // 2
    while bit > 1:
        bits.append(bit)
        bit //= 2
    return [bit for bit in bits if bit < axis_size]


def added(left_side, right_side):
    return left_side.astype(f32) + right_side.astype(f32)


def core_sum(given, kept, axis_size):
    arrived = swap(given, "fsdp", axis_size, 1)
    return {2 * at: added(kept[at], arrived[at]).astype(bf16) for at in range(axis_size // 2)}


def far_sum(pieces, axis_size, early=None, late=None, cuts=1):
    for bit in scatter_bits(axis_size):
        if bit == 1:
            continue
        left = {}
        for offset in sorted(pieces):
            if offset & bit:
                continue
            found = []
            for leaving in jnp.split(pieces[offset | bit].astype(bf16), cuts, axis=0):
                if early is not None:
                    leaving = ordered(leaving, early)[0]
                found.append(swap(leaving, "fsdp", axis_size, bit))
                early = found[-1]
            if late is not None:
                found[-1] = ordered(found[-1], late)[0]
            left[offset] = added(pieces[offset], jnp.concatenate(found, axis=0))
        pieces = left
    return pieces[0]


def far_steps(pieces, axis_size, fractions, early=None):
    bits = [bit for bit in scatter_bits(axis_size) if bit > 1]
    for bit in bits[:-1]:
        pieces = {
            offset: added(
                pieces[offset], swap(pieces[offset | bit].astype(bf16), "fsdp", axis_size, bit)
            )
            for offset in sorted(pieces)
            if not offset & bit
        }
    bit = bits[-1]
    rows = pieces[0].shape[0]
    leaving = pieces[bit].astype(bf16)
    found, begin = [], 0
    for step, fraction in enumerate(fractions):
        end = rows if step == len(fractions) - 1 else begin + rows * fraction // 12
        part = leaving[begin:end]
        if early is not None:
            part = ordered(part, early)[0]
        early = yield swap(part, "fsdp", axis_size, bit)
        found.append(early)
        begin = end
    yield added(pieces[0], jnp.concatenate(found, axis=0))


def all_sum_expert(value, axis_size, index, before_last=None):
    rows = value.shape[0]
    parts = jnp.pad(value.astype(bf16), ((0, -rows % (axis_size // 2)), (0, 0)))
    bit, bits = 1, []
    while bit < axis_size:
        bits.append(bit)
        bit *= 2
    inner = bits.pop()
    first_arrived = None
    for bit in bits:
        low_half, high_half = jnp.split(parts, 2, axis=0)
        upper = (index & bit) != 0
        keep = jnp.where(upper, high_half, low_half)
        give = jnp.where(upper, low_half, high_half)
        arrived = swap(give, "expert", axis_size, bit)
        first_arrived = arrived if first_arrived is None else first_arrived
        parts = added(keep, arrived).astype(bf16)
    parts = added(parts, swap(parts, "expert", axis_size, inner)).astype(bf16)
    for bit in reversed(bits):
        if bit == 1 and before_last is not None:
            parts = ordered(parts, before_last)[0]
        other = swap(parts, "expert", axis_size, bit)
        upper = (index & bit) != 0
        parts = jnp.concatenate(
            [jnp.where(upper, other, parts), jnp.where(upper, parts, other)], axis=0
        )
    return parts[:rows], first_arrived


def ordered(*values):
    return lax.optimization_barrier(values)


def build(count, expert_ranks):
    def per_device(
        tokens_in,
        seg_ids,
        routes,
        buckets,
        attn_gain,
        w_query,
        w_key,
        w_value,
        w_output,
        bias_table,
        ffn_gain,
        w_router,
        w_in,
        w_out,
        cotangent,
    ):
        tokens, width = tokens_in.shape
        shards, experts = w_router.shape
        bucket_rows, heads = bias_table.shape
        bucket_count = bucket_rows * count
        head_dim = width // heads
        seq = buckets.shape[0]
        top_count = routes.shape[1]
        capacity = 3 * top_count * tokens // (2 * experts)
        slots = experts * capacity
        fsdp_index = lax.axis_index("fsdp")
        expert_index = lax.axis_index("expert")
        me = jnp.stack([fsdp_index, expert_index]).astype(jnp.int32)

        used = experts + heads + 3
        small_rows = -(-used // 16) * 16
        packed = pack_call(
            me, (w_query, w_key, w_value), tokens_in, seg_ids[None, :],
            jnp.stack([attn_gain, ffn_gain]), bias_table, w_router.T, small_rows, width,
        )
        blocks = gather_blocks(packed, count)
        out_blocks = gather_blocks(ordered(w_output, blocks[-2])[0], count)
        routes, blocks[1] = ordered(routes, blocks[1])
        padded_buckets = jnp.concatenate([jnp.full((seq,), -1, jnp.int32), buckets])
        bucket_window = lax.dynamic_slice_in_dim(
            padded_buckets, fsdp_index * tokens, seq + tokens, 0
        )[None, :]

        slot_map, back0, back1, grad_rows_out, places = route_call(routes, cotangent, capacity, experts)
        grad_rows_in = lax.all_to_all(
            grad_rows_out, "expert", split_axis=0, concat_axis=0, tiled=True
        )
        others = grad_rows_in[:, capacity, :capacity].reshape(1, slots)
        grad_rows_in = grad_rows_in[:, :capacity, :].reshape(slots, width)

        (queries, keys, values, normed, sequence, wq, wk, wv, smalls, bias, mask) = project_call(
            me, blocks, shards, small_rows, bucket_window, heads, bucket_count, experts
        )
        queries, grad_rows_in, others = ordered(queries, grad_rows_in, others)
        context, lse = attend_call(queries, keys, values, bias, mask, head_dim)
        wo, context_low, residual, ffn_low, gates, rows_out = dispatch_call(
            me, context, out_blocks, tokens_in, smalls, routes, slot_map, heads
        )(experts)
        normed_t = ordered(normed, rows_out)[0].T
        rows_in = lax.all_to_all(
            rows_out.reshape(experts, capacity, width),
            "expert",
            split_axis=0,
            concat_axis=0,
            tiled=True,
        ).reshape(slots, width)
        rows_in, normed_t = ordered(rows_in, normed_t)
        active, grad_hidden, made, row_grads = expert_call(
            rows_in, grad_rows_in, w_in[0], w_out[0], experts
        )
        row_grads_back = lax.all_to_all(
            row_grads, "expert", split_axis=0, concat_axis=0, tiled=True
        )

        rows_t = rows_in.T
        give = [offset for offset in range(count) if offset & 1]
        keep = [offset for offset in range(count) if not offset & 1]
        router = smalls[:experts]
        in_give, in_keep, out_give, out_keep = expert_grads_call(
            me, rows_t, rows_in, grad_rows_in, active, grad_hidden, router, others, give + keep
        )
        in_give, out_give, row_grads_back = ordered(in_give, out_give, row_grads_back)
        in_pieces = core_sum(in_give, in_keep, count)
        out_pieces = core_sum(out_give, out_keep, count)

        grad_residual, branch, grad_context, grad_router, grad_gain_ffn = combine_call(
            experts, heads, row_grads_back, places, gates, routes, cotangent,
            residual, ffn_low, smalls, wo,
        )
        pairs = width // tile
        near = pairs // 2
        last = max(in_pieces)
        grad_context, in_pieces[last] = ordered(grad_context, in_pieces[last])
        *part1, table1 = attend_back_call(
            queries, keys, values, bias, mask, lse, context, grad_context, bucket_window,
            bucket_count, head_dim, 0, near,
        )
        in_steps = far_steps(in_pieces, count, (5, 3, 4))
        arrived = next(in_steps)
        part1[0], arrived = ordered(part1[0], arrived)
        give1, keep1 = first_grads_call(
            me, *part1, normed_t, context_low, branch, grad_router, grad_gain_ffn, table1, count
        )
        arrived = in_steps.send(arrived)
        made = ordered(made, give1)[0]
        made_back = lax.all_to_all(
            made.reshape(experts, capacity, width),
            "expert",
            split_axis=0,
            concat_axis=0,
            tiled=True,
        ).reshape(slots, width)
        pieces1 = core_sum(give1, keep1, count)
        last = max(pieces1)
        grad_context, pieces1[last], arrived = ordered(grad_context, pieces1[last], arrived)
        *part2, table2 = attend_back_call(
            queries, keys, values, bias, mask, lse, context, grad_context, bucket_window,
            bucket_count, head_dim, near, pairs - near,
        )
        give2, keep2 = second_grads_call(me, *part2, normed_t, table2, count)
        sum1 = far_sum(pieces1, count, None, give2)
        rows_give, rows_keep = rows_back_call(me, part1, part2, (wq, wk, wv), count)
        sum2 = far_sum(core_sum(give2, keep2, count), count)
        arrived = in_steps.send(ordered(arrived, sum1)[0])
        in_sum = in_steps.send(arrived)
        out_steps = far_steps(out_pieces, count, (6, 6), arrived)
        arrived = out_steps.send(ordered(next(out_steps), sum2)[0])
        out_sum = out_steps.send(arrived)
        grad_shards = [in_sum, out_sum]
        chain1, _ = all_sum_expert(sum1, expert_ranks, expert_index)
        chain2, first_arrived = all_sum_expert(sum2, expert_ranks, expert_index)
        half_cols = near * tile

        grad_normed = far_sum(core_sum(rows_give, rows_keep, count), count, sum2)
        inputs = tokens_in.astype(f32)
        inverse = lax.rsqrt(jnp.mean(inputs * inputs, axis=-1, keepdims=True) + eps)
        gain_attn = smalls[experts + heads]
        scaled = grad_normed * gain_attn
        inner = jnp.mean(scaled * inputs, axis=-1, keepdims=True)
        grad_tokens = grad_residual + inverse * scaled - inputs * inverse**3 * inner

        made_back = ordered(made_back, sum2)[0]
        picked0 = mm(back0, made_back)
        picked1 = mm(back1, made_back)
        block_out = (residual + gates[:, 0:1] * picked0 + gates[:, 1:2] * picked1).astype(bf16)

        rest = width - half_cols
        *shards_out, grad_gain_attn = finish_call(
            chain1, chain2, (w_query, w_key, w_value), attn_gain, half_cols
        )
        router_sum, gain_sum, table_left = first_smalls(
            chain1[:, width + 3 * half_cols :].astype(f32), experts, 2 * near, bucket_count, width, shards
        )
        table_right = chain2[: heads - 2 * near, 3 * rest : 3 * rest + bucket_count].astype(f32)
        table_cols = lax.dynamic_slice_in_dim(
            jnp.concatenate([table_left, table_right], axis=0), fsdp_index * bucket_rows, bucket_rows, 1
        )
        return (
            block_out,
            grad_tokens,
            grad_gain_attn[0],
            shards_out[0],
            shards_out[1],
            shards_out[2],
            shards_out[3],
            table_cols.T,
            lax.dynamic_slice_in_dim(gain_sum, fsdp_index * shards, shards, 0),
            lax.dynamic_slice_in_dim(router_sum, fsdp_index * shards, shards, 1).T,
            grad_shards[0][None],
            grad_shards[1][None],
        )

    return per_device


def solution(mesh):
    return jax.shard_map(
        build(mesh.shape["fsdp"], mesh.shape["expert"]),
        mesh=mesh,
        in_specs=(
            P(("expert", "fsdp"), None),
            P(("expert", "fsdp")),
            P(("expert", "fsdp"), None),
            P(),
            P("fsdp"),
            P("fsdp", None),
            P("fsdp", None),
            P("fsdp", None),
            P("fsdp", None),
            P("fsdp", None),
            P("fsdp"),
            P("fsdp", None),
            P("expert", None, None),
            P("expert", None, None),
            P(("expert", "fsdp"), None),
        ),
        out_specs=(
            P(("expert", "fsdp"), None),
            P(("expert", "fsdp"), None),
            P("fsdp"),
            P("fsdp", None),
            P("fsdp", None),
            P("fsdp", None),
            P("fsdp", None),
            P("fsdp", None),
            P("fsdp"),
            P("fsdp", None),
            P("expert", "fsdp", None),
            P("expert", "fsdp", None),
        ),
        check_vma=False,
    )
```

```python
import math

import jax
import jax.numpy as jnp
from jax import lax
from jax.experimental import pallas as pl
from jax.experimental.pallas import tpu as pltpu
from jax.sharding import PartitionSpec as P

eps = 1e-06
log2e = math.log2(math.e)
masked_score = -1e30
f32 = jnp.float32
bf16 = jnp.bfloat16
tile = 128
extra_rows = 16


def mm(left_side, right_side):
    return lax.dot_general(
        left_side, right_side, (((1,), (0,)), ((), ())), preferred_element_type=f32
    )


def mm_t(left_side, right_side):
    return lax.dot_general(
        left_side, right_side, (((1,), (1,)), ((), ())), preferred_element_type=f32
    )


def t_mm(left_side, right_side):
    return lax.dot_general(
        left_side, right_side, (((0,), (0,)), ((), ())), preferred_element_type=f32
    )


def swap(value, axis_name, axis_size, bit):
    return lax.ppermute(value, axis_name, [(i, i ^ bit) for i in range(axis_size)])


def params(megabytes=56):
    return pltpu.CompilerParams(vmem_limit_bytes=megabytes << 20)


def cost(flops, moved):
    return pl.CostEstimate(flops=int(flops) >> 8, bytes_accessed=int(moved) >> 8, transcendentals=0)


def shape_of(dims, dtype):
    return jax.ShapeDtypeStruct(dims, dtype)


def whole_spec(dims):
    return pl.BlockSpec(dims, lambda *unused: (0,) * len(dims))


def to_column(row):
    return jnp.broadcast_to(row, (tile, row.shape[1])).T


def route_kernel(capacity, routes_ref, cot_ref, map_ref, back0_ref, back1_ref, out_ref, slot_ref):
    tokens = routes_ref.shape[0]
    slots = map_ref.shape[0]
    experts = slots // capacity
    routes = routes_ref[...]
    first, second = routes[:, 0:1], routes[:, 1:2]
    numbers = lax.broadcasted_iota(jnp.int32, (tokens, experts), 1)
    hot0 = (first == numbers).astype(f32)
    hot1 = (second == numbers).astype(f32)
    rows = lax.broadcasted_iota(jnp.int32, (tokens, tokens), 0)
    cols = lax.broadcasted_iota(jnp.int32, (tokens, tokens), 1)
    before = (cols < rows).astype(f32).astype(bf16)
    earlier = mm(before, (hot0 + hot1).astype(bf16))
    slot0 = jnp.sum(hot0 * earlier, axis=1, keepdims=True)
    slot1 = jnp.sum(hot1 * (earlier + hot0), axis=1, keepdims=True)
    slot_ref[...] = jnp.concatenate([slot0, slot1], axis=1)
    dest0 = first.astype(f32) * capacity + slot0
    dest1 = second.astype(f32) * capacity + slot1
    lane_slot = lax.broadcasted_iota(jnp.int32, (tokens, slots), 1).astype(f32)
    back0_ref[...] = (lane_slot == dest0).astype(f32).astype(bf16)
    back1_ref[...] = (lane_slot == dest1).astype(f32).astype(bf16)
    row0 = jnp.broadcast_to(dest0, (tokens, tile)).T[0:1, :]
    row1 = jnp.broadcast_to(dest1, (tokens, tile)).T[0:1, :]
    row_slot = lax.broadcasted_iota(jnp.int32, (slots, tokens), 0).astype(f32)
    hot = ((row_slot == row0).astype(f32) + (row_slot == row1).astype(f32)).astype(bf16)
    map_ref[...] = hot
    rows = mm(hot, cot_ref[...]).astype(bf16)
    others = back0_ref[...].astype(f32) * second.astype(f32) + back1_ref[...].astype(f32) * first.astype(f32)
    others = jnp.broadcast_to(jnp.sum(others, axis=0, keepdims=True), (extra_rows, slots))
    width = rows.shape[1]
    for expert in range(experts):
        at = expert * capacity
        lanes = pltpu.roll(others, (slots - at) % slots, 1)[:, :tile]
        lanes = jnp.concatenate([lanes, jnp.zeros((extra_rows, width - tile), f32)], axis=1)
        out_ref[expert, :capacity, :] = rows[at : at + capacity, :]
        out_ref[expert, capacity:, :] = lanes.astype(bf16)


def route_call(routes, cotangent, capacity, experts):
    tokens, width = cotangent.shape
    slots = experts * capacity
    return pl.pallas_call(
        lambda *refs: route_kernel(capacity, *refs),
        out_shape=(
            shape_of((slots, tokens), bf16),
            shape_of((tokens, slots), bf16),
            shape_of((tokens, slots), bf16),
            shape_of((experts, capacity + extra_rows, width), bf16),
            shape_of((tokens, 2), f32),
        ),
        compiler_params=params(),
        cost_estimate=cost(2 * slots * tokens * width, 4 * slots * width),
        name="route",
    )(routes, cotangent)


def pack_call(me, weights, tokens_in, seg_row, gains, table, router, small, width):
    shards = weights[0].shape[0]
    tokens = tokens_in.shape[0]
    experts, heads = router.shape[0], table.shape[1]
    used = experts + heads + 3

    def placed(me_ref, rows):
        at = lax.broadcasted_iota(jnp.int32, (rows, width), 1)
        own = lax.broadcasted_iota(jnp.int32, (rows, width), 0) + me_ref[0] * rows
        return (at == own).astype(f32).astype(bf16)

    def kernel(me_ref, wq_ref, wk_ref, wv_ref, x_ref, seg_ref, gain_ref, table_ref, router_ref, out_ref):
        for at, ref in enumerate((wq_ref, wk_ref, wv_ref)):
            out_ref[at * shards : (at + 1) * shards, :] = ref[...]
        out_ref[3 * shards : 3 * shards + tokens, :] = x_ref[...]
        columns = placed(me_ref, shards)
        rows = [
            mm(router_ref[...], columns),
            t_mm(table_ref[...], placed(me_ref, table_ref.shape[0])),
            mm(gain_ref[...], columns),
            jnp.zeros((small - used, width), f32),
            jnp.concatenate([seg_ref[...].astype(f32), jnp.zeros((1, width - tokens), f32)], axis=1),
        ]
        out_ref[3 * shards + tokens :, :] = jnp.concatenate(rows, axis=0).astype(bf16)

    vmem = pl.BlockSpec(memory_space=pltpu.VMEM)
    return pl.pallas_call(
        kernel,
        in_specs=[pl.BlockSpec(memory_space=pltpu.SMEM)] + [vmem] * 8,
        out_shape=shape_of((3 * shards + tokens + small, width), bf16),
        compiler_params=params(),
        cost_estimate=cost(1, 4 * shards * width),
        name="pack",
    )(me, *weights, tokens_in, seg_row, gains, table, router)


def project_call(me, blocks, shards, small, bucket_window, heads, buckets, experts):
    count = len(blocks)
    rows, width = blocks[0].shape
    tokens = rows - 3 * shards - small
    seq = count * tokens
    window = bucket_window.shape[1]

    def kernel(me_ref, *refs):
        block_refs = refs[:count]
        (bucket_ref, q_ref, k_ref, v_ref, normed_ref, tok_ref, wq_ref, wk_ref, wv_ref, small_ref, bias_ref, mask_ref) = refs[count:]
        me_index = me_ref[0]
        totals = jnp.zeros((small, width), f32)
        own_docs = block_refs[0][rows - small :, :].astype(f32)[small - 1 :, :tokens]
        for offset in range(count):
            place = lax.bitwise_xor(me_index, offset)
            row = pl.multiple_of(place * shards, shards)
            for part, full_ref in enumerate((wq_ref, wk_ref, wv_ref)):
                full_ref[pl.ds(row, shards), :] = block_refs[offset][part * shards : (part + 1) * shards, :]
            token_row = pl.multiple_of(place * tokens, tokens)
            tok_ref[pl.ds(token_row, tokens), :] = block_refs[offset][3 * shards : rows - small, :]
            extra = block_refs[offset][rows - small :, :].astype(f32)
            totals = totals + extra
            docs = to_column(extra[small - 1 :, :tokens])
            docs = jnp.concatenate([docs] * (tokens // tile), axis=1)
            mask_ref[pl.ds(token_row, tokens), :] = jnp.where(docs == own_docs, 0.0, masked_score)
        small_ref[...] = totals
        gain = totals[experts + heads : experts + heads + 1, :]
        table = totals[experts : experts + heads, :buckets].astype(bf16)
        numbers = lax.broadcasted_iota(jnp.int32, (buckets, window), 0)
        hot = (numbers == bucket_ref[...]).astype(f32).astype(bf16)
        by_distance = mm(table, hot) * log2e
        by_distance = jnp.where(bucket_ref[...] < 0, masked_score, by_distance)
        for head in range(heads):
            bias_ref[head] = by_distance[head : head + 1, :]

        @pl.loop(0, count)
        def chunk(index):
            rows = pl.ds(pl.multiple_of(index * tokens, tokens), tokens)
            values = tok_ref[rows, :].astype(f32)
            inverse = lax.rsqrt(jnp.mean(values * values, axis=-1, keepdims=True) + eps)
            normed = (values * inverse * gain).astype(bf16)
            normed_ref[rows, :] = normed
            k_ref[rows, :] = mm(normed, wk_ref[...]).astype(bf16)
            v_ref[rows, :] = mm(normed, wv_ref[...]).astype(bf16)

        own = normed_ref[pl.ds(pl.multiple_of(me_index * tokens, tokens), tokens), :]
        q_ref[...] = mm(own, wq_ref[...]).astype(bf16)

    vmem = pl.BlockSpec(memory_space=pltpu.VMEM)
    return pl.pallas_call(
        kernel,
        in_specs=[pl.BlockSpec(memory_space=pltpu.SMEM)] + [vmem] * (count + 1),
        out_shape=(
            shape_of((tokens, width), bf16),
            shape_of((seq, width), bf16),
            shape_of((seq, width), bf16),
            shape_of((seq, width), bf16),
            shape_of((seq, width), bf16),
            shape_of((width, width), bf16),
            shape_of((width, width), bf16),
            shape_of((width, width), bf16),
            shape_of((small, width), f32),
            shape_of((heads, 1, window), f32),
            shape_of((seq, tokens), f32),
        ),
        compiler_params=params(),
        cost_estimate=cost(2 * width * width * (2 * seq + tokens), 20 * seq * width),
        name="project",
    )(me, *blocks, bucket_window)


def skewed(bias_row, window):
    spread = jnp.broadcast_to(bias_row, (tile, window))
    return pltpu.roll(spread, 0, 1, stride=1, stride_axis=0)


def attend_call(queries, keys, values, bias, mask, head_dim):
    tokens, width = queries.shape
    seq = keys.shape[0]
    heads, _, window = bias.shape
    pairs = width // tile
    per_step = heads // pairs
    key_blocks = seq // tile
    scale = head_dim**-0.5 * log2e

    def kernel(q_ref, k_ref, v_ref, bias_ref, mask_ref, ctx_ref, lse_ref, score_ref, prob_ref, skew_ref):
        lane = lax.broadcasted_iota(jnp.int32, (tokens, tile), 1)
        row = lax.broadcasted_iota(jnp.int32, (tile, tokens), 0)
        query = q_ref[...]
        values_t = v_ref[...].T
        result = jnp.zeros((tile, tokens), f32)
        for half in range(per_step):
            mine = jnp.where(lane // head_dim == half, query, jnp.zeros_like(query))
            skew_ref[...] = skewed(bias_ref[half], window)
            top = jnp.full((8, tokens), -3e38, f32)
            for block in range(key_blocks):
                rows = pl.ds(block * tile, tile)
                begin = tile * (key_blocks - block)
                scores = mm_t(k_ref[rows, :], mine) * scale
                scores = scores + (skew_ref[:, begin : begin + tokens] + mask_ref[rows, :])
                score_ref[rows, :] = scores
                top = jnp.maximum(top, jnp.max(scores.reshape(tile // 8, 8, tokens), axis=0))
            top = jnp.max(top, axis=0, keepdims=True)
            total = jnp.zeros((8, tokens), f32)
            for block in range(key_blocks):
                rows = pl.ds(block * tile, tile)
                probs = jnp.exp2(score_ref[rows, :] - top)
                prob_ref[rows, :] = probs.astype(bf16)
                total = total + jnp.sum(probs.reshape(tile // 8, 8, tokens), axis=0)
            total = jnp.sum(total, axis=0, keepdims=True)
            lse_ref[half] = top + jnp.log2(total)
            mixed = mm(values_t, prob_ref[...]) * (1.0 / total)
            result = jnp.where(row // head_dim == half, mixed, result)
        ctx_ref[...] = result.T

    return pl.pallas_call(
        kernel,
        grid=(pairs,),
        in_specs=[
            pl.BlockSpec((tokens, tile), lambda p: (0, p)),
            pl.BlockSpec((seq, tile), lambda p: (0, p)),
            pl.BlockSpec((seq, tile), lambda p: (0, p)),
            pl.BlockSpec((per_step, 1, window), lambda p: (p, 0, 0)),
            pl.BlockSpec((seq, tokens), lambda p: (0, 0)),
        ],
        out_specs=(
            pl.BlockSpec((tokens, tile), lambda p: (0, p)),
            pl.BlockSpec((per_step, 1, tokens), lambda p: (p, 0, 0)),
        ),
        out_shape=(shape_of((tokens, width), f32), shape_of((heads, 1, tokens), f32)),
        scratch_shapes=[
            pltpu.VMEM((seq, tokens), f32),
            pltpu.VMEM((seq, tokens), bf16),
            pltpu.VMEM((tile, window), f32),
        ],
        compiler_params=params(),
        cost_estimate=cost(16 * heads * tokens * seq * tile, 4 * seq * width),
        name="attend",
    )(queries, keys, values, bias, mask)


def unskewed(total):
    window = total.shape[1]
    rows = total.shape[0]
    while rows > 8:
        rows = rows // 2
        total = total[:rows, :] + pltpu.roll(total[rows:, :], window - rows, 1)
    step = 4
    while step:
        moved = pltpu.roll(pltpu.roll(total, 8 - step, 0), window - step, 1)
        total = total + moved
        step = step // 2
    return total[0:1, :]


def attend_back_call(queries, keys, values, bias, mask, lse, context, grad_context, bucket_window, buckets, head_dim, first, pairs):
    tokens, width = queries.shape
    seq = keys.shape[0]
    heads, _, window = bias.shape
    per_step = heads // (width // tile)
    key_blocks = seq // tile
    scale = head_dim**-0.5

    def kernel(
        q_ref, k_ref, v_ref, bias_ref, mask_ref, lse_ref, ctx_ref, grad_ref, bucket_ref,
        dq_ref, dk_ref, dv_ref, table_ref, prob_ref, ds_ref, skew_ref, sum_ref,
    ):
        lane = lax.broadcasted_iota(jnp.int32, (tokens, tile), 1)
        row = lax.broadcasted_iota(jnp.int32, (tile, tokens), 0)
        query = q_ref[...]
        grad = grad_ref[...]
        keys_t = k_ref[...].T
        products = (grad.astype(f32) * ctx_ref[...]).T
        result = jnp.zeros((tile, tokens), f32)
        numbers = lax.broadcasted_iota(jnp.int32, (buckets, window), 0)
        hot = (numbers == bucket_ref[...]).astype(f32)
        mine_q, mine_g = [], []
        for half in range(per_step):
            mine_q.append(jnp.where(lane // head_dim == half, query, jnp.zeros_like(query)))
            mine_g.append(jnp.where(lane // head_dim == half, grad, jnp.zeros_like(grad)))
        for half in range(per_step):
            delta = jnp.sum(
                products[half * head_dim : (half + 1) * head_dim, :], axis=0, keepdims=True
            )
            lse_row = lse_ref[half]
            skew_ref[...] = skewed(bias_ref[half], window)
            sum_ref[...] = jnp.zeros((tile, window), f32)
            cols = slice(half * tokens, (half + 1) * tokens)
            for block in range(key_blocks):
                rows = pl.ds(block * tile, tile)
                begin = tile * (key_blocks - block)
                scores = mm_t(k_ref[rows, :], mine_q[half]) * (scale * log2e)
                scores = scores + (skew_ref[:, begin : begin + tokens] + mask_ref[rows, :])
                probs = jnp.exp2(scores - lse_row)
                grad_probs = mm_t(v_ref[rows, :], mine_g[half])
                grad_scores = (probs * (grad_probs - delta)).astype(bf16)
                prob_ref[rows, cols] = probs.astype(bf16)
                ds_ref[rows, cols] = grad_scores
                sum_ref[:, begin : begin + tokens] += grad_scores.astype(f32)
            grad_q = mm(keys_t, ds_ref[:, cols])
            result = jnp.where(row // head_dim == half, grad_q, result)
            by_distance = unskewed(sum_ref[...])
            column = jnp.sum(hot * by_distance, axis=1, keepdims=True)
            table_ref[half] = jnp.broadcast_to(column, (buckets, tile)).T[0:1, :]
        dq_ref[...] = (result * scale).T.astype(bf16)
        dk_ref[...] = (mm(ds_ref[...], jnp.concatenate(mine_q, axis=0)) * scale).astype(bf16)
        dv_ref[...] = mm(prob_ref[...], jnp.concatenate(mine_g, axis=0)).astype(bf16)

    narrow = pl.BlockSpec((tokens, tile), lambda p: (0, p + first))
    tall = pl.BlockSpec((seq, tile), lambda p: (0, p + first))
    narrow_out = pl.BlockSpec((tokens, tile), lambda p: (0, p))
    tall_out = pl.BlockSpec((seq, tile), lambda p: (0, p))
    return pl.pallas_call(
        kernel,
        grid=(pairs,),
        in_specs=[
            narrow,
            tall,
            tall,
            pl.BlockSpec((per_step, 1, window), lambda p: (p + first, 0, 0)),
            pl.BlockSpec((seq, tokens), lambda p: (0, 0)),
            pl.BlockSpec((per_step, 1, tokens), lambda p: (p + first, 0, 0)),
            narrow,
            narrow,
            pl.BlockSpec((1, window), lambda p: (0, 0)),
        ],
        out_specs=(
            narrow_out,
            tall_out,
            tall_out,
            pl.BlockSpec((per_step, 1, buckets), lambda p: (p, 0, 0)),
        ),
        out_shape=(
            shape_of((tokens, pairs * tile), bf16),
            shape_of((seq, pairs * tile), bf16),
            shape_of((seq, pairs * tile), bf16),
            shape_of((pairs * per_step, 1, buckets), f32),
        ),
        scratch_shapes=[
            pltpu.VMEM((seq, per_step * tokens), bf16),
            pltpu.VMEM((seq, per_step * tokens), bf16),
            pltpu.VMEM((tile, window), f32),
            pltpu.VMEM((tile, window), f32),
        ],
        compiler_params=params(),
        cost_estimate=cost(40 * pairs * per_step * tokens * seq * tile, 8 * seq * pairs * tile),
        name="attend_back",
    )(queries, keys, values, bias, mask, lse, context, grad_context, bucket_window)


def chosen_logits(routes, logits):
    numbers = lax.broadcasted_iota(jnp.int32, logits.shape, 1)
    hot0 = routes[:, 0:1] == numbers
    hot1 = routes[:, 1:2] == numbers
    return hot0, hot1


def dispatch_call(me, context, out_blocks, tokens_in, smalls, routes, slot_map, heads):
    tokens, width = tokens_in.shape
    count = len(out_blocks)
    shards = out_blocks[0].shape[0]
    slots = slot_map.shape[0]

    def make(experts):
        def kernel(me_ref, ctx_ref, *refs):
            block_refs = refs[:count]
            (x_ref, small_ref, routes_ref, map_ref, wo_ref, low_ref, res_ref, ffn_ref, gate_ref, rows_ref) = refs[count:]
            for offset in range(count):
                place = lax.bitwise_xor(me_ref[0], offset)
                wo_ref[pl.ds(pl.multiple_of(place * shards, shards), shards), :] = block_refs[offset][...]
            context_low = ctx_ref[...].astype(bf16)
            low_ref[...] = context_low
            residual = x_ref[...].astype(f32) + mm(context_low, wo_ref[...])
            res_ref[...] = residual
            gain = small_ref[experts + heads + 1 : experts + heads + 2, :]
            inverse = lax.rsqrt(jnp.mean(residual * residual, axis=-1, keepdims=True) + eps)
            ffn_low = (residual * inverse * gain).astype(bf16)
            ffn_ref[...] = ffn_low
            rows_ref[...] = mm(map_ref[...], ffn_low).astype(bf16)
            logits = mm_t(ffn_low, small_ref[0:experts, :].astype(bf16))
            hot0, hot1 = chosen_logits(routes_ref[...], logits)
            first = jnp.sum(jnp.where(hot0, logits, 0.0), axis=1, keepdims=True)
            second = jnp.sum(jnp.where(hot1, logits, 0.0), axis=1, keepdims=True)
            top = jnp.maximum(first, second)
            weight0 = jnp.exp(first - top)
            weight1 = jnp.exp(second - top)
            whole = weight0 + weight1
            gate0 = weight0 / whole
            gate1 = weight1 / whole
            gate_ref[...] = jnp.concatenate([gate0, gate1], axis=1)

        return kernel

    def run(experts):
        vmem = pl.BlockSpec(memory_space=pltpu.VMEM)
        return pl.pallas_call(
            make(experts),
            in_specs=[pl.BlockSpec(memory_space=pltpu.SMEM)] + [vmem] * (count + 5),
            out_shape=(
                shape_of((width, width), bf16),
                shape_of((tokens, width), bf16),
                shape_of((tokens, width), f32),
                shape_of((tokens, width), bf16),
                shape_of((tokens, 2), f32),
                shape_of((slots, width), bf16),
            ),
            compiler_params=params(),
            cost_estimate=cost(4 * tokens * width * width, 8 * width * width),
            name="dispatch",
        )(me, context, *out_blocks, tokens_in, smalls, routes, slot_map)

    return run


def upstream_call(grads, expert_out):
    count, width = grads.shape
    hidden_width = expert_out.shape[0]
    step_width = 512

    def kernel(g_ref, out_ref, up_ref):
        up_ref[...] = mm_t(g_ref[...], out_ref[...])

    return pl.pallas_call(
        kernel,
        grid=(hidden_width // step_width,),
        in_specs=[whole_spec((count, width)), pl.BlockSpec((step_width, width), lambda s: (s, 0))],
        out_specs=pl.BlockSpec((count, step_width), lambda s: (0, s)),
        out_shape=shape_of((count, hidden_width), f32),
        compiler_params=params(),
        cost_estimate=cost(2 * count * width * hidden_width, 6 * count * hidden_width),
        name="upstream",
    )(grads, expert_out)


def expert_call(rows, grads, upstream, expert_in, expert_out, experts):
    count, width = rows.shape
    capacity = count // experts
    stride = capacity + extra_rows
    hidden_width = expert_in.shape[1]
    step_width = 512
    chunk_rows = count
    steps = hidden_width // step_width
    half_root = math.sqrt(0.5)
    density = 1.0 / math.sqrt(2.0 * math.pi)

    def kernel(x_ref, g_ref, up_ref, in_ref, out_ref, active_ref, gh_ref, made_ref, back_ref, made_sum, back_sum):
        step = pl.program_id(0)

        @pl.when(step == 0)
        def start():
            made_sum[...] = jnp.zeros((count, width), f32)
            back_sum[...] = jnp.zeros((count, width), f32)

        @pl.loop(0, count // chunk_rows)
        def chunk(index):
            at = pl.ds(pl.multiple_of(index * chunk_rows, chunk_rows), chunk_rows)
            hidden = mm(x_ref[at, :], in_ref[...])
            share = 0.5 + 0.5 * lax.erf(hidden * half_root)
            active = (hidden * share).astype(bf16)
            slope = share + hidden * (jnp.exp(hidden * hidden * -0.5) * density)
            grad_hidden = (up_ref[at, :] * slope).astype(bf16)
            active_ref[at, :] = active
            gh_ref[at, :] = grad_hidden
            made_sum[at, :] += mm(active, out_ref[...])
            back_sum[at, :] += mm_t(grad_hidden, in_ref[...])

        @pl.when(step == steps - 1)
        def finish():
            made = made_sum[...].astype(bf16)
            made_ref[...] = made
            products = made.astype(f32) * g_ref[...].astype(f32)
            folded = products[:, :tile]
            for at in range(tile, width, tile):
                folded = folded + products[:, at : at + tile]
            dots = jnp.broadcast_to(jnp.sum(folded.T, axis=0, keepdims=True), (8, count))
            coarse = dots.astype(bf16).astype(f32)
            fine = dots - coarse
            for expert in range(experts):
                at = expert * capacity
                shift = (count - at) % count
                lanes = [pltpu.roll(half, shift, 1)[:, :tile] for half in (coarse, fine)]
                lanes = jnp.concatenate(lanes, axis=0)
                lanes = jnp.concatenate([lanes, jnp.zeros((extra_rows, width - tile), f32)], axis=1)
                back_ref[expert, :capacity, :] = back_sum[at : at + capacity, :].astype(bf16)
                back_ref[expert, capacity:, :] = lanes.astype(bf16)

    full = whole_spec((count, width))
    return pl.pallas_call(
        kernel,
        grid=(steps,),
        in_specs=[
            full,
            full,
            pl.BlockSpec((count, step_width), lambda s: (0, s)),
            pl.BlockSpec((width, step_width), lambda s: (0, s)),
            pl.BlockSpec((step_width, width), lambda s: (s, 0)),
        ],
        out_specs=(
            pl.BlockSpec((count, step_width), lambda s: (0, s)),
            pl.BlockSpec((count, step_width), lambda s: (0, s)),
            full,
            whole_spec((experts, stride, width)),
        ),
        out_shape=(
            shape_of((count, hidden_width), bf16),
            shape_of((count, hidden_width), bf16),
            shape_of((count, width), bf16),
            shape_of((experts, stride, width), bf16),
        ),
        scratch_shapes=[pltpu.VMEM((count, width), f32), pltpu.VMEM((count, width), f32)],
        compiler_params=params(),
        cost_estimate=cost(8 * count * width * hidden_width, 8 * width * hidden_width),
        name="experts",
    )(rows, grads, upstream, expert_in, expert_out)


def offset_place(offsets, step, me_ref):
    offset = offsets[0]
    for at in range(1, len(offsets)):
        offset = jnp.where(step == at, offsets[at], offset)
    return lax.bitwise_xor(me_ref[0], offset)


def gate_column(me_ref, rows_ref, router_ref, others_ref):
    logits = mm_t(router_ref[...].astype(bf16), rows_ref[...])
    numbers = lax.broadcasted_iota(jnp.int32, logits.shape, 0).astype(f32)
    mine = jnp.sum(jnp.where(numbers == me_ref[1].astype(f32), logits, 0.0), axis=0, keepdims=True)
    other = jnp.sum(
        jnp.where(numbers == others_ref[...].astype(f32), logits, 0.0), axis=0, keepdims=True
    )
    return to_column(1.0 / (1.0 + jnp.exp(other - mine)))[:, 0:1]


def expert_grads_call(me, rows_t, rows_in, grads, active, grad_hidden, router, others, offsets):
    width, rows = rows_t.shape
    hidden_width = grad_hidden.shape[1]
    count = len(offsets)
    half = count // 2
    in_rows, out_rows = width // count, hidden_width // count

    def kernel(
        me_ref, xt_ref, rows_ref, g_ref, active_ref, gh_ref, router_ref, others_ref,
        in_give_ref, in_keep_ref, out_give_ref, out_keep_ref, gh_scr, g_scr,
    ):
        step = pl.program_id(0)

        @pl.when(step == 0)
        def start():
            column = gate_column(me_ref, rows_ref, router_ref, others_ref)
            g_scr[...] = (g_ref[...].astype(f32) * column).astype(bf16)
            for at in range(0, hidden_width, width):
                gh_scr[:, at : at + width] = (gh_ref[:, at : at + width].astype(f32) * column).astype(bf16)

        def shard(in_ref, out_ref):
            for at in range(0, hidden_width, width):
                in_ref[0, :, at : at + width] = mm(xt_ref[...], gh_scr[:, at : at + width]).astype(bf16)
            out_ref[0] = t_mm(active_ref[...], g_scr[...]).astype(bf16)

        @pl.when(step < half)
        def first():
            shard(in_give_ref, out_give_ref)

        @pl.when(step >= half)
        def second():
            shard(in_keep_ref, out_keep_ref)

    def give_at(s, me_ref):
        return (jnp.minimum(s, half - 1), 0, 0)

    def keep_at(s, me_ref):
        return (jnp.maximum(s - half, 0), 0, 0)

    return pl.pallas_call(
        kernel,
        grid_spec=pltpu.PrefetchScalarGridSpec(
            num_scalar_prefetch=1,
            grid=(count,),
            in_specs=[
                pl.BlockSpec((in_rows, rows), lambda s, me_ref: (offset_place(offsets, s, me_ref), 0)),
                whole_spec((rows, width)),
                whole_spec((rows, width)),
                pl.BlockSpec((rows, out_rows), lambda s, me_ref: (0, offset_place(offsets, s, me_ref))),
                whole_spec((rows, hidden_width)),
                whole_spec(router.shape),
                whole_spec((1, rows)),
            ],
            out_specs=(
                pl.BlockSpec((1, in_rows, hidden_width), give_at),
                pl.BlockSpec((1, in_rows, hidden_width), keep_at),
                pl.BlockSpec((1, out_rows, width), give_at),
                pl.BlockSpec((1, out_rows, width), keep_at),
            ),
            scratch_shapes=[pltpu.VMEM((rows, hidden_width), bf16), pltpu.VMEM((rows, width), bf16)],
        ),
        out_shape=(
            shape_of((half, in_rows, hidden_width), bf16),
            shape_of((half, in_rows, hidden_width), bf16),
            shape_of((half, out_rows, width), bf16),
            shape_of((half, out_rows, width), bf16),
        ),
        compiler_params=params(),
        cost_estimate=cost(4 * rows * width * hidden_width, 8 * width * hidden_width),
        name="expert_grads",
    )(me, rows_t, rows_in, grads, active, grad_hidden, router, others)


def combine_call(experts, heads, rows, places, gates, routes, cotangent, residual, ffn_low, smalls, w_output):
    tokens, width = cotangent.shape
    stride = rows.shape[1]
    capacity = stride - extra_rows

    def kernel(
        rows_ref, place_ref, gate_ref, routes_ref, cot_ref, res_ref, ffn_ref, small_ref, wo_ref,
        grad_res_ref, branch_ref, ctx_ref, router_ref, gain_ref,
    ):
        gate0, gate1 = gate_ref[:, 0:1], gate_ref[:, 1:2]
        lane_row = lax.broadcasted_iota(jnp.int32, (tokens, stride * experts), 1).astype(f32)
        rows = rows_ref[...].reshape(stride * experts, width)
        lane_slot = lax.broadcasted_iota(jnp.int32, (tokens, tile), 1).astype(f32)
        grad_ffn = jnp.zeros((tokens, width), f32)
        grad_gate = []
        for k, gate in enumerate((gate0, gate1)):
            first_row = routes_ref[:, k : k + 1].astype(f32) * stride
            place = place_ref[:, k : k + 1]
            back = (lane_row == first_row + place).astype(f32).astype(bf16)
            grad_ffn = grad_ffn + mm(back, rows) * gate
            coarse = (lane_row == first_row + capacity).astype(f32)
            fine = (lane_row == first_row + (capacity + 8)).astype(f32)
            dots = mm((coarse + fine).astype(bf16), rows[:, :tile])
            grad_gate.append(jnp.sum(jnp.where(lane_slot == place, dots, 0.0), axis=1, keepdims=True))
        grad_gate0, grad_gate1 = grad_gate
        mean_grad = gate0 * grad_gate0 + gate1 * grad_gate1
        chosen0 = gate0 * (grad_gate0 - mean_grad)
        chosen1 = gate1 * (grad_gate1 - mean_grad)
        numbers = lax.broadcasted_iota(jnp.int32, (tokens, experts), 1)
        hot0 = routes_ref[:, 0:1] == numbers
        hot1 = routes_ref[:, 1:2] == numbers
        grad_logits = jnp.where(hot0, chosen0, 0.0) + jnp.where(hot1, chosen1, 0.0)
        grad_logits = grad_logits.astype(bf16)
        router_ref[...] = t_mm(grad_logits, ffn_ref[...])
        grad_ffn = grad_ffn + mm(grad_logits, small_ref[0:experts, :].astype(bf16))
        gain = small_ref[experts + heads + 1 : experts + heads + 2, :]
        residual = res_ref[...]
        inverse = lax.rsqrt(jnp.mean(residual * residual, axis=-1, keepdims=True) + eps)
        scaled = grad_ffn * gain
        inner = jnp.mean(scaled * residual, axis=-1, keepdims=True)
        gain_ref[...] = jnp.sum(grad_ffn * residual * inverse, axis=0, keepdims=True)
        grad_res = cot_ref[...].astype(f32) + inverse * scaled - residual * (inverse * inverse * inverse * inner)
        grad_res_ref[...] = grad_res
        branch = grad_res.astype(bf16)
        branch_ref[...] = branch
        ctx_ref[...] = mm_t(branch, wo_ref[...]).astype(bf16)

    return pl.pallas_call(
        kernel,
        out_shape=(
            shape_of((tokens, width), f32),
            shape_of((tokens, width), bf16),
            shape_of((tokens, width), bf16),
            shape_of((experts, width), f32),
            shape_of((1, width), f32),
        ),
        compiler_params=params(),
        cost_estimate=cost(6 * tokens * width * width, 8 * width * width),
        name="combine",
    )(rows, places, gates, routes, cotangent, residual, ffn_low, smalls, w_output)


def split_rows(full_ref, me_index, count, shards, main, give_ref, keep_ref):
    for offset in range(count):
        place = lax.bitwise_xor(me_index, offset)
        target = give_ref if offset & 1 else keep_ref
        target[offset // 2, :, :main] = full_ref[
            pl.ds(pl.multiple_of(place * shards, shards), shards), :
        ].astype(bf16)


def small_tiles(pieces, rows, shards):
    per_tile = shards // rows
    return -(-pieces // per_tile), per_tile


def first_grads_call(me, dq, dk, dv, normed_t, context_low, branch, grad_router, grad_gain, table, count):
    tokens, part = dq.shape
    width, seq = normed_t.shape
    shards = width // count
    experts = grad_router.shape[0]
    heads, _, buckets = table.shape
    piece_rows = -(-(experts + 1) // 16) * 16
    pieces = width // tile + 1
    tiles, per_tile = small_tiles(pieces, piece_rows, shards)
    main = width + 3 * part

    def kernel(
        me_ref, dq_ref, dk_ref, dv_ref, normed_ref, ctx_ref, branch_ref, router_ref, gain_ref, table_ref,
        give_ref, keep_ref, full_ref,
    ):
        own = pl.ds(pl.multiple_of(me_ref[0] * tokens, tokens), tokens)
        full_ref[:, :width] = t_mm(ctx_ref[...], branch_ref[...])
        full_ref[:, width : width + part] = mm(normed_ref[:, own], dq_ref[...])
        full_ref[:, width + part : width + 2 * part] = mm(normed_ref[...], dk_ref[...])
        full_ref[:, width + 2 * part :] = mm(normed_ref[...], dv_ref[...])
        split_rows(full_ref, me_ref[0], count, shards, main, give_ref, keep_ref)
        small = jnp.concatenate(
            [router_ref[...], gain_ref[...], jnp.zeros((piece_rows - experts - 1, width), f32)], axis=0
        )
        rows = [table_ref[head] for head in range(heads)]
        rows = jnp.concatenate(rows + [jnp.zeros((piece_rows - heads, buckets), f32)], axis=0)
        rows = jnp.concatenate([rows, jnp.zeros((piece_rows, tile - buckets), f32)], axis=1)
        blocks = [small[:, at : at + tile] for at in range(0, width, tile)] + [rows]
        blocks = [block.astype(bf16) for block in blocks]
        for target in (give_ref, keep_ref):
            for at in range(count // 2):
                target[at, :, main:] = jnp.zeros((shards, tiles * tile), bf16)
                for index, block in enumerate(blocks):
                    row = index % per_tile * piece_rows
                    col = main + index // per_tile * tile
                    target[at, row : row + piece_rows, col : col + tile] = block

    vmem = pl.BlockSpec(memory_space=pltpu.VMEM)
    return pl.pallas_call(
        kernel,
        in_specs=[pl.BlockSpec(memory_space=pltpu.SMEM)] + [vmem] * 9,
        out_shape=(shape_of((count // 2, shards, main + tiles * tile), bf16),) * 2,
        scratch_shapes=[pltpu.VMEM((width, main), f32)],
        compiler_params=params(),
        cost_estimate=cost(5 * seq * width * part, 10 * seq * width),
        name="first_grads",
    )(me, dq, dk, dv, normed_t, context_low, branch, grad_router, grad_gain, table)


def first_smalls(columns, experts, heads, buckets, width, shards):
    piece_rows = -(-(experts + 1) // 16) * 16
    pieces = width // tile + 1
    _, per_tile = small_tiles(pieces, piece_rows, shards)
    found = []
    for index in range(pieces):
        row, col = index % per_tile * piece_rows, index // per_tile * tile
        found.append(columns[row : row + piece_rows, col : col + tile])
    wide = jnp.concatenate(found[:-1], axis=1)
    return wide[:experts], wide[experts], found[-1][:heads, :buckets]


def second_grads_call(me, dq, dk, dv, normed_t, table, count):
    tokens, part = dq.shape
    width, seq = normed_t.shape
    shards = width // count
    heads, _, buckets = table.shape
    main = 3 * part

    def kernel(me_ref, dq_ref, dk_ref, dv_ref, normed_ref, table_ref, give_ref, keep_ref, full_ref):
        own = pl.ds(pl.multiple_of(me_ref[0] * tokens, tokens), tokens)
        full_ref[:, :part] = mm(normed_ref[:, own], dq_ref[...])
        full_ref[:, part : 2 * part] = mm(normed_ref[...], dk_ref[...])
        full_ref[:, 2 * part :] = mm(normed_ref[...], dv_ref[...])
        split_rows(full_ref, me_ref[0], count, shards, main, give_ref, keep_ref)
        rows = [table_ref[head] for head in range(heads)]
        rows = jnp.concatenate(rows + [jnp.zeros((16 - heads, buckets), f32)], axis=0)
        rows = jnp.concatenate([rows, jnp.zeros((16, tile - buckets), f32)], axis=1).astype(bf16)
        for target in (give_ref, keep_ref):
            for at in range(count // 2):
                target[at, :, main:] = jnp.zeros((shards, tile), bf16)
                target[at, :16, main:] = rows

    vmem = pl.BlockSpec(memory_space=pltpu.VMEM)
    return pl.pallas_call(
        kernel,
        in_specs=[pl.BlockSpec(memory_space=pltpu.SMEM)] + [vmem] * 5,
        out_shape=(shape_of((count // 2, shards, main + tile), bf16),) * 2,
        scratch_shapes=[pltpu.VMEM((width, main), f32)],
        compiler_params=params(),
        cost_estimate=cost(5 * seq * width * part, 10 * seq * width),
        name="second_grads",
    )(me, dq, dk, dv, normed_t, table)


def rows_back_call(me, first, second, weights, count):
    tokens, part = first[0].shape
    width = weights[0].shape[0]

    def kernel(
        me_ref, dq1_ref, dk1_ref, dv1_ref, dq2_ref, dk2_ref, dv2_ref, wq_ref, wk_ref, wv_ref, give_ref, keep_ref,
    ):
        for offset in range(count):
            place = lax.bitwise_xor(me_ref[0], offset)
            at = pl.ds(pl.multiple_of(place * tokens, tokens), tokens)
            total = mm_t(dk1_ref[at, :], wk_ref[:, :part]) + mm_t(dk2_ref[at, :], wk_ref[:, part:])
            total = total + mm_t(dv1_ref[at, :], wv_ref[:, :part]) + mm_t(dv2_ref[at, :], wv_ref[:, part:])
            if offset == 0:
                total = total + mm_t(dq1_ref[...], wq_ref[:, :part]) + mm_t(dq2_ref[...], wq_ref[:, part:])
            target = give_ref if offset & 1 else keep_ref
            target[offset // 2] = total.astype(bf16)

    vmem = pl.BlockSpec(memory_space=pltpu.VMEM)
    return pl.pallas_call(
        kernel,
        in_specs=[pl.BlockSpec(memory_space=pltpu.SMEM)] + [vmem] * 9,
        out_shape=(shape_of((count // 2, tokens, width), bf16),) * 2,
        compiler_params=params(),
        cost_estimate=cost(10 * count * tokens * width * width, 10 * count * tokens * width),
        name="rows_back",
    )(me, *first, *second, *weights)


def finish_call(chain1, chain2, weights, gain, half_cols):
    shards, width = weights[0].shape
    rest = width - half_cols

    def kernel(c1_ref, c2_ref, wq_ref, wk_ref, wv_ref, gain_ref, gq_ref, gk_ref, gv_ref, go_ref, out_ref):
        total = jnp.zeros((shards, 1), f32)
        go_ref[...] = c1_ref[:, :width].astype(f32)
        for part, (weight_ref, grad_ref) in enumerate(((wq_ref, gq_ref), (wk_ref, gk_ref), (wv_ref, gv_ref))):
            left = c1_ref[:, width + part * half_cols : width + (part + 1) * half_cols].astype(f32)
            right = c2_ref[:, part * rest : (part + 1) * rest].astype(f32)
            grad_ref[:, :half_cols] = left
            grad_ref[:, half_cols:] = right
            weight = weight_ref[...].astype(f32)
            total = total + jnp.sum(left * weight[:, :half_cols], axis=1, keepdims=True)
            total = total + jnp.sum(right * weight[:, half_cols:], axis=1, keepdims=True)
        out_ref[...] = jnp.broadcast_to(total, (shards, tile)).T[0:1, :] / gain_ref[...].astype(f32)

    return pl.pallas_call(
        kernel,
        out_shape=(shape_of((shards, width), f32),) * 4 + (shape_of((1, shards), f32),),
        compiler_params=params(),
        cost_estimate=cost(6 * shards * width, 30 * shards * width),
        name="finish",
    )(chain1, chain2, *weights, gain[None, :])


def gather_blocks(value, axis_size, late=None):
    blocks = {0: value}
    bit = 2
    while bit < axis_size:
        for offset in sorted(blocks):
            blocks[offset | bit] = swap(blocks[offset], "fsdp", axis_size, bit)
            if late is not None:
                blocks[offset | bit] = ordered(blocks[offset | bit], late)[0]
        bit *= 2
    for offset in sorted(blocks):
        blocks[offset | 1] = swap(blocks[offset], "fsdp", axis_size, 1)
    return [blocks[offset] for offset in range(axis_size)]


def scatter_bits(axis_size):
    bits, bit = [1], axis_size // 2
    while bit > 1:
        bits.append(bit)
        bit //= 2
    return [bit for bit in bits if bit < axis_size]


def added(left_side, right_side):
    return left_side.astype(f32) + right_side.astype(f32)


def core_sum(given, kept, axis_size):
    arrived = swap(given, "fsdp", axis_size, 1)
    return {2 * at: added(kept[at], arrived[at]).astype(bf16) for at in range(axis_size // 2)}


def far_sum(pieces, axis_size, early=None, late=None, cuts=1):
    for bit in scatter_bits(axis_size):
        if bit == 1:
            continue
        left = {}
        for offset in sorted(pieces):
            if offset & bit:
                continue
            found = []
            for leaving in jnp.split(pieces[offset | bit].astype(bf16), cuts, axis=0):
                if early is not None:
                    leaving = ordered(leaving, early)[0]
                found.append(swap(leaving, "fsdp", axis_size, bit))
                early = found[-1]
            if late is not None:
                found[-1] = ordered(found[-1], late)[0]
            left[offset] = added(pieces[offset], jnp.concatenate(found, axis=0))
        pieces = left
    return pieces[0]


def far_steps(pieces, axis_size, fractions, early=None):
    bits = [bit for bit in scatter_bits(axis_size) if bit > 1]
    for bit in bits[:-1]:
        pieces = {
            offset: added(
                pieces[offset], swap(pieces[offset | bit].astype(bf16), "fsdp", axis_size, bit)
            )
            for offset in sorted(pieces)
            if not offset & bit
        }
    bit = bits[-1]
    rows = pieces[0].shape[0]
    leaving = pieces[bit].astype(bf16)
    found, begin = [], 0
    for step, fraction in enumerate(fractions):
        end = rows if step == len(fractions) - 1 else begin + rows * fraction // 12
        part = leaving[begin:end]
        if early is not None:
            part = ordered(part, early)[0]
        early = yield swap(part, "fsdp", axis_size, bit)
        found.append(early)
        begin = end
    yield added(pieces[0], jnp.concatenate(found, axis=0))


def all_sum_expert(value, axis_size, index, before_last=None):
    rows = value.shape[0]
    parts = jnp.pad(value.astype(bf16), ((0, -rows % (axis_size // 2)), (0, 0)))
    bit, bits = 1, []
    while bit < axis_size:
        bits.append(bit)
        bit *= 2
    inner = bits.pop()
    first_arrived = None
    for bit in bits:
        low_half, high_half = jnp.split(parts, 2, axis=0)
        upper = (index & bit) != 0
        keep = jnp.where(upper, high_half, low_half)
        give = jnp.where(upper, low_half, high_half)
        arrived = swap(give, "expert", axis_size, bit)
        first_arrived = arrived if first_arrived is None else first_arrived
        parts = added(keep, arrived).astype(bf16)
    parts = added(parts, swap(parts, "expert", axis_size, inner)).astype(bf16)
    for bit in reversed(bits):
        if bit == 1 and before_last is not None:
            parts = ordered(parts, before_last)[0]
        other = swap(parts, "expert", axis_size, bit)
        upper = (index & bit) != 0
        parts = jnp.concatenate(
            [jnp.where(upper, other, parts), jnp.where(upper, parts, other)], axis=0
        )
    return parts[:rows], first_arrived


def ordered(*values):
    return lax.optimization_barrier(values)


def build(count, expert_ranks):
    def per_device(
        tokens_in,
        seg_ids,
        routes,
        buckets,
        attn_gain,
        w_query,
        w_key,
        w_value,
        w_output,
        bias_table,
        ffn_gain,
        w_router,
        w_in,
        w_out,
        cotangent,
    ):
        tokens, width = tokens_in.shape
        shards, experts = w_router.shape
        bucket_rows, heads = bias_table.shape
        bucket_count = bucket_rows * count
        head_dim = width // heads
        seq = buckets.shape[0]
        top_count = routes.shape[1]
        capacity = 3 * top_count * tokens // (2 * experts)
        slots = experts * capacity
        fsdp_index = lax.axis_index("fsdp")
        expert_index = lax.axis_index("expert")
        me = jnp.stack([fsdp_index, expert_index]).astype(jnp.int32)

        used = experts + heads + 3
        small_rows = -(-used // 16) * 16
        packed = pack_call(
            me, (w_query, w_key, w_value), tokens_in, seg_ids[None, :],
            jnp.stack([attn_gain, ffn_gain]), bias_table, w_router.T, small_rows, width,
        )
        blocks = gather_blocks(packed, count)
        leaving_output = ordered(w_output, blocks[-2])[0]
        routes, blocks[1] = ordered(routes, blocks[1])
        padded_buckets = jnp.concatenate([jnp.full((seq,), -1, jnp.int32), buckets])
        bucket_window = lax.dynamic_slice_in_dim(
            padded_buckets, fsdp_index * tokens, seq + tokens, 0
        )[None, :]

        slot_map, back0, back1, grad_rows_out, places = route_call(routes, cotangent, capacity, experts)
        grad_rows_in = lax.all_to_all(
            grad_rows_out, "expert", split_axis=0, concat_axis=0, tiled=True
        )
        others = grad_rows_in[:, capacity, :capacity].reshape(1, slots)
        grad_rows_in = grad_rows_in[:, :capacity, :].reshape(slots, width)

        (queries, keys, values, normed, sequence, wq, wk, wv, smalls, bias, mask) = project_call(
            me, blocks, shards, small_rows, bucket_window, heads, bucket_count, experts
        )
        out_blocks = gather_blocks(leaving_output, count, queries)
        queries, grad_rows_in, others = ordered(queries, grad_rows_in, others)
        context, lse = attend_call(queries, keys, values, bias, mask, head_dim)
        wo, context_low, residual, ffn_low, gates, rows_out = dispatch_call(
            me, context, out_blocks, tokens_in, smalls, routes, slot_map, heads
        )(experts)
        normed_t = ordered(normed, rows_out)[0].T
        upstream = upstream_call(ordered(grad_rows_in, rows_out)[0], w_out[0])
        rows_in = lax.all_to_all(
            rows_out.reshape(experts, capacity, width),
            "expert",
            split_axis=0,
            concat_axis=0,
            tiled=True,
        ).reshape(slots, width)
        rows_in, normed_t, upstream = ordered(rows_in, normed_t, upstream)
        active, grad_hidden, made, row_grads = expert_call(
            rows_in, grad_rows_in, upstream, w_in[0], w_out[0], experts
        )
        row_grads_back = lax.all_to_all(
            row_grads, "expert", split_axis=0, concat_axis=0, tiled=True
        )

        rows_t = rows_in.T
        give = [offset for offset in range(count) if offset & 1]
        keep = [offset for offset in range(count) if not offset & 1]
        router = smalls[:experts]
        in_give, in_keep, out_give, out_keep = expert_grads_call(
            me, rows_t, rows_in, grad_rows_in, active, grad_hidden, router, others, give + keep
        )
        in_give, out_give, row_grads_back = ordered(in_give, out_give, row_grads_back)
        in_pieces = core_sum(in_give, in_keep, count)
        out_pieces = core_sum(out_give, out_keep, count)

        grad_residual, branch, grad_context, grad_router, grad_gain_ffn = combine_call(
            experts, heads, row_grads_back, places, gates, routes, cotangent,
            residual, ffn_low, smalls, wo,
        )
        pairs = width // tile
        near = pairs // 2
        last = max(in_pieces)
        grad_context, in_pieces[last] = ordered(grad_context, in_pieces[last])
        *part1, table1 = attend_back_call(
            queries, keys, values, bias, mask, lse, context, grad_context, bucket_window,
            bucket_count, head_dim, 0, near,
        )
        in_steps = far_steps(in_pieces, count, (5, 3, 4))
        arrived = next(in_steps)
        part1[0], arrived = ordered(part1[0], arrived)
        give1, keep1 = first_grads_call(
            me, *part1, normed_t, context_low, branch, grad_router, grad_gain_ffn, table1, count
        )
        arrived = in_steps.send(arrived)
        made = ordered(made, give1)[0]
        made_back = lax.all_to_all(
            made.reshape(experts, capacity, width),
            "expert",
            split_axis=0,
            concat_axis=0,
            tiled=True,
        ).reshape(slots, width)
        pieces1 = core_sum(give1, keep1, count)
        last = max(pieces1)
        grad_context, pieces1[last], arrived = ordered(grad_context, pieces1[last], arrived)
        *part2, table2 = attend_back_call(
            queries, keys, values, bias, mask, lse, context, grad_context, bucket_window,
            bucket_count, head_dim, near, pairs - near,
        )
        give2, keep2 = second_grads_call(me, *part2, normed_t, table2, count)
        sum1 = far_sum(pieces1, count, None, give2)
        pieces2 = core_sum(give2, keep2, count)
        last = max(pieces2)
        dv2, pieces2[last] = ordered(part2[2], pieces2[last])
        rows_give, rows_keep = rows_back_call(
            me, part1, (part2[0], part2[1], dv2), (wq, wk, wv), count
        )
        steps2 = far_steps(pieces2, count, (9, 3))
        sum2 = steps2.send(steps2.send(ordered(next(steps2), rows_give)[0]))
        arrived = in_steps.send(ordered(arrived, sum1)[0])
        in_sum = in_steps.send(arrived)
        grad_normed = far_sum(core_sum(rows_give, rows_keep, count), count, sum2)
        arrived, _ = ordered(arrived, sum2)
        out_steps = far_steps(out_pieces, count, (6, 6), arrived)
        out_sum = out_steps.send(out_steps.send(ordered(next(out_steps), grad_normed)[0]))
        grad_shards = [in_sum, out_sum]
        chain1, _ = all_sum_expert(sum1, expert_ranks, expert_index)
        chain2, first_arrived = all_sum_expert(sum2, expert_ranks, expert_index)
        half_cols = near * tile

        inputs = tokens_in.astype(f32)
        inverse = lax.rsqrt(jnp.mean(inputs * inputs, axis=-1, keepdims=True) + eps)
        gain_attn = smalls[experts + heads]
        scaled = grad_normed * gain_attn
        inner = jnp.mean(scaled * inputs, axis=-1, keepdims=True)
        grad_tokens = grad_residual + inverse * scaled - inputs * inverse**3 * inner

        made_back = ordered(made_back, sum2)[0]
        picked0 = mm(back0, made_back)
        picked1 = mm(back1, made_back)
        block_out = (residual + gates[:, 0:1] * picked0 + gates[:, 1:2] * picked1).astype(bf16)

        rest = width - half_cols
        *shards_out, grad_gain_attn = finish_call(
            chain1, chain2, (w_query, w_key, w_value), attn_gain, half_cols
        )
        router_sum, gain_sum, table_left = first_smalls(
            chain1[:, width + 3 * half_cols :].astype(f32), experts, 2 * near, bucket_count, width, shards
        )
        table_right = chain2[: heads - 2 * near, 3 * rest : 3 * rest + bucket_count].astype(f32)
        table_cols = lax.dynamic_slice_in_dim(
            jnp.concatenate([table_left, table_right], axis=0), fsdp_index * bucket_rows, bucket_rows, 1
        )
        return (
            block_out,
            grad_tokens,
            grad_gain_attn[0],
            shards_out[0],
            shards_out[1],
            shards_out[2],
            shards_out[3],
            table_cols.T,
            lax.dynamic_slice_in_dim(gain_sum, fsdp_index * shards, shards, 0),
            lax.dynamic_slice_in_dim(router_sum, fsdp_index * shards, shards, 1).T,
            grad_shards[0][None],
            grad_shards[1][None],
        )

    return per_device


def solution(mesh):
    return jax.shard_map(
        build(mesh.shape["fsdp"], mesh.shape["expert"]),
        mesh=mesh,
        in_specs=(
            P(("expert", "fsdp"), None),
            P(("expert", "fsdp")),
            P(("expert", "fsdp"), None),
            P(),
            P("fsdp"),
            P("fsdp", None),
            P("fsdp", None),
            P("fsdp", None),
            P("fsdp", None),
            P("fsdp", None),
            P("fsdp"),
            P("fsdp", None),
            P("expert", None, None),
            P("expert", None, None),
            P(("expert", "fsdp"), None),
        ),
        out_specs=(
            P(("expert", "fsdp"), None),
            P(("expert", "fsdp"), None),
            P("fsdp"),
            P("fsdp", None),
            P("fsdp", None),
            P("fsdp", None),
            P("fsdp", None),
            P("fsdp", None),
            P("fsdp"),
            P("fsdp", None),
            P("expert", "fsdp", None),
            P("expert", "fsdp", None),
        ),
        check_vma=False,
    )
```

```python
import math

import jax
import jax.numpy as jnp
from jax import lax
from jax.experimental import pallas as pl
from jax.experimental.pallas import tpu as pltpu
from jax.sharding import PartitionSpec as P

eps = 1e-06
log2e = math.log2(math.e)
masked_score = -1e30
f32 = jnp.float32
bf16 = jnp.bfloat16
tile = 128
extra_rows = 16


def mm(left_side, right_side):
    return lax.dot_general(
        left_side, right_side, (((1,), (0,)), ((), ())), preferred_element_type=f32
    )


def mm_t(left_side, right_side):
    return lax.dot_general(
        left_side, right_side, (((1,), (1,)), ((), ())), preferred_element_type=f32
    )


def t_mm(left_side, right_side):
    return lax.dot_general(
        left_side, right_side, (((0,), (0,)), ((), ())), preferred_element_type=f32
    )


def swap(value, axis_name, axis_size, bit):
    return lax.ppermute(value, axis_name, [(i, i ^ bit) for i in range(axis_size)])


def params(megabytes=56):
    return pltpu.CompilerParams(vmem_limit_bytes=megabytes << 20)


def cost(flops, moved):
    return pl.CostEstimate(flops=int(flops) >> 8, bytes_accessed=int(moved) >> 8, transcendentals=0)


def shape_of(dims, dtype):
    return jax.ShapeDtypeStruct(dims, dtype)


def whole_spec(dims):
    return pl.BlockSpec(dims, lambda *unused: (0,) * len(dims))


def to_column(row):
    return jnp.broadcast_to(row, (tile, row.shape[1])).T


def route_kernel(capacity, routes_ref, cot_ref, map_ref, back0_ref, back1_ref, out_ref, slot_ref):
    tokens = routes_ref.shape[0]
    slots = map_ref.shape[0]
    experts = slots // capacity
    routes = routes_ref[...]
    first, second = routes[:, 0:1], routes[:, 1:2]
    numbers = lax.broadcasted_iota(jnp.int32, (tokens, experts), 1)
    hot0 = (first == numbers).astype(f32)
    hot1 = (second == numbers).astype(f32)
    rows = lax.broadcasted_iota(jnp.int32, (tokens, tokens), 0)
    cols = lax.broadcasted_iota(jnp.int32, (tokens, tokens), 1)
    before = (cols < rows).astype(f32).astype(bf16)
    earlier = mm(before, (hot0 + hot1).astype(bf16))
    slot0 = jnp.sum(hot0 * earlier, axis=1, keepdims=True)
    slot1 = jnp.sum(hot1 * (earlier + hot0), axis=1, keepdims=True)
    slot_ref[...] = jnp.concatenate([slot0, slot1], axis=1)
    dest0 = first.astype(f32) * capacity + slot0
    dest1 = second.astype(f32) * capacity + slot1
    lane_slot = lax.broadcasted_iota(jnp.int32, (tokens, slots), 1).astype(f32)
    back0_ref[...] = (lane_slot == dest0).astype(f32).astype(bf16)
    back1_ref[...] = (lane_slot == dest1).astype(f32).astype(bf16)
    row0 = jnp.broadcast_to(dest0, (tokens, tile)).T[0:1, :]
    row1 = jnp.broadcast_to(dest1, (tokens, tile)).T[0:1, :]
    row_slot = lax.broadcasted_iota(jnp.int32, (slots, tokens), 0).astype(f32)
    hot = ((row_slot == row0).astype(f32) + (row_slot == row1).astype(f32)).astype(bf16)
    map_ref[...] = hot
    rows = mm(hot, cot_ref[...]).astype(bf16)
    others = back0_ref[...].astype(f32) * second.astype(f32) + back1_ref[...].astype(f32) * first.astype(f32)
    others = jnp.broadcast_to(jnp.sum(others, axis=0, keepdims=True), (extra_rows, slots))
    width = rows.shape[1]
    for expert in range(experts):
        at = expert * capacity
        lanes = pltpu.roll(others, (slots - at) % slots, 1)[:, :tile]
        lanes = jnp.concatenate([lanes, jnp.zeros((extra_rows, width - tile), f32)], axis=1)
        out_ref[expert, :capacity, :] = rows[at : at + capacity, :]
        out_ref[expert, capacity:, :] = lanes.astype(bf16)


def route_call(routes, cotangent, capacity, experts):
    tokens, width = cotangent.shape
    slots = experts * capacity
    return pl.pallas_call(
        lambda *refs: route_kernel(capacity, *refs),
        out_shape=(
            shape_of((slots, tokens), bf16),
            shape_of((tokens, slots), bf16),
            shape_of((tokens, slots), bf16),
            shape_of((experts, capacity + extra_rows, width), bf16),
            shape_of((tokens, 2), f32),
        ),
        compiler_params=params(),
        cost_estimate=cost(2 * slots * tokens * width, 4 * slots * width),
        name="route",
    )(routes, cotangent)


def pack_call(me, weights, tokens_in, seg_row, gains, table, router, small, width):
    shards = weights[0].shape[0]
    tokens = tokens_in.shape[0]
    experts, heads = router.shape[0], table.shape[1]
    used = experts + heads + 3

    def placed(me_ref, rows):
        at = lax.broadcasted_iota(jnp.int32, (rows, width), 1)
        own = lax.broadcasted_iota(jnp.int32, (rows, width), 0) + me_ref[0] * rows
        return (at == own).astype(f32).astype(bf16)

    def kernel(me_ref, wq_ref, wk_ref, wv_ref, x_ref, seg_ref, gain_ref, table_ref, router_ref, out_ref):
        for at, ref in enumerate((wq_ref, wk_ref, wv_ref)):
            out_ref[at * shards : (at + 1) * shards, :] = ref[...]
        out_ref[3 * shards : 3 * shards + tokens, :] = x_ref[...]
        columns = placed(me_ref, shards)
        rows = [
            mm(router_ref[...], columns),
            t_mm(table_ref[...], placed(me_ref, table_ref.shape[0])),
            mm(gain_ref[...], columns),
            jnp.zeros((small - used, width), f32),
            jnp.concatenate([seg_ref[...].astype(f32), jnp.zeros((1, width - tokens), f32)], axis=1),
        ]
        out_ref[3 * shards + tokens :, :] = jnp.concatenate(rows, axis=0).astype(bf16)

    vmem = pl.BlockSpec(memory_space=pltpu.VMEM)
    return pl.pallas_call(
        kernel,
        in_specs=[pl.BlockSpec(memory_space=pltpu.SMEM)] + [vmem] * 8,
        out_shape=shape_of((3 * shards + tokens + small, width), bf16),
        compiler_params=params(),
        cost_estimate=cost(1, 4 * shards * width),
        name="pack",
    )(me, *weights, tokens_in, seg_row, gains, table, router)


def project_call(me, blocks, shards, small, bucket_window, heads, buckets, experts):
    count = len(blocks)
    rows, width = blocks[0].shape
    tokens = rows - 3 * shards - small
    seq = count * tokens
    window = bucket_window.shape[1]

    def kernel(me_ref, *refs):
        block_refs = refs[:count]
        (bucket_ref, q_ref, k_ref, v_ref, normed_ref, tok_ref, wq_ref, wk_ref, wv_ref, small_ref, bias_ref, mask_ref) = refs[count:]
        me_index = me_ref[0]
        totals = jnp.zeros((small, width), f32)
        own_docs = block_refs[0][rows - small :, :].astype(f32)[small - 1 :, :tokens]
        for offset in range(count):
            place = lax.bitwise_xor(me_index, offset)
            row = pl.multiple_of(place * shards, shards)
            for part, full_ref in enumerate((wq_ref, wk_ref, wv_ref)):
                full_ref[pl.ds(row, shards), :] = block_refs[offset][part * shards : (part + 1) * shards, :]
            token_row = pl.multiple_of(place * tokens, tokens)
            tok_ref[pl.ds(token_row, tokens), :] = block_refs[offset][3 * shards : rows - small, :]
            extra = block_refs[offset][rows - small :, :].astype(f32)
            totals = totals + extra
            docs = to_column(extra[small - 1 :, :tokens])
            docs = jnp.concatenate([docs] * (tokens // tile), axis=1)
            mask_ref[pl.ds(token_row, tokens), :] = jnp.where(docs == own_docs, 0.0, masked_score)
        small_ref[...] = totals
        gain = totals[experts + heads : experts + heads + 1, :]
        table = totals[experts : experts + heads, :buckets].astype(bf16)
        numbers = lax.broadcasted_iota(jnp.int32, (buckets, window), 0)
        hot = (numbers == bucket_ref[...]).astype(f32).astype(bf16)
        by_distance = mm(table, hot) * log2e
        by_distance = jnp.where(bucket_ref[...] < 0, masked_score, by_distance)
        for head in range(heads):
            bias_ref[head] = by_distance[head : head + 1, :]

        @pl.loop(0, count)
        def chunk(index):
            rows = pl.ds(pl.multiple_of(index * tokens, tokens), tokens)
            values = tok_ref[rows, :].astype(f32)
            inverse = lax.rsqrt(jnp.mean(values * values, axis=-1, keepdims=True) + eps)
            normed = (values * inverse * gain).astype(bf16)
            normed_ref[rows, :] = normed
            k_ref[rows, :] = mm(normed, wk_ref[...]).astype(bf16)
            v_ref[rows, :] = mm(normed, wv_ref[...]).astype(bf16)

        own = normed_ref[pl.ds(pl.multiple_of(me_index * tokens, tokens), tokens), :]
        q_ref[...] = mm(own, wq_ref[...]).astype(bf16)

    vmem = pl.BlockSpec(memory_space=pltpu.VMEM)
    return pl.pallas_call(
        kernel,
        in_specs=[pl.BlockSpec(memory_space=pltpu.SMEM)] + [vmem] * (count + 1),
        out_shape=(
            shape_of((tokens, width), bf16),
            shape_of((seq, width), bf16),
            shape_of((seq, width), bf16),
            shape_of((seq, width), bf16),
            shape_of((seq, width), bf16),
            shape_of((width, width), bf16),
            shape_of((width, width), bf16),
            shape_of((width, width), bf16),
            shape_of((small, width), f32),
            shape_of((heads, 1, window), f32),
            shape_of((seq, tokens), f32),
        ),
        compiler_params=params(),
        cost_estimate=cost(2 * width * width * (2 * seq + tokens), 20 * seq * width),
        name="project",
    )(me, *blocks, bucket_window)


def skewed(bias_row, window):
    spread = jnp.broadcast_to(bias_row, (tile, window))
    return pltpu.roll(spread, 0, 1, stride=1, stride_axis=0)


def attend_call(queries, keys, values, bias, mask, head_dim):
    tokens, width = queries.shape
    seq = keys.shape[0]
    heads, _, window = bias.shape
    pairs = width // tile
    per_step = heads // pairs
    key_blocks = seq // tile
    scale = head_dim**-0.5 * log2e

    def kernel(q_ref, k_ref, v_ref, bias_ref, mask_ref, ctx_ref, lse_ref, score_ref, prob_ref, skew_ref):
        lane = lax.broadcasted_iota(jnp.int32, (tokens, tile), 1)
        row = lax.broadcasted_iota(jnp.int32, (tile, tokens), 0)
        query = q_ref[...]
        values_t = v_ref[...].T
        result = jnp.zeros((tile, tokens), f32)
        for half in range(per_step):
            mine = jnp.where(lane // head_dim == half, query, jnp.zeros_like(query))
            skew_ref[...] = skewed(bias_ref[half], window)
            top = jnp.full((8, tokens), -3e38, f32)
            for block in range(key_blocks):
                rows = pl.ds(block * tile, tile)
                begin = tile * (key_blocks - block)
                scores = mm_t(k_ref[rows, :], mine) * scale
                scores = scores + (skew_ref[:, begin : begin + tokens] + mask_ref[rows, :])
                score_ref[rows, :] = scores
                top = jnp.maximum(top, jnp.max(scores.reshape(tile // 8, 8, tokens), axis=0))
            top = jnp.max(top, axis=0, keepdims=True)
            total = jnp.zeros((8, tokens), f32)
            for block in range(key_blocks):
                rows = pl.ds(block * tile, tile)
                probs = jnp.exp2(score_ref[rows, :] - top)
                prob_ref[rows, :] = probs.astype(bf16)
                total = total + jnp.sum(probs.reshape(tile // 8, 8, tokens), axis=0)
            total = jnp.sum(total, axis=0, keepdims=True)
            lse_ref[half] = top + jnp.log2(total)
            mixed = mm(values_t, prob_ref[...]) * (1.0 / total)
            result = jnp.where(row // head_dim == half, mixed, result)
        ctx_ref[...] = result.T

    return pl.pallas_call(
        kernel,
        grid=(pairs,),
        in_specs=[
            pl.BlockSpec((tokens, tile), lambda p: (0, p)),
            pl.BlockSpec((seq, tile), lambda p: (0, p)),
            pl.BlockSpec((seq, tile), lambda p: (0, p)),
            pl.BlockSpec((per_step, 1, window), lambda p: (p, 0, 0)),
            pl.BlockSpec((seq, tokens), lambda p: (0, 0)),
        ],
        out_specs=(
            pl.BlockSpec((tokens, tile), lambda p: (0, p)),
            pl.BlockSpec((per_step, 1, tokens), lambda p: (p, 0, 0)),
        ),
        out_shape=(shape_of((tokens, width), f32), shape_of((heads, 1, tokens), f32)),
        scratch_shapes=[
            pltpu.VMEM((seq, tokens), f32),
            pltpu.VMEM((seq, tokens), bf16),
            pltpu.VMEM((tile, window), f32),
        ],
        compiler_params=params(),
        cost_estimate=cost(16 * heads * tokens * seq * tile, 4 * seq * width),
        name="attend",
    )(queries, keys, values, bias, mask)


def unskewed(total):
    window = total.shape[1]
    rows = total.shape[0]
    while rows > 8:
        rows = rows // 2
        total = total[:rows, :] + pltpu.roll(total[rows:, :], window - rows, 1)
    step = 4
    while step:
        moved = pltpu.roll(pltpu.roll(total, 8 - step, 0), window - step, 1)
        total = total + moved
        step = step // 2
    return total[0:1, :]


def attend_back_call(queries, keys, values, bias, mask, lse, context, grad_context, bucket_window, buckets, head_dim, first, pairs):
    tokens, width = queries.shape
    seq = keys.shape[0]
    heads, _, window = bias.shape
    per_step = heads // (width // tile)
    key_blocks = seq // tile
    scale = head_dim**-0.5

    def kernel(
        q_ref, k_ref, v_ref, bias_ref, mask_ref, lse_ref, ctx_ref, grad_ref, bucket_ref,
        dq_ref, dk_ref, dv_ref, table_ref, prob_ref, ds_ref, skew_ref, sum_ref,
    ):
        lane = lax.broadcasted_iota(jnp.int32, (tokens, tile), 1)
        row = lax.broadcasted_iota(jnp.int32, (tile, tokens), 0)
        query = q_ref[...]
        grad = grad_ref[...]
        keys_t = k_ref[...].T
        products = (grad.astype(f32) * ctx_ref[...]).T
        result = jnp.zeros((tile, tokens), f32)
        numbers = lax.broadcasted_iota(jnp.int32, (buckets, window), 0)
        hot = (numbers == bucket_ref[...]).astype(f32)
        mine_q, mine_g = [], []
        for half in range(per_step):
            mine_q.append(jnp.where(lane // head_dim == half, query, jnp.zeros_like(query)))
            mine_g.append(jnp.where(lane // head_dim == half, grad, jnp.zeros_like(grad)))
        for half in range(per_step):
            delta = jnp.sum(
                products[half * head_dim : (half + 1) * head_dim, :], axis=0, keepdims=True
            )
            lse_row = lse_ref[half]
            skew_ref[...] = skewed(bias_ref[half], window)
            sum_ref[...] = jnp.zeros((tile, window), f32)
            cols = slice(half * tokens, (half + 1) * tokens)
            for block in range(key_blocks):
                rows = pl.ds(block * tile, tile)
                begin = tile * (key_blocks - block)
                scores = mm_t(k_ref[rows, :], mine_q[half]) * (scale * log2e)
                scores = scores + (skew_ref[:, begin : begin + tokens] + mask_ref[rows, :])
                probs = jnp.exp2(scores - lse_row)
                grad_probs = mm_t(v_ref[rows, :], mine_g[half])
                grad_scores = (probs * (grad_probs - delta)).astype(bf16)
                prob_ref[rows, cols] = probs.astype(bf16)
                ds_ref[rows, cols] = grad_scores
                sum_ref[:, begin : begin + tokens] += grad_scores.astype(f32)
            grad_q = mm(keys_t, ds_ref[:, cols])
            result = jnp.where(row // head_dim == half, grad_q, result)
            by_distance = unskewed(sum_ref[...])
            column = jnp.sum(hot * by_distance, axis=1, keepdims=True)
            table_ref[half] = jnp.broadcast_to(column, (buckets, tile)).T[0:1, :]
        dq_ref[...] = (result * scale).T.astype(bf16)
        dk_ref[...] = (mm(ds_ref[...], jnp.concatenate(mine_q, axis=0)) * scale).astype(bf16)
        dv_ref[...] = mm(prob_ref[...], jnp.concatenate(mine_g, axis=0)).astype(bf16)

    narrow = pl.BlockSpec((tokens, tile), lambda p: (0, p + first))
    tall = pl.BlockSpec((seq, tile), lambda p: (0, p + first))
    narrow_out = pl.BlockSpec((tokens, tile), lambda p: (0, p))
    tall_out = pl.BlockSpec((seq, tile), lambda p: (0, p))
    return pl.pallas_call(
        kernel,
        grid=(pairs,),
        in_specs=[
            narrow,
            tall,
            tall,
            pl.BlockSpec((per_step, 1, window), lambda p: (p + first, 0, 0)),
            pl.BlockSpec((seq, tokens), lambda p: (0, 0)),
            pl.BlockSpec((per_step, 1, tokens), lambda p: (p + first, 0, 0)),
            narrow,
            narrow,
            pl.BlockSpec((1, window), lambda p: (0, 0)),
        ],
        out_specs=(
            narrow_out,
            tall_out,
            tall_out,
            pl.BlockSpec((per_step, 1, buckets), lambda p: (p, 0, 0)),
        ),
        out_shape=(
            shape_of((tokens, pairs * tile), bf16),
            shape_of((seq, pairs * tile), bf16),
            shape_of((seq, pairs * tile), bf16),
            shape_of((pairs * per_step, 1, buckets), f32),
        ),
        scratch_shapes=[
            pltpu.VMEM((seq, per_step * tokens), bf16),
            pltpu.VMEM((seq, per_step * tokens), bf16),
            pltpu.VMEM((tile, window), f32),
            pltpu.VMEM((tile, window), f32),
        ],
        compiler_params=params(),
        cost_estimate=cost(40 * pairs * per_step * tokens * seq * tile, 8 * seq * pairs * tile),
        name="attend_back",
    )(queries, keys, values, bias, mask, lse, context, grad_context, bucket_window)


def chosen_logits(routes, logits):
    numbers = lax.broadcasted_iota(jnp.int32, logits.shape, 1)
    hot0 = routes[:, 0:1] == numbers
    hot1 = routes[:, 1:2] == numbers
    return hot0, hot1


def dispatch_call(me, context, out_blocks, tokens_in, smalls, routes, slot_map, heads):
    tokens, width = tokens_in.shape
    count = len(out_blocks)
    shards = out_blocks[0].shape[0]
    slots = slot_map.shape[0]

    def make(experts):
        def kernel(me_ref, ctx_ref, *refs):
            block_refs = refs[:count]
            (x_ref, small_ref, routes_ref, map_ref, wo_ref, low_ref, res_ref, ffn_ref, gate_ref, rows_ref) = refs[count:]
            for offset in range(count):
                place = lax.bitwise_xor(me_ref[0], offset)
                wo_ref[pl.ds(pl.multiple_of(place * shards, shards), shards), :] = block_refs[offset][...]
            context_low = ctx_ref[...].astype(bf16)
            low_ref[...] = context_low
            residual = x_ref[...].astype(f32) + mm(context_low, wo_ref[...])
            res_ref[...] = residual
            gain = small_ref[experts + heads + 1 : experts + heads + 2, :]
            inverse = lax.rsqrt(jnp.mean(residual * residual, axis=-1, keepdims=True) + eps)
            ffn_low = (residual * inverse * gain).astype(bf16)
            ffn_ref[...] = ffn_low
            rows_ref[...] = mm(map_ref[...], ffn_low).astype(bf16)
            logits = mm_t(ffn_low, small_ref[0:experts, :].astype(bf16))
            hot0, hot1 = chosen_logits(routes_ref[...], logits)
            first = jnp.sum(jnp.where(hot0, logits, 0.0), axis=1, keepdims=True)
            second = jnp.sum(jnp.where(hot1, logits, 0.0), axis=1, keepdims=True)
            top = jnp.maximum(first, second)
            weight0 = jnp.exp(first - top)
            weight1 = jnp.exp(second - top)
            whole = weight0 + weight1
            gate0 = weight0 / whole
            gate1 = weight1 / whole
            gate_ref[...] = jnp.concatenate([gate0, gate1], axis=1)

        return kernel

    def run(experts):
        vmem = pl.BlockSpec(memory_space=pltpu.VMEM)
        return pl.pallas_call(
            make(experts),
            in_specs=[pl.BlockSpec(memory_space=pltpu.SMEM)] + [vmem] * (count + 5),
            out_shape=(
                shape_of((width, width), bf16),
                shape_of((tokens, width), bf16),
                shape_of((tokens, width), f32),
                shape_of((tokens, width), bf16),
                shape_of((tokens, 2), f32),
                shape_of((slots, width), bf16),
            ),
            compiler_params=params(),
            cost_estimate=cost(4 * tokens * width * width, 8 * width * width),
            name="dispatch",
        )(me, context, *out_blocks, tokens_in, smalls, routes, slot_map)

    return run


def upstream_call(grads, expert_out):
    count, width = grads.shape
    hidden_width = expert_out.shape[0]
    step_width = 512

    def kernel(g_ref, out_ref, up_ref):
        up_ref[...] = mm_t(g_ref[...], out_ref[...])

    return pl.pallas_call(
        kernel,
        grid=(hidden_width // step_width,),
        in_specs=[whole_spec((count, width)), pl.BlockSpec((step_width, width), lambda s: (s, 0))],
        out_specs=pl.BlockSpec((count, step_width), lambda s: (0, s)),
        out_shape=shape_of((count, hidden_width), f32),
        compiler_params=params(),
        cost_estimate=cost(2 * count * width * hidden_width, 6 * count * hidden_width),
        name="upstream",
    )(grads, expert_out)


def expert_call(rows, grads, upstream, expert_in, expert_out, experts):
    count, width = rows.shape
    capacity = count // experts
    stride = capacity + extra_rows
    hidden_width = expert_in.shape[1]
    step_width = 512
    chunk_rows = count
    steps = hidden_width // step_width
    half_root = math.sqrt(0.5)
    density = 1.0 / math.sqrt(2.0 * math.pi)

    def kernel(x_ref, g_ref, up_ref, in_ref, out_ref, active_ref, gh_ref, made_ref, back_ref, made_sum, back_sum):
        step = pl.program_id(0)

        @pl.when(step == 0)
        def start():
            made_sum[...] = jnp.zeros((count, width), f32)
            back_sum[...] = jnp.zeros((count, width), f32)

        @pl.loop(0, count // chunk_rows)
        def chunk(index):
            at = pl.ds(pl.multiple_of(index * chunk_rows, chunk_rows), chunk_rows)
            hidden = mm(x_ref[at, :], in_ref[...])
            share = 0.5 + 0.5 * lax.erf(hidden * half_root)
            active = (hidden * share).astype(bf16)
            slope = share + hidden * (jnp.exp(hidden * hidden * -0.5) * density)
            grad_hidden = (up_ref[at, :] * slope).astype(bf16)
            active_ref[at, :] = active
            gh_ref[at, :] = grad_hidden
            made_sum[at, :] += mm(active, out_ref[...])
            back_sum[at, :] += mm_t(grad_hidden, in_ref[...])

        @pl.when(step == steps - 1)
        def finish():
            made = made_sum[...].astype(bf16)
            made_ref[...] = made
            products = made.astype(f32) * g_ref[...].astype(f32)
            folded = products[:, :tile]
            for at in range(tile, width, tile):
                folded = folded + products[:, at : at + tile]
            dots = jnp.broadcast_to(jnp.sum(folded.T, axis=0, keepdims=True), (8, count))
            coarse = dots.astype(bf16).astype(f32)
            fine = dots - coarse
            for expert in range(experts):
                at = expert * capacity
                shift = (count - at) % count
                lanes = [pltpu.roll(half, shift, 1)[:, :tile] for half in (coarse, fine)]
                lanes = jnp.concatenate(lanes, axis=0)
                lanes = jnp.concatenate([lanes, jnp.zeros((extra_rows, width - tile), f32)], axis=1)
                back_ref[expert, :capacity, :] = back_sum[at : at + capacity, :].astype(bf16)
                back_ref[expert, capacity:, :] = lanes.astype(bf16)

    full = whole_spec((count, width))
    return pl.pallas_call(
        kernel,
        grid=(steps,),
        in_specs=[
            full,
            full,
            pl.BlockSpec((count, step_width), lambda s: (0, s)),
            pl.BlockSpec((width, step_width), lambda s: (0, s)),
            pl.BlockSpec((step_width, width), lambda s: (s, 0)),
        ],
        out_specs=(
            pl.BlockSpec((count, step_width), lambda s: (0, s)),
            pl.BlockSpec((count, step_width), lambda s: (0, s)),
            full,
            whole_spec((experts, stride, width)),
        ),
        out_shape=(
            shape_of((count, hidden_width), bf16),
            shape_of((count, hidden_width), bf16),
            shape_of((count, width), bf16),
            shape_of((experts, stride, width), bf16),
        ),
        scratch_shapes=[pltpu.VMEM((count, width), f32), pltpu.VMEM((count, width), f32)],
        compiler_params=params(),
        cost_estimate=cost(8 * count * width * hidden_width, 8 * width * hidden_width),
        name="experts",
    )(rows, grads, upstream, expert_in, expert_out)


def offset_place(offsets, step, me_ref):
    offset = offsets[0]
    for at in range(1, len(offsets)):
        offset = jnp.where(step == at, offsets[at], offset)
    return lax.bitwise_xor(me_ref[0], offset)


def gate_column(me_ref, rows_ref, router_ref, others_ref):
    logits = mm_t(router_ref[...].astype(bf16), rows_ref[...])
    numbers = lax.broadcasted_iota(jnp.int32, logits.shape, 0).astype(f32)
    mine = jnp.sum(jnp.where(numbers == me_ref[1].astype(f32), logits, 0.0), axis=0, keepdims=True)
    other = jnp.sum(
        jnp.where(numbers == others_ref[...].astype(f32), logits, 0.0), axis=0, keepdims=True
    )
    return to_column(1.0 / (1.0 + jnp.exp(other - mine)))[:, 0:1]


def expert_grads_call(me, rows_t, rows_in, grads, active, grad_hidden, router, others, offsets):
    width, rows = rows_t.shape
    hidden_width = grad_hidden.shape[1]
    count = len(offsets)
    half = count // 2
    in_rows, out_rows = width // count, hidden_width // count

    def kernel(
        me_ref, xt_ref, rows_ref, g_ref, active_ref, gh_ref, router_ref, others_ref,
        in_give_ref, in_keep_ref, out_give_ref, out_keep_ref, gh_scr, g_scr,
    ):
        step = pl.program_id(0)

        @pl.when(step == 0)
        def start():
            column = gate_column(me_ref, rows_ref, router_ref, others_ref)
            g_scr[...] = (g_ref[...].astype(f32) * column).astype(bf16)
            for at in range(0, hidden_width, width):
                gh_scr[:, at : at + width] = (gh_ref[:, at : at + width].astype(f32) * column).astype(bf16)

        def shard(in_ref, out_ref):
            for at in range(0, hidden_width, width):
                in_ref[0, :, at : at + width] = mm(xt_ref[...], gh_scr[:, at : at + width]).astype(bf16)
            out_ref[0] = t_mm(active_ref[...], g_scr[...]).astype(bf16)

        @pl.when(step < half)
        def first():
            shard(in_give_ref, out_give_ref)

        @pl.when(step >= half)
        def second():
            shard(in_keep_ref, out_keep_ref)

    def give_at(s, me_ref):
        return (jnp.minimum(s, half - 1), 0, 0)

    def keep_at(s, me_ref):
        return (jnp.maximum(s - half, 0), 0, 0)

    return pl.pallas_call(
        kernel,
        grid_spec=pltpu.PrefetchScalarGridSpec(
            num_scalar_prefetch=1,
            grid=(count,),
            in_specs=[
                pl.BlockSpec((in_rows, rows), lambda s, me_ref: (offset_place(offsets, s, me_ref), 0)),
                whole_spec((rows, width)),
                whole_spec((rows, width)),
                pl.BlockSpec((rows, out_rows), lambda s, me_ref: (0, offset_place(offsets, s, me_ref))),
                whole_spec((rows, hidden_width)),
                whole_spec(router.shape),
                whole_spec((1, rows)),
            ],
            out_specs=(
                pl.BlockSpec((1, in_rows, hidden_width), give_at),
                pl.BlockSpec((1, in_rows, hidden_width), keep_at),
                pl.BlockSpec((1, out_rows, width), give_at),
                pl.BlockSpec((1, out_rows, width), keep_at),
            ),
            scratch_shapes=[pltpu.VMEM((rows, hidden_width), bf16), pltpu.VMEM((rows, width), bf16)],
        ),
        out_shape=(
            shape_of((half, in_rows, hidden_width), bf16),
            shape_of((half, in_rows, hidden_width), bf16),
            shape_of((half, out_rows, width), bf16),
            shape_of((half, out_rows, width), bf16),
        ),
        compiler_params=params(),
        cost_estimate=cost(4 * rows * width * hidden_width, 8 * width * hidden_width),
        name="expert_grads",
    )(me, rows_t, rows_in, grads, active, grad_hidden, router, others)


def combine_call(experts, heads, rows, places, gates, routes, cotangent, residual, ffn_low, smalls, w_output):
    tokens, width = cotangent.shape
    stride = rows.shape[1]
    capacity = stride - extra_rows

    def kernel(
        rows_ref, place_ref, gate_ref, routes_ref, cot_ref, res_ref, ffn_ref, small_ref, wo_ref,
        grad_res_ref, branch_ref, ctx_ref, router_ref, gain_ref,
    ):
        gate0, gate1 = gate_ref[:, 0:1], gate_ref[:, 1:2]
        lane_row = lax.broadcasted_iota(jnp.int32, (tokens, stride * experts), 1).astype(f32)
        rows = rows_ref[...].reshape(stride * experts, width)
        lane_slot = lax.broadcasted_iota(jnp.int32, (tokens, tile), 1).astype(f32)
        grad_ffn = jnp.zeros((tokens, width), f32)
        grad_gate = []
        for k, gate in enumerate((gate0, gate1)):
            first_row = routes_ref[:, k : k + 1].astype(f32) * stride
            place = place_ref[:, k : k + 1]
            back = (lane_row == first_row + place).astype(f32).astype(bf16)
            grad_ffn = grad_ffn + mm(back, rows) * gate
            coarse = (lane_row == first_row + capacity).astype(f32)
            fine = (lane_row == first_row + (capacity + 8)).astype(f32)
            dots = mm((coarse + fine).astype(bf16), rows[:, :tile])
            grad_gate.append(jnp.sum(jnp.where(lane_slot == place, dots, 0.0), axis=1, keepdims=True))
        grad_gate0, grad_gate1 = grad_gate
        mean_grad = gate0 * grad_gate0 + gate1 * grad_gate1
        chosen0 = gate0 * (grad_gate0 - mean_grad)
        chosen1 = gate1 * (grad_gate1 - mean_grad)
        numbers = lax.broadcasted_iota(jnp.int32, (tokens, experts), 1)
        hot0 = routes_ref[:, 0:1] == numbers
        hot1 = routes_ref[:, 1:2] == numbers
        grad_logits = jnp.where(hot0, chosen0, 0.0) + jnp.where(hot1, chosen1, 0.0)
        grad_logits = grad_logits.astype(bf16)
        router_ref[...] = t_mm(grad_logits, ffn_ref[...])
        grad_ffn = grad_ffn + mm(grad_logits, small_ref[0:experts, :].astype(bf16))
        gain = small_ref[experts + heads + 1 : experts + heads + 2, :]
        residual = res_ref[...]
        inverse = lax.rsqrt(jnp.mean(residual * residual, axis=-1, keepdims=True) + eps)
        scaled = grad_ffn * gain
        inner = jnp.mean(scaled * residual, axis=-1, keepdims=True)
        gain_ref[...] = jnp.sum(grad_ffn * residual * inverse, axis=0, keepdims=True)
        grad_res = cot_ref[...].astype(f32) + inverse * scaled - residual * (inverse * inverse * inverse * inner)
        grad_res_ref[...] = grad_res
        branch = grad_res.astype(bf16)
        branch_ref[...] = branch
        ctx_ref[...] = mm_t(branch, wo_ref[...]).astype(bf16)

    return pl.pallas_call(
        kernel,
        out_shape=(
            shape_of((tokens, width), f32),
            shape_of((tokens, width), bf16),
            shape_of((tokens, width), bf16),
            shape_of((experts, width), f32),
            shape_of((1, width), f32),
        ),
        compiler_params=params(),
        cost_estimate=cost(6 * tokens * width * width, 8 * width * width),
        name="combine",
    )(rows, places, gates, routes, cotangent, residual, ffn_low, smalls, w_output)


def split_rows(full_ref, me_index, count, shards, main, give_ref, keep_ref):
    for offset in range(count):
        place = lax.bitwise_xor(me_index, offset)
        target = give_ref if offset & 1 else keep_ref
        target[offset // 2, :, :main] = full_ref[
            pl.ds(pl.multiple_of(place * shards, shards), shards), :
        ].astype(bf16)


def small_tiles(pieces, rows, shards):
    per_tile = shards // rows
    return -(-pieces // per_tile), per_tile


def first_grads_call(me, dq, dk, dv, normed_t, context_low, branch, grad_router, grad_gain, table, count):
    tokens, part = dq.shape
    width, seq = normed_t.shape
    shards = width // count
    experts = grad_router.shape[0]
    heads, _, buckets = table.shape
    piece_rows = -(-(experts + 1) // 16) * 16
    pieces = width // tile + 1
    tiles, per_tile = small_tiles(pieces, piece_rows, shards)
    main = width + 3 * part

    def kernel(
        me_ref, dq_ref, dk_ref, dv_ref, normed_ref, ctx_ref, branch_ref, router_ref, gain_ref, table_ref,
        give_ref, keep_ref, full_ref,
    ):
        own = pl.ds(pl.multiple_of(me_ref[0] * tokens, tokens), tokens)
        full_ref[:, :width] = t_mm(ctx_ref[...], branch_ref[...])
        full_ref[:, width : width + part] = mm(normed_ref[:, own], dq_ref[...])
        full_ref[:, width + part : width + 2 * part] = mm(normed_ref[...], dk_ref[...])
        full_ref[:, width + 2 * part :] = mm(normed_ref[...], dv_ref[...])
        split_rows(full_ref, me_ref[0], count, shards, main, give_ref, keep_ref)
        small = jnp.concatenate(
            [router_ref[...], gain_ref[...], jnp.zeros((piece_rows - experts - 1, width), f32)], axis=0
        )
        rows = [table_ref[head] for head in range(heads)]
        rows = jnp.concatenate(rows + [jnp.zeros((piece_rows - heads, buckets), f32)], axis=0)
        rows = jnp.concatenate([rows, jnp.zeros((piece_rows, tile - buckets), f32)], axis=1)
        blocks = [small[:, at : at + tile] for at in range(0, width, tile)] + [rows]
        blocks = [block.astype(bf16) for block in blocks]
        for target in (give_ref, keep_ref):
            for at in range(count // 2):
                target[at, :, main:] = jnp.zeros((shards, tiles * tile), bf16)
                for index, block in enumerate(blocks):
                    row = index % per_tile * piece_rows
                    col = main + index // per_tile * tile
                    target[at, row : row + piece_rows, col : col + tile] = block

    vmem = pl.BlockSpec(memory_space=pltpu.VMEM)
    return pl.pallas_call(
        kernel,
        in_specs=[pl.BlockSpec(memory_space=pltpu.SMEM)] + [vmem] * 9,
        out_shape=(shape_of((count // 2, shards, main + tiles * tile), bf16),) * 2,
        scratch_shapes=[pltpu.VMEM((width, main), f32)],
        compiler_params=params(),
        cost_estimate=cost(5 * seq * width * part, 10 * seq * width),
        name="first_grads",
    )(me, dq, dk, dv, normed_t, context_low, branch, grad_router, grad_gain, table)


def first_smalls(columns, experts, heads, buckets, width, shards):
    piece_rows = -(-(experts + 1) // 16) * 16
    pieces = width // tile + 1
    _, per_tile = small_tiles(pieces, piece_rows, shards)
    found = []
    for index in range(pieces):
        row, col = index % per_tile * piece_rows, index // per_tile * tile
        found.append(columns[row : row + piece_rows, col : col + tile])
    wide = jnp.concatenate(found[:-1], axis=1)
    return wide[:experts], wide[experts], found[-1][:heads, :buckets]


def second_grads_call(me, dq, dk, dv, normed_t, table, count):
    tokens, part = dq.shape
    width, seq = normed_t.shape
    shards = width // count
    heads, _, buckets = table.shape
    main = 3 * part

    def kernel(me_ref, dq_ref, dk_ref, dv_ref, normed_ref, table_ref, give_ref, keep_ref, full_ref):
        own = pl.ds(pl.multiple_of(me_ref[0] * tokens, tokens), tokens)
        full_ref[:, :part] = mm(normed_ref[:, own], dq_ref[...])
        full_ref[:, part : 2 * part] = mm(normed_ref[...], dk_ref[...])
        full_ref[:, 2 * part :] = mm(normed_ref[...], dv_ref[...])
        split_rows(full_ref, me_ref[0], count, shards, main, give_ref, keep_ref)
        rows = [table_ref[head] for head in range(heads)]
        rows = jnp.concatenate(rows + [jnp.zeros((16 - heads, buckets), f32)], axis=0)
        rows = jnp.concatenate([rows, jnp.zeros((16, tile - buckets), f32)], axis=1).astype(bf16)
        for target in (give_ref, keep_ref):
            for at in range(count // 2):
                target[at, :, main:] = jnp.zeros((shards, tile), bf16)
                target[at, :16, main:] = rows

    vmem = pl.BlockSpec(memory_space=pltpu.VMEM)
    return pl.pallas_call(
        kernel,
        in_specs=[pl.BlockSpec(memory_space=pltpu.SMEM)] + [vmem] * 5,
        out_shape=(shape_of((count // 2, shards, main + tile), bf16),) * 2,
        scratch_shapes=[pltpu.VMEM((width, main), f32)],
        compiler_params=params(),
        cost_estimate=cost(5 * seq * width * part, 10 * seq * width),
        name="second_grads",
    )(me, dq, dk, dv, normed_t, table)


def rows_back_call(me, first, second, weights, count):
    tokens, part = first[0].shape
    width = weights[0].shape[0]

    def kernel(
        me_ref, dq1_ref, dk1_ref, dv1_ref, dq2_ref, dk2_ref, dv2_ref, wq_ref, wk_ref, wv_ref, give_ref, keep_ref,
    ):
        for offset in range(count):
            place = lax.bitwise_xor(me_ref[0], offset)
            at = pl.ds(pl.multiple_of(place * tokens, tokens), tokens)
            total = mm_t(dk1_ref[at, :], wk_ref[:, :part]) + mm_t(dk2_ref[at, :], wk_ref[:, part:])
            total = total + mm_t(dv1_ref[at, :], wv_ref[:, :part]) + mm_t(dv2_ref[at, :], wv_ref[:, part:])
            if offset == 0:
                total = total + mm_t(dq1_ref[...], wq_ref[:, :part]) + mm_t(dq2_ref[...], wq_ref[:, part:])
            target = give_ref if offset & 1 else keep_ref
            target[offset // 2] = total.astype(bf16)

    vmem = pl.BlockSpec(memory_space=pltpu.VMEM)
    return pl.pallas_call(
        kernel,
        in_specs=[pl.BlockSpec(memory_space=pltpu.SMEM)] + [vmem] * 9,
        out_shape=(shape_of((count // 2, tokens, width), bf16),) * 2,
        compiler_params=params(),
        cost_estimate=cost(10 * count * tokens * width * width, 10 * count * tokens * width),
        name="rows_back",
    )(me, *first, *second, *weights)


def finish_call(chain1, chain2, weights, gain, half_cols):
    shards, width = weights[0].shape
    rest = width - half_cols

    def kernel(c1_ref, c2_ref, wq_ref, wk_ref, wv_ref, gain_ref, gq_ref, gk_ref, gv_ref, go_ref, out_ref):
        total = jnp.zeros((shards, 1), f32)
        go_ref[...] = c1_ref[:, :width].astype(f32)
        for part, (weight_ref, grad_ref) in enumerate(((wq_ref, gq_ref), (wk_ref, gk_ref), (wv_ref, gv_ref))):
            left = c1_ref[:, width + part * half_cols : width + (part + 1) * half_cols].astype(f32)
            right = c2_ref[:, part * rest : (part + 1) * rest].astype(f32)
            grad_ref[:, :half_cols] = left
            grad_ref[:, half_cols:] = right
            weight = weight_ref[...].astype(f32)
            total = total + jnp.sum(left * weight[:, :half_cols], axis=1, keepdims=True)
            total = total + jnp.sum(right * weight[:, half_cols:], axis=1, keepdims=True)
        out_ref[...] = jnp.broadcast_to(total, (shards, tile)).T[0:1, :] / gain_ref[...].astype(f32)

    return pl.pallas_call(
        kernel,
        out_shape=(shape_of((shards, width), f32),) * 4 + (shape_of((1, shards), f32),),
        compiler_params=params(),
        cost_estimate=cost(6 * shards * width, 30 * shards * width),
        name="finish",
    )(chain1, chain2, *weights, gain[None, :])


def gather_blocks(value, axis_size, late=None):
    blocks = {0: value}
    bit = 2
    while bit < axis_size:
        for offset in sorted(blocks):
            blocks[offset | bit] = swap(blocks[offset], "fsdp", axis_size, bit)
            if late is not None:
                blocks[offset | bit] = ordered(blocks[offset | bit], late)[0]
        bit *= 2
    for offset in sorted(blocks):
        blocks[offset | 1] = swap(blocks[offset], "fsdp", axis_size, 1)
    return [blocks[offset] for offset in range(axis_size)]


def scatter_bits(axis_size):
    bits, bit = [1], axis_size // 2
    while bit > 1:
        bits.append(bit)
        bit //= 2
    return [bit for bit in bits if bit < axis_size]


def added(left_side, right_side):
    return left_side.astype(f32) + right_side.astype(f32)


def core_sum(given, kept, axis_size):
    arrived = swap(given, "fsdp", axis_size, 1)
    return {2 * at: added(kept[at], arrived[at]).astype(bf16) for at in range(axis_size // 2)}


def far_sum(pieces, axis_size, early=None, late=None, cuts=1):
    for bit in scatter_bits(axis_size):
        if bit == 1:
            continue
        left = {}
        for offset in sorted(pieces):
            if offset & bit:
                continue
            found = []
            for leaving in jnp.split(pieces[offset | bit].astype(bf16), cuts, axis=0):
                if early is not None:
                    leaving = ordered(leaving, early)[0]
                found.append(swap(leaving, "fsdp", axis_size, bit))
                early = found[-1]
            if late is not None:
                found[-1] = ordered(found[-1], late)[0]
            left[offset] = added(pieces[offset], jnp.concatenate(found, axis=0))
        pieces = left
    return pieces[0]


def far_steps(pieces, axis_size, fractions, early=None):
    bits = [bit for bit in scatter_bits(axis_size) if bit > 1]
    for bit in bits[:-1]:
        pieces = {
            offset: added(
                pieces[offset], swap(pieces[offset | bit].astype(bf16), "fsdp", axis_size, bit)
            )
            for offset in sorted(pieces)
            if not offset & bit
        }
    bit = bits[-1]
    rows = pieces[0].shape[0]
    leaving = pieces[bit].astype(bf16)
    found, begin = [], 0
    for step, fraction in enumerate(fractions):
        end = rows if step == len(fractions) - 1 else begin + rows * fraction // 12
        part = leaving[begin:end]
        if early is not None:
            part = ordered(part, early)[0]
        early = yield swap(part, "fsdp", axis_size, bit)
        found.append(early)
        begin = end
    yield added(pieces[0], jnp.concatenate(found, axis=0))


def all_sum_expert(value, axis_size, index, before_last=()):
    rows = value.shape[0]
    parts = jnp.pad(value.astype(bf16), ((0, -rows % (axis_size // 2)), (0, 0)))
    bit, bits = 1, []
    while bit < axis_size:
        bits.append(bit)
        bit *= 2
    inner = bits.pop()
    for bit in bits:
        low_half, high_half = jnp.split(parts, 2, axis=0)
        upper = (index & bit) != 0
        keep = jnp.where(upper, high_half, low_half)
        give = jnp.where(upper, low_half, high_half)
        arrived = swap(give, "expert", axis_size, bit)
        parts = added(keep, arrived).astype(bf16)
    parts = added(parts, swap(parts, "expert", axis_size, inner)).astype(bf16)
    for bit in reversed(bits):
        if bit == 1 and before_last:
            parts, *before_last = ordered(parts, *before_last)
        other = swap(parts, "expert", axis_size, bit)
        upper = (index & bit) != 0
        parts = jnp.concatenate(
            [jnp.where(upper, other, parts), jnp.where(upper, parts, other)], axis=0
        )
    return parts[:rows], before_last


def ordered(*values):
    return lax.optimization_barrier(values)


def build(count, expert_ranks):
    def per_device(
        tokens_in,
        seg_ids,
        routes,
        buckets,
        attn_gain,
        w_query,
        w_key,
        w_value,
        w_output,
        bias_table,
        ffn_gain,
        w_router,
        w_in,
        w_out,
        cotangent,
    ):
        tokens, width = tokens_in.shape
        shards, experts = w_router.shape
        bucket_rows, heads = bias_table.shape
        bucket_count = bucket_rows * count
        head_dim = width // heads
        seq = buckets.shape[0]
        top_count = routes.shape[1]
        capacity = 3 * top_count * tokens // (2 * experts)
        slots = experts * capacity
        fsdp_index = lax.axis_index("fsdp")
        expert_index = lax.axis_index("expert")
        me = jnp.stack([fsdp_index, expert_index]).astype(jnp.int32)

        used = experts + heads + 3
        small_rows = -(-used // 16) * 16
        packed = pack_call(
            me, (w_query, w_key, w_value), tokens_in, seg_ids[None, :],
            jnp.stack([attn_gain, ffn_gain]), bias_table, w_router.T, small_rows, width,
        )
        blocks = gather_blocks(packed, count)
        leaving_output = ordered(w_output, blocks[-2])[0]
        routes, blocks[1] = ordered(routes, blocks[1])
        padded_buckets = jnp.concatenate([jnp.full((seq,), -1, jnp.int32), buckets])
        bucket_window = lax.dynamic_slice_in_dim(
            padded_buckets, fsdp_index * tokens, seq + tokens, 0
        )[None, :]

        slot_map, back0, back1, grad_rows_out, places = route_call(routes, cotangent, capacity, experts)
        grad_rows_in = lax.all_to_all(
            grad_rows_out, "expert", split_axis=0, concat_axis=0, tiled=True
        )
        others = grad_rows_in[:, capacity, :capacity].reshape(1, slots)
        grad_rows_in = grad_rows_in[:, :capacity, :].reshape(slots, width)

        (queries, keys, values, normed, sequence, wq, wk, wv, smalls, bias, mask) = project_call(
            me, blocks, shards, small_rows, bucket_window, heads, bucket_count, experts
        )
        out_blocks = gather_blocks(leaving_output, count, queries)
        queries, grad_rows_in, others = ordered(queries, grad_rows_in, others)
        context, lse = attend_call(queries, keys, values, bias, mask, head_dim)
        wo, context_low, residual, ffn_low, gates, rows_out = dispatch_call(
            me, context, out_blocks, tokens_in, smalls, routes, slot_map, heads
        )(experts)
        normed_t = ordered(normed, rows_out)[0].T
        upstream = upstream_call(ordered(grad_rows_in, rows_out)[0], w_out[0])
        rows_in = lax.all_to_all(
            rows_out.reshape(experts, capacity, width),
            "expert",
            split_axis=0,
            concat_axis=0,
            tiled=True,
        ).reshape(slots, width)
        rows_in, normed_t, upstream = ordered(rows_in, normed_t, upstream)
        active, grad_hidden, made, row_grads = expert_call(
            rows_in, grad_rows_in, upstream, w_in[0], w_out[0], experts
        )
        row_grads_back = lax.all_to_all(
            row_grads, "expert", split_axis=0, concat_axis=0, tiled=True
        )

        rows_t = rows_in.T
        give = [offset for offset in range(count) if offset & 1]
        keep = [offset for offset in range(count) if not offset & 1]
        router = smalls[:experts]
        in_give, in_keep, out_give, out_keep = expert_grads_call(
            me, rows_t, rows_in, grad_rows_in, active, grad_hidden, router, others, give + keep
        )
        in_give, out_give, row_grads_back = ordered(in_give, out_give, row_grads_back)
        in_pieces = core_sum(in_give, in_keep, count)
        out_pieces = core_sum(out_give, out_keep, count)

        grad_residual, branch, grad_context, grad_router, grad_gain_ffn = combine_call(
            experts, heads, row_grads_back, places, gates, routes, cotangent,
            residual, ffn_low, smalls, wo,
        )
        pairs = width // tile
        near = pairs // 2
        last = max(in_pieces)
        grad_context, in_pieces[last] = ordered(grad_context, in_pieces[last])
        *part1, table1 = attend_back_call(
            queries, keys, values, bias, mask, lse, context, grad_context, bucket_window,
            bucket_count, head_dim, 0, near,
        )
        in_steps = far_steps(in_pieces, count, (5, 3, 4))
        arrived = next(in_steps)
        part1[0], arrived = ordered(part1[0], arrived)
        give1, keep1 = first_grads_call(
            me, *part1, normed_t, context_low, branch, grad_router, grad_gain_ffn, table1, count
        )
        arrived = in_steps.send(arrived)
        made = ordered(made, give1)[0]
        made_back = lax.all_to_all(
            made.reshape(experts, capacity, width),
            "expert",
            split_axis=0,
            concat_axis=0,
            tiled=True,
        ).reshape(slots, width)
        pieces1 = core_sum(give1, keep1, count)
        last = max(pieces1)
        grad_context, pieces1[last], arrived = ordered(grad_context, pieces1[last], arrived)
        *part2, table2 = attend_back_call(
            queries, keys, values, bias, mask, lse, context, grad_context, bucket_window,
            bucket_count, head_dim, near, pairs - near,
        )
        give2, keep2 = second_grads_call(me, *part2, normed_t, table2, count)
        sum1 = far_sum(pieces1, count, None, give2)
        pieces2 = core_sum(give2, keep2, count)
        last = max(pieces2)
        dv2, pieces2[last] = ordered(part2[2], pieces2[last])
        rows_give, rows_keep = rows_back_call(
            me, part1, (part2[0], part2[1], dv2), (wq, wk, wv), count
        )
        steps2 = far_steps(pieces2, count, (9, 3))
        sum2 = steps2.send(steps2.send(ordered(next(steps2), rows_give)[0]))
        arrived = in_steps.send(ordered(arrived, sum1)[0])
        in_sum = in_steps.send(arrived)
        grad_normed = far_sum(core_sum(rows_give, rows_keep, count), count, sum2)
        out_steps = far_steps(out_pieces, count, (6, 6), arrived)
        arrived, sum2 = ordered(next(out_steps), sum2)
        out_sum = out_steps.send(out_steps.send(arrived))
        chain1, _ = all_sum_expert(sum1, expert_ranks, expert_index)
        chain2, (out_sum, grad_normed) = all_sum_expert(
            sum2, expert_ranks, expert_index, (out_sum, grad_normed)
        )
        grad_shards = [in_sum, out_sum]
        half_cols = near * tile

        inputs = tokens_in.astype(f32)
        inverse = lax.rsqrt(jnp.mean(inputs * inputs, axis=-1, keepdims=True) + eps)
        gain_attn = smalls[experts + heads]
        scaled = grad_normed * gain_attn
        inner = jnp.mean(scaled * inputs, axis=-1, keepdims=True)
        grad_tokens = grad_residual + inverse * scaled - inputs * inverse**3 * inner

        made_back = ordered(made_back, sum2)[0]
        picked0 = mm(back0, made_back)
        picked1 = mm(back1, made_back)
        block_out = (residual + gates[:, 0:1] * picked0 + gates[:, 1:2] * picked1).astype(bf16)

        rest = width - half_cols
        *shards_out, grad_gain_attn = finish_call(
            chain1, chain2, (w_query, w_key, w_value), attn_gain, half_cols
        )
        router_sum, gain_sum, table_left = first_smalls(
            chain1[:, width + 3 * half_cols :].astype(f32), experts, 2 * near, bucket_count, width, shards
        )
        table_right = chain2[: heads - 2 * near, 3 * rest : 3 * rest + bucket_count].astype(f32)
        table_cols = lax.dynamic_slice_in_dim(
            jnp.concatenate([table_left, table_right], axis=0), fsdp_index * bucket_rows, bucket_rows, 1
        )
        return (
            block_out,
            grad_tokens,
            grad_gain_attn[0],
            shards_out[0],
            shards_out[1],
            shards_out[2],
            shards_out[3],
            table_cols.T,
            lax.dynamic_slice_in_dim(gain_sum, fsdp_index * shards, shards, 0),
            lax.dynamic_slice_in_dim(router_sum, fsdp_index * shards, shards, 1).T,
            grad_shards[0][None],
            grad_shards[1][None],
        )

    return per_device


def solution(mesh):
    return jax.shard_map(
        build(mesh.shape["fsdp"], mesh.shape["expert"]),
        mesh=mesh,
        in_specs=(
            P(("expert", "fsdp"), None),
            P(("expert", "fsdp")),
            P(("expert", "fsdp"), None),
            P(),
            P("fsdp"),
            P("fsdp", None),
            P("fsdp", None),
            P("fsdp", None),
            P("fsdp", None),
            P("fsdp", None),
            P("fsdp"),
            P("fsdp", None),
            P("expert", None, None),
            P("expert", None, None),
            P(("expert", "fsdp"), None),
        ),
        out_specs=(
            P(("expert", "fsdp"), None),
            P(("expert", "fsdp"), None),
            P("fsdp"),
            P("fsdp", None),
            P("fsdp", None),
            P("fsdp", None),
            P("fsdp", None),
            P("fsdp", None),
            P("fsdp"),
            P("fsdp", None),
            P("expert", "fsdp", None),
            P("expert", "fsdp", None),
        ),
        check_vma=False,
    )
```

```python
import math

import jax
import jax.numpy as jnp
from jax import lax
from jax.experimental import pallas as pl
from jax.experimental.pallas import tpu as pltpu
from jax.sharding import PartitionSpec as P

eps = 1e-06
log2e = math.log2(math.e)
masked_score = -1e30
f32 = jnp.float32
bf16 = jnp.bfloat16
tile = 128
extra_rows = 16


def mm(left_side, right_side):
    return lax.dot_general(
        left_side, right_side, (((1,), (0,)), ((), ())), preferred_element_type=f32
    )


def mm_t(left_side, right_side):
    return lax.dot_general(
        left_side, right_side, (((1,), (1,)), ((), ())), preferred_element_type=f32
    )


def t_mm(left_side, right_side):
    return lax.dot_general(
        left_side, right_side, (((0,), (0,)), ((), ())), preferred_element_type=f32
    )


def swap(value, axis_name, axis_size, bit):
    return lax.ppermute(value, axis_name, [(i, i ^ bit) for i in range(axis_size)])


def params(megabytes=56):
    return pltpu.CompilerParams(vmem_limit_bytes=megabytes << 20)


def cost(flops, moved):
    return pl.CostEstimate(flops=int(flops) >> 8, bytes_accessed=int(moved) >> 8, transcendentals=0)


def shape_of(dims, dtype):
    return jax.ShapeDtypeStruct(dims, dtype)


def whole_spec(dims):
    return pl.BlockSpec(dims, lambda *unused: (0,) * len(dims))


def to_column(row):
    return jnp.broadcast_to(row, (tile, row.shape[1])).T


def route_kernel(capacity, routes_ref, cot_ref, map_ref, back0_ref, back1_ref, out_ref, slot_ref):
    tokens = routes_ref.shape[0]
    slots = map_ref.shape[0]
    experts = slots // capacity
    routes = routes_ref[...]
    first, second = routes[:, 0:1], routes[:, 1:2]
    numbers = lax.broadcasted_iota(jnp.int32, (tokens, experts), 1)
    hot0 = (first == numbers).astype(f32)
    hot1 = (second == numbers).astype(f32)
    rows = lax.broadcasted_iota(jnp.int32, (tokens, tokens), 0)
    cols = lax.broadcasted_iota(jnp.int32, (tokens, tokens), 1)
    before = (cols < rows).astype(f32).astype(bf16)
    earlier = mm(before, (hot0 + hot1).astype(bf16))
    slot0 = jnp.sum(hot0 * earlier, axis=1, keepdims=True)
    slot1 = jnp.sum(hot1 * (earlier + hot0), axis=1, keepdims=True)
    slot_ref[...] = jnp.concatenate([slot0, slot1], axis=1)
    dest0 = first.astype(f32) * capacity + slot0
    dest1 = second.astype(f32) * capacity + slot1
    lane_slot = lax.broadcasted_iota(jnp.int32, (tokens, slots), 1).astype(f32)
    back0_ref[...] = (lane_slot == dest0).astype(f32).astype(bf16)
    back1_ref[...] = (lane_slot == dest1).astype(f32).astype(bf16)
    row0 = jnp.broadcast_to(dest0, (tokens, tile)).T[0:1, :]
    row1 = jnp.broadcast_to(dest1, (tokens, tile)).T[0:1, :]
    row_slot = lax.broadcasted_iota(jnp.int32, (slots, tokens), 0).astype(f32)
    hot = ((row_slot == row0).astype(f32) + (row_slot == row1).astype(f32)).astype(bf16)
    map_ref[...] = hot
    rows = mm(hot, cot_ref[...]).astype(bf16)
    others = back0_ref[...].astype(f32) * second.astype(f32) + back1_ref[...].astype(f32) * first.astype(f32)
    others = jnp.broadcast_to(jnp.sum(others, axis=0, keepdims=True), (extra_rows, slots))
    width = rows.shape[1]
    for expert in range(experts):
        at = expert * capacity
        lanes = pltpu.roll(others, (slots - at) % slots, 1)[:, :tile]
        lanes = jnp.concatenate([lanes, jnp.zeros((extra_rows, width - tile), f32)], axis=1)
        out_ref[expert, :capacity, :] = rows[at : at + capacity, :]
        out_ref[expert, capacity:, :] = lanes.astype(bf16)


def route_call(routes, cotangent, capacity, experts):
    tokens, width = cotangent.shape
    slots = experts * capacity
    return pl.pallas_call(
        lambda *refs: route_kernel(capacity, *refs),
        out_shape=(
            shape_of((slots, tokens), bf16),
            shape_of((tokens, slots), bf16),
            shape_of((tokens, slots), bf16),
            shape_of((experts, capacity + extra_rows, width), bf16),
            shape_of((tokens, 2), f32),
        ),
        compiler_params=params(),
        cost_estimate=cost(2 * slots * tokens * width, 4 * slots * width),
        name="route",
    )(routes, cotangent)


def pack_call(me, weights, tokens_in, seg_row, gains, table, router, small, width):
    shards = weights[0].shape[0]
    tokens = tokens_in.shape[0]
    experts, heads = router.shape[0], table.shape[1]
    used = experts + heads + 3

    def placed(me_ref, rows):
        at = lax.broadcasted_iota(jnp.int32, (rows, width), 1)
        own = lax.broadcasted_iota(jnp.int32, (rows, width), 0) + me_ref[0] * rows
        return (at == own).astype(f32).astype(bf16)

    def kernel(me_ref, wq_ref, wk_ref, wv_ref, x_ref, seg_ref, gain_ref, table_ref, router_ref, out_ref):
        for at, ref in enumerate((wq_ref, wk_ref, wv_ref)):
            out_ref[at * shards : (at + 1) * shards, :] = ref[...]
        out_ref[3 * shards : 3 * shards + tokens, :] = x_ref[...]
        columns = placed(me_ref, shards)
        rows = [
            mm(router_ref[...], columns),
            t_mm(table_ref[...], placed(me_ref, table_ref.shape[0])),
            mm(gain_ref[...], columns),
            jnp.zeros((small - used, width), f32),
            jnp.concatenate([seg_ref[...].astype(f32), jnp.zeros((1, width - tokens), f32)], axis=1),
        ]
        out_ref[3 * shards + tokens :, :] = jnp.concatenate(rows, axis=0).astype(bf16)

    vmem = pl.BlockSpec(memory_space=pltpu.VMEM)
    return pl.pallas_call(
        kernel,
        in_specs=[pl.BlockSpec(memory_space=pltpu.SMEM)] + [vmem] * 8,
        out_shape=shape_of((3 * shards + tokens + small, width), bf16),
        compiler_params=params(),
        cost_estimate=cost(1, 4 * shards * width),
        name="pack",
    )(me, *weights, tokens_in, seg_row, gains, table, router)


def project_call(me, blocks, shards, small, bucket_window, heads, buckets, experts):
    count = len(blocks)
    rows, width = blocks[0].shape
    tokens = rows - 3 * shards - small
    seq = count * tokens
    window = bucket_window.shape[1]

    def kernel(me_ref, *refs):
        block_refs = refs[:count]
        (bucket_ref, q_ref, k_ref, v_ref, normed_ref, tok_ref, wq_ref, wk_ref, wv_ref, small_ref, bias_ref, mask_ref) = refs[count:]
        me_index = me_ref[0]
        totals = jnp.zeros((small, width), f32)
        own_docs = block_refs[0][rows - small :, :].astype(f32)[small - 1 :, :tokens]
        for offset in range(count):
            place = lax.bitwise_xor(me_index, offset)
            row = pl.multiple_of(place * shards, shards)
            for part, full_ref in enumerate((wq_ref, wk_ref, wv_ref)):
                full_ref[pl.ds(row, shards), :] = block_refs[offset][part * shards : (part + 1) * shards, :]
            token_row = pl.multiple_of(place * tokens, tokens)
            tok_ref[pl.ds(token_row, tokens), :] = block_refs[offset][3 * shards : rows - small, :]
            extra = block_refs[offset][rows - small :, :].astype(f32)
            totals = totals + extra
            docs = to_column(extra[small - 1 :, :tokens])
            docs = jnp.concatenate([docs] * (tokens // tile), axis=1)
            mask_ref[pl.ds(token_row, tokens), :] = jnp.where(docs == own_docs, 0.0, masked_score)
        small_ref[...] = totals
        gain = totals[experts + heads : experts + heads + 1, :]
        table = totals[experts : experts + heads, :buckets].astype(bf16)
        numbers = lax.broadcasted_iota(jnp.int32, (buckets, window), 0)
        hot = (numbers == bucket_ref[...]).astype(f32).astype(bf16)
        by_distance = mm(table, hot) * log2e
        by_distance = jnp.where(bucket_ref[...] < 0, masked_score, by_distance)
        for head in range(heads):
            bias_ref[head] = by_distance[head : head + 1, :]

        @pl.loop(0, count)
        def chunk(index):
            rows = pl.ds(pl.multiple_of(index * tokens, tokens), tokens)
            values = tok_ref[rows, :].astype(f32)
            inverse = lax.rsqrt(jnp.mean(values * values, axis=-1, keepdims=True) + eps)
            normed = (values * inverse * gain).astype(bf16)
            normed_ref[rows, :] = normed
            k_ref[rows, :] = mm(normed, wk_ref[...]).astype(bf16)
            v_ref[rows, :] = mm(normed, wv_ref[...]).astype(bf16)

        own = normed_ref[pl.ds(pl.multiple_of(me_index * tokens, tokens), tokens), :]
        q_ref[...] = mm(own, wq_ref[...]).astype(bf16)

    vmem = pl.BlockSpec(memory_space=pltpu.VMEM)
    return pl.pallas_call(
        kernel,
        in_specs=[pl.BlockSpec(memory_space=pltpu.SMEM)] + [vmem] * (count + 1),
        out_shape=(
            shape_of((tokens, width), bf16),
            shape_of((seq, width), bf16),
            shape_of((seq, width), bf16),
            shape_of((seq, width), bf16),
            shape_of((seq, width), bf16),
            shape_of((width, width), bf16),
            shape_of((width, width), bf16),
            shape_of((width, width), bf16),
            shape_of((small, width), f32),
            shape_of((heads, 1, window), f32),
            shape_of((seq, tokens), f32),
        ),
        compiler_params=params(),
        cost_estimate=cost(2 * width * width * (2 * seq + tokens), 20 * seq * width),
        name="project",
    )(me, *blocks, bucket_window)


def skewed(bias_row, window):
    spread = jnp.broadcast_to(bias_row, (tile, window))
    return pltpu.roll(spread, 0, 1, stride=1, stride_axis=0)


def attend_call(queries, keys, values, bias, mask, head_dim):
    tokens, width = queries.shape
    seq = keys.shape[0]
    heads, _, window = bias.shape
    pairs = width // tile
    per_step = heads // pairs
    key_blocks = seq // tile
    scale = head_dim**-0.5 * log2e

    def kernel(q_ref, k_ref, v_ref, bias_ref, mask_ref, ctx_ref, lse_ref, score_ref, prob_ref, skew_ref):
        lane = lax.broadcasted_iota(jnp.int32, (tokens, tile), 1)
        row = lax.broadcasted_iota(jnp.int32, (tile, tokens), 0)
        query = q_ref[...]
        values_t = v_ref[...].T
        result = jnp.zeros((tile, tokens), f32)
        for half in range(per_step):
            mine = jnp.where(lane // head_dim == half, query, jnp.zeros_like(query))
            skew_ref[...] = skewed(bias_ref[half], window)
            top = jnp.full((8, tokens), -3e38, f32)
            for block in range(key_blocks):
                rows = pl.ds(block * tile, tile)
                begin = tile * (key_blocks - block)
                scores = mm_t(k_ref[rows, :], mine) * scale
                scores = scores + (skew_ref[:, begin : begin + tokens] + mask_ref[rows, :])
                score_ref[rows, :] = scores
                top = jnp.maximum(top, jnp.max(scores.reshape(tile // 8, 8, tokens), axis=0))
            top = jnp.max(top, axis=0, keepdims=True)
            total = jnp.zeros((8, tokens), f32)
            for block in range(key_blocks):
                rows = pl.ds(block * tile, tile)
                probs = jnp.exp2(score_ref[rows, :] - top)
                prob_ref[rows, :] = probs.astype(bf16)
                total = total + jnp.sum(probs.reshape(tile // 8, 8, tokens), axis=0)
            total = jnp.sum(total, axis=0, keepdims=True)
            lse_ref[half] = top + jnp.log2(total)
            mixed = mm(values_t, prob_ref[...]) * (1.0 / total)
            result = jnp.where(row // head_dim == half, mixed, result)
        ctx_ref[...] = result.T

    return pl.pallas_call(
        kernel,
        grid=(pairs,),
        in_specs=[
            pl.BlockSpec((tokens, tile), lambda p: (0, p)),
            pl.BlockSpec((seq, tile), lambda p: (0, p)),
            pl.BlockSpec((seq, tile), lambda p: (0, p)),
            pl.BlockSpec((per_step, 1, window), lambda p: (p, 0, 0)),
            pl.BlockSpec((seq, tokens), lambda p: (0, 0)),
        ],
        out_specs=(
            pl.BlockSpec((tokens, tile), lambda p: (0, p)),
            pl.BlockSpec((per_step, 1, tokens), lambda p: (p, 0, 0)),
        ),
        out_shape=(shape_of((tokens, width), f32), shape_of((heads, 1, tokens), f32)),
        scratch_shapes=[
            pltpu.VMEM((seq, tokens), f32),
            pltpu.VMEM((seq, tokens), bf16),
            pltpu.VMEM((tile, window), f32),
        ],
        compiler_params=params(),
        cost_estimate=cost(16 * heads * tokens * seq * tile, 4 * seq * width),
        name="attend",
    )(queries, keys, values, bias, mask)


def unskewed(total):
    window = total.shape[1]
    rows = total.shape[0]
    while rows > 8:
        rows = rows // 2
        total = total[:rows, :] + pltpu.roll(total[rows:, :], window - rows, 1)
    step = 4
    while step:
        moved = pltpu.roll(pltpu.roll(total, 8 - step, 0), window - step, 1)
        total = total + moved
        step = step // 2
    return total[0:1, :]


def attend_back_call(queries, keys, values, bias, mask, lse, context, grad_context, bucket_window, buckets, head_dim, first, pairs):
    tokens, width = queries.shape
    seq = keys.shape[0]
    heads, _, window = bias.shape
    per_step = heads // (width // tile)
    key_blocks = seq // tile
    scale = head_dim**-0.5

    def kernel(
        q_ref, k_ref, v_ref, bias_ref, mask_ref, lse_ref, ctx_ref, grad_ref, bucket_ref,
        dq_ref, dk_ref, dv_ref, table_ref, prob_ref, ds_ref, skew_ref, sum_ref,
    ):
        lane = lax.broadcasted_iota(jnp.int32, (tokens, tile), 1)
        row = lax.broadcasted_iota(jnp.int32, (tile, tokens), 0)
        query = q_ref[...]
        grad = grad_ref[...]
        keys_t = k_ref[...].T
        products = (grad.astype(f32) * ctx_ref[...]).T
        result = jnp.zeros((tile, tokens), f32)
        numbers = lax.broadcasted_iota(jnp.int32, (buckets, window), 0)
        hot = (numbers == bucket_ref[...]).astype(f32)
        mine_q, mine_g = [], []
        for half in range(per_step):
            mine_q.append(jnp.where(lane // head_dim == half, query, jnp.zeros_like(query)))
            mine_g.append(jnp.where(lane // head_dim == half, grad, jnp.zeros_like(grad)))
        for half in range(per_step):
            delta = jnp.sum(
                products[half * head_dim : (half + 1) * head_dim, :], axis=0, keepdims=True
            )
            lse_row = lse_ref[half]
            skew_ref[...] = skewed(bias_ref[half], window)
            sum_ref[...] = jnp.zeros((tile, window), f32)
            cols = slice(half * tokens, (half + 1) * tokens)
            for block in range(key_blocks):
                rows = pl.ds(block * tile, tile)
                begin = tile * (key_blocks - block)
                scores = mm_t(k_ref[rows, :], mine_q[half]) * (scale * log2e)
                scores = scores + (skew_ref[:, begin : begin + tokens] + mask_ref[rows, :])
                probs = jnp.exp2(scores - lse_row)
                grad_probs = mm_t(v_ref[rows, :], mine_g[half])
                grad_scores = (probs * (grad_probs - delta)).astype(bf16)
                prob_ref[rows, cols] = probs.astype(bf16)
                ds_ref[rows, cols] = grad_scores
                sum_ref[:, begin : begin + tokens] += grad_scores.astype(f32)
            grad_q = mm(keys_t, ds_ref[:, cols])
            result = jnp.where(row // head_dim == half, grad_q, result)
            by_distance = unskewed(sum_ref[...])
            column = jnp.sum(hot * by_distance, axis=1, keepdims=True)
            table_ref[half] = jnp.broadcast_to(column, (buckets, tile)).T[0:1, :]
        dq_ref[...] = (result * scale).T.astype(bf16)
        dk_ref[...] = (mm(ds_ref[...], jnp.concatenate(mine_q, axis=0)) * scale).astype(bf16)
        dv_ref[...] = mm(prob_ref[...], jnp.concatenate(mine_g, axis=0)).astype(bf16)

    narrow = pl.BlockSpec((tokens, tile), lambda p: (0, p + first))
    tall = pl.BlockSpec((seq, tile), lambda p: (0, p + first))
    narrow_out = pl.BlockSpec((tokens, tile), lambda p: (0, p))
    tall_out = pl.BlockSpec((seq, tile), lambda p: (0, p))
    return pl.pallas_call(
        kernel,
        grid=(pairs,),
        in_specs=[
            narrow,
            tall,
            tall,
            pl.BlockSpec((per_step, 1, window), lambda p: (p + first, 0, 0)),
            pl.BlockSpec((seq, tokens), lambda p: (0, 0)),
            pl.BlockSpec((per_step, 1, tokens), lambda p: (p + first, 0, 0)),
            narrow,
            narrow,
            pl.BlockSpec((1, window), lambda p: (0, 0)),
        ],
        out_specs=(
            narrow_out,
            tall_out,
            tall_out,
            pl.BlockSpec((per_step, 1, buckets), lambda p: (p, 0, 0)),
        ),
        out_shape=(
            shape_of((tokens, pairs * tile), bf16),
            shape_of((seq, pairs * tile), bf16),
            shape_of((seq, pairs * tile), bf16),
            shape_of((pairs * per_step, 1, buckets), f32),
        ),
        scratch_shapes=[
            pltpu.VMEM((seq, per_step * tokens), bf16),
            pltpu.VMEM((seq, per_step * tokens), bf16),
            pltpu.VMEM((tile, window), f32),
            pltpu.VMEM((tile, window), f32),
        ],
        compiler_params=params(),
        cost_estimate=cost(40 * pairs * per_step * tokens * seq * tile, 8 * seq * pairs * tile),
        name="attend_back",
    )(queries, keys, values, bias, mask, lse, context, grad_context, bucket_window)


def chosen_logits(routes, logits):
    numbers = lax.broadcasted_iota(jnp.int32, logits.shape, 1)
    hot0 = routes[:, 0:1] == numbers
    hot1 = routes[:, 1:2] == numbers
    return hot0, hot1


def dispatch_call(me, context, out_blocks, tokens_in, smalls, routes, slot_map, heads):
    tokens, width = tokens_in.shape
    count = len(out_blocks)
    shards = out_blocks[0].shape[0]
    slots = slot_map.shape[0]

    def make(experts):
        def kernel(me_ref, ctx_ref, *refs):
            block_refs = refs[:count]
            (x_ref, small_ref, routes_ref, map_ref, wo_ref, low_ref, res_ref, ffn_ref, gate_ref, rows_ref) = refs[count:]
            for offset in range(count):
                place = lax.bitwise_xor(me_ref[0], offset)
                wo_ref[pl.ds(pl.multiple_of(place * shards, shards), shards), :] = block_refs[offset][...]
            context_low = ctx_ref[...].astype(bf16)
            low_ref[...] = context_low
            residual = x_ref[...].astype(f32) + mm(context_low, wo_ref[...])
            res_ref[...] = residual
            gain = small_ref[experts + heads + 1 : experts + heads + 2, :]
            inverse = lax.rsqrt(jnp.mean(residual * residual, axis=-1, keepdims=True) + eps)
            ffn_low = (residual * inverse * gain).astype(bf16)
            ffn_ref[...] = ffn_low
            rows_ref[...] = mm(map_ref[...], ffn_low).astype(bf16)
            logits = mm_t(ffn_low, small_ref[0:experts, :].astype(bf16))
            hot0, hot1 = chosen_logits(routes_ref[...], logits)
            first = jnp.sum(jnp.where(hot0, logits, 0.0), axis=1, keepdims=True)
            second = jnp.sum(jnp.where(hot1, logits, 0.0), axis=1, keepdims=True)
            top = jnp.maximum(first, second)
            weight0 = jnp.exp(first - top)
            weight1 = jnp.exp(second - top)
            whole = weight0 + weight1
            gate0 = weight0 / whole
            gate1 = weight1 / whole
            gate_ref[...] = jnp.concatenate([gate0, gate1], axis=1)

        return kernel

    def run(experts):
        vmem = pl.BlockSpec(memory_space=pltpu.VMEM)
        return pl.pallas_call(
            make(experts),
            in_specs=[pl.BlockSpec(memory_space=pltpu.SMEM)] + [vmem] * (count + 5),
            out_shape=(
                shape_of((width, width), bf16),
                shape_of((tokens, width), bf16),
                shape_of((tokens, width), f32),
                shape_of((tokens, width), bf16),
                shape_of((tokens, 2), f32),
                shape_of((slots, width), bf16),
            ),
            compiler_params=params(),
            cost_estimate=cost(4 * tokens * width * width, 8 * width * width),
            name="dispatch",
        )(me, context, *out_blocks, tokens_in, smalls, routes, slot_map)

    return run


def upstream_call(grads, expert_out):
    count, width = grads.shape
    hidden_width = expert_out.shape[0]
    step_width = 512

    def kernel(g_ref, out_ref, up_ref):
        up_ref[...] = mm_t(g_ref[...], out_ref[...])

    return pl.pallas_call(
        kernel,
        grid=(hidden_width // step_width,),
        in_specs=[whole_spec((count, width)), pl.BlockSpec((step_width, width), lambda s: (s, 0))],
        out_specs=pl.BlockSpec((count, step_width), lambda s: (0, s)),
        out_shape=shape_of((count, hidden_width), f32),
        compiler_params=params(),
        cost_estimate=cost(2 * count * width * hidden_width, 6 * count * hidden_width),
        name="upstream",
    )(grads, expert_out)


def expert_call(rows, grads, upstream, expert_in, expert_out, experts):
    count, width = rows.shape
    capacity = count // experts
    stride = capacity + extra_rows
    hidden_width = expert_in.shape[1]
    step_width = 512
    chunk_rows = count
    steps = hidden_width // step_width
    half_root = math.sqrt(0.5)
    density = 1.0 / math.sqrt(2.0 * math.pi)

    def kernel(x_ref, g_ref, up_ref, in_ref, out_ref, active_ref, gh_ref, made_ref, back_ref, made_sum, back_sum):
        step = pl.program_id(0)

        @pl.when(step == 0)
        def start():
            made_sum[...] = jnp.zeros((count, width), f32)
            back_sum[...] = jnp.zeros((count, width), f32)

        @pl.loop(0, count // chunk_rows)
        def chunk(index):
            at = pl.ds(pl.multiple_of(index * chunk_rows, chunk_rows), chunk_rows)
            hidden = mm(x_ref[at, :], in_ref[...])
            share = 0.5 + 0.5 * lax.erf(hidden * half_root)
            active = (hidden * share).astype(bf16)
            slope = share + hidden * (jnp.exp(hidden * hidden * -0.5) * density)
            grad_hidden = (up_ref[at, :] * slope).astype(bf16)
            active_ref[at, :] = active
            gh_ref[at, :] = grad_hidden
            made_sum[at, :] += mm(active, out_ref[...])
            back_sum[at, :] += mm_t(grad_hidden, in_ref[...])

        @pl.when(step == steps - 1)
        def finish():
            made = made_sum[...].astype(bf16)
            made_ref[...] = made
            products = made.astype(f32) * g_ref[...].astype(f32)
            folded = products[:, :tile]
            for at in range(tile, width, tile):
                folded = folded + products[:, at : at + tile]
            dots = jnp.broadcast_to(jnp.sum(folded.T, axis=0, keepdims=True), (8, count))
            coarse = dots.astype(bf16).astype(f32)
            fine = dots - coarse
            for expert in range(experts):
                at = expert * capacity
                shift = (count - at) % count
                lanes = [pltpu.roll(half, shift, 1)[:, :tile] for half in (coarse, fine)]
                lanes = jnp.concatenate(lanes, axis=0)
                lanes = jnp.concatenate([lanes, jnp.zeros((extra_rows, width - tile), f32)], axis=1)
                back_ref[expert, :capacity, :] = back_sum[at : at + capacity, :].astype(bf16)
                back_ref[expert, capacity:, :] = lanes.astype(bf16)

    full = whole_spec((count, width))
    return pl.pallas_call(
        kernel,
        grid=(steps,),
        in_specs=[
            full,
            full,
            pl.BlockSpec((count, step_width), lambda s: (0, s)),
            pl.BlockSpec((width, step_width), lambda s: (0, s)),
            pl.BlockSpec((step_width, width), lambda s: (s, 0)),
        ],
        out_specs=(
            pl.BlockSpec((count, step_width), lambda s: (0, s)),
            pl.BlockSpec((count, step_width), lambda s: (0, s)),
            full,
            whole_spec((experts, stride, width)),
        ),
        out_shape=(
            shape_of((count, hidden_width), bf16),
            shape_of((count, hidden_width), bf16),
            shape_of((count, width), bf16),
            shape_of((experts, stride, width), bf16),
        ),
        scratch_shapes=[pltpu.VMEM((count, width), f32), pltpu.VMEM((count, width), f32)],
        compiler_params=params(),
        cost_estimate=cost(8 * count * width * hidden_width, 8 * width * hidden_width),
        name="experts",
    )(rows, grads, upstream, expert_in, expert_out)


def offset_place(offsets, step, me_ref):
    offset = offsets[0]
    for at in range(1, len(offsets)):
        offset = jnp.where(step == at, offsets[at], offset)
    return lax.bitwise_xor(me_ref[0], offset)


def gate_column(me_ref, rows_ref, router_ref, others_ref):
    logits = mm_t(router_ref[...].astype(bf16), rows_ref[...])
    numbers = lax.broadcasted_iota(jnp.int32, logits.shape, 0).astype(f32)
    mine = jnp.sum(jnp.where(numbers == me_ref[1].astype(f32), logits, 0.0), axis=0, keepdims=True)
    other = jnp.sum(
        jnp.where(numbers == others_ref[...].astype(f32), logits, 0.0), axis=0, keepdims=True
    )
    return to_column(1.0 / (1.0 + jnp.exp(other - mine)))[:, 0:1]


def expert_grads_call(me, rows_t, rows_in, grads, active, grad_hidden, router, others, offsets):
    width, rows = rows_t.shape
    hidden_width = grad_hidden.shape[1]
    count = len(offsets)
    half = count // 2
    in_rows, out_rows = width // count, hidden_width // count

    def kernel(
        me_ref, xt_ref, rows_ref, g_ref, active_ref, gh_ref, router_ref, others_ref,
        in_give_ref, in_keep_ref, out_give_ref, out_keep_ref, gh_scr, g_scr,
    ):
        step = pl.program_id(0)

        @pl.when(step == 0)
        def start():
            column = gate_column(me_ref, rows_ref, router_ref, others_ref)
            g_scr[...] = (g_ref[...].astype(f32) * column).astype(bf16)
            for at in range(0, hidden_width, width):
                gh_scr[:, at : at + width] = (gh_ref[:, at : at + width].astype(f32) * column).astype(bf16)

        def shard(in_ref, out_ref):
            for at in range(0, hidden_width, width):
                in_ref[0, :, at : at + width] = mm(xt_ref[...], gh_scr[:, at : at + width]).astype(bf16)
            out_ref[0] = t_mm(active_ref[...], g_scr[...]).astype(bf16)

        @pl.when(step < half)
        def first():
            shard(in_give_ref, out_give_ref)

        @pl.when(step >= half)
        def second():
            shard(in_keep_ref, out_keep_ref)

    def give_at(s, me_ref):
        return (jnp.minimum(s, half - 1), 0, 0)

    def keep_at(s, me_ref):
        return (jnp.maximum(s - half, 0), 0, 0)

    return pl.pallas_call(
        kernel,
        grid_spec=pltpu.PrefetchScalarGridSpec(
            num_scalar_prefetch=1,
            grid=(count,),
            in_specs=[
                pl.BlockSpec((in_rows, rows), lambda s, me_ref: (offset_place(offsets, s, me_ref), 0)),
                whole_spec((rows, width)),
                whole_spec((rows, width)),
                pl.BlockSpec((rows, out_rows), lambda s, me_ref: (0, offset_place(offsets, s, me_ref))),
                whole_spec((rows, hidden_width)),
                whole_spec(router.shape),
                whole_spec((1, rows)),
            ],
            out_specs=(
                pl.BlockSpec((1, in_rows, hidden_width), give_at),
                pl.BlockSpec((1, in_rows, hidden_width), keep_at),
                pl.BlockSpec((1, out_rows, width), give_at),
                pl.BlockSpec((1, out_rows, width), keep_at),
            ),
            scratch_shapes=[pltpu.VMEM((rows, hidden_width), bf16), pltpu.VMEM((rows, width), bf16)],
        ),
        out_shape=(
            shape_of((half, in_rows, hidden_width), bf16),
            shape_of((half, in_rows, hidden_width), bf16),
            shape_of((half, out_rows, width), bf16),
            shape_of((half, out_rows, width), bf16),
        ),
        compiler_params=params(),
        cost_estimate=cost(4 * rows * width * hidden_width, 8 * width * hidden_width),
        name="expert_grads",
    )(me, rows_t, rows_in, grads, active, grad_hidden, router, others)


def combine_call(experts, heads, rows, places, gates, routes, cotangent, residual, ffn_low, smalls, w_output):
    tokens, width = cotangent.shape
    stride = rows.shape[1]
    capacity = stride - extra_rows

    def kernel(
        rows_ref, place_ref, gate_ref, routes_ref, cot_ref, res_ref, ffn_ref, small_ref, wo_ref,
        grad_res_ref, branch_ref, ctx_ref, router_ref, gain_ref,
    ):
        gate0, gate1 = gate_ref[:, 0:1], gate_ref[:, 1:2]
        lane_row = lax.broadcasted_iota(jnp.int32, (tokens, stride * experts), 1).astype(f32)
        rows = rows_ref[...].reshape(stride * experts, width)
        lane_slot = lax.broadcasted_iota(jnp.int32, (tokens, tile), 1).astype(f32)
        grad_ffn = jnp.zeros((tokens, width), f32)
        grad_gate = []
        for k, gate in enumerate((gate0, gate1)):
            first_row = routes_ref[:, k : k + 1].astype(f32) * stride
            place = place_ref[:, k : k + 1]
            back = (lane_row == first_row + place).astype(f32).astype(bf16)
            grad_ffn = grad_ffn + mm(back, rows) * gate
            coarse = (lane_row == first_row + capacity).astype(f32)
            fine = (lane_row == first_row + (capacity + 8)).astype(f32)
            dots = mm((coarse + fine).astype(bf16), rows[:, :tile])
            grad_gate.append(jnp.sum(jnp.where(lane_slot == place, dots, 0.0), axis=1, keepdims=True))
        grad_gate0, grad_gate1 = grad_gate
        mean_grad = gate0 * grad_gate0 + gate1 * grad_gate1
        chosen0 = gate0 * (grad_gate0 - mean_grad)
        chosen1 = gate1 * (grad_gate1 - mean_grad)
        numbers = lax.broadcasted_iota(jnp.int32, (tokens, experts), 1)
        hot0 = routes_ref[:, 0:1] == numbers
        hot1 = routes_ref[:, 1:2] == numbers
        grad_logits = jnp.where(hot0, chosen0, 0.0) + jnp.where(hot1, chosen1, 0.0)
        grad_logits = grad_logits.astype(bf16)
        router_ref[...] = t_mm(grad_logits, ffn_ref[...])
        grad_ffn = grad_ffn + mm(grad_logits, small_ref[0:experts, :].astype(bf16))
        gain = small_ref[experts + heads + 1 : experts + heads + 2, :]
        residual = res_ref[...]
        inverse = lax.rsqrt(jnp.mean(residual * residual, axis=-1, keepdims=True) + eps)
        scaled = grad_ffn * gain
        inner = jnp.mean(scaled * residual, axis=-1, keepdims=True)
        gain_ref[...] = jnp.sum(grad_ffn * residual * inverse, axis=0, keepdims=True)
        grad_res = cot_ref[...].astype(f32) + inverse * scaled - residual * (inverse * inverse * inverse * inner)
        grad_res_ref[...] = grad_res
        branch = grad_res.astype(bf16)
        branch_ref[...] = branch
        ctx_ref[...] = mm_t(branch, wo_ref[...]).astype(bf16)

    return pl.pallas_call(
        kernel,
        out_shape=(
            shape_of((tokens, width), f32),
            shape_of((tokens, width), bf16),
            shape_of((tokens, width), bf16),
            shape_of((experts, width), f32),
            shape_of((1, width), f32),
        ),
        compiler_params=params(),
        cost_estimate=cost(6 * tokens * width * width, 8 * width * width),
        name="combine",
    )(rows, places, gates, routes, cotangent, residual, ffn_low, smalls, w_output)


def split_rows(full_ref, me_index, count, shards, main, give_ref, keep_ref):
    for offset in range(count):
        place = lax.bitwise_xor(me_index, offset)
        target = give_ref if offset & 1 else keep_ref
        target[offset // 2, :, :main] = full_ref[
            pl.ds(pl.multiple_of(place * shards, shards), shards), :
        ].astype(bf16)


def small_tiles(pieces, rows, shards):
    per_tile = shards // rows
    return -(-pieces // per_tile), per_tile


def first_grads_call(me, dq, dk, dv, normed_t, context_low, branch, grad_router, grad_gain, table, count):
    tokens, part = dq.shape
    width, seq = normed_t.shape
    shards = width // count
    experts = grad_router.shape[0]
    heads, _, buckets = table.shape
    piece_rows = -(-(experts + 1) // 16) * 16
    pieces = width // tile + 1
    tiles, per_tile = small_tiles(pieces, piece_rows, shards)
    main = width + 3 * part

    def kernel(
        me_ref, dq_ref, dk_ref, dv_ref, normed_ref, ctx_ref, branch_ref, router_ref, gain_ref, table_ref,
        give_ref, keep_ref, full_ref,
    ):
        own = pl.ds(pl.multiple_of(me_ref[0] * tokens, tokens), tokens)
        full_ref[:, :width] = t_mm(ctx_ref[...], branch_ref[...])
        full_ref[:, width : width + part] = mm(normed_ref[:, own], dq_ref[...])
        full_ref[:, width + part : width + 2 * part] = mm(normed_ref[...], dk_ref[...])
        full_ref[:, width + 2 * part :] = mm(normed_ref[...], dv_ref[...])
        split_rows(full_ref, me_ref[0], count, shards, main, give_ref, keep_ref)
        small = jnp.concatenate(
            [router_ref[...], gain_ref[...], jnp.zeros((piece_rows - experts - 1, width), f32)], axis=0
        )
        rows = [table_ref[head] for head in range(heads)]
        rows = jnp.concatenate(rows + [jnp.zeros((piece_rows - heads, buckets), f32)], axis=0)
        rows = jnp.concatenate([rows, jnp.zeros((piece_rows, tile - buckets), f32)], axis=1)
        blocks = [small[:, at : at + tile] for at in range(0, width, tile)] + [rows]
        blocks = [block.astype(bf16) for block in blocks]
        for target in (give_ref, keep_ref):
            for at in range(count // 2):
                target[at, :, main:] = jnp.zeros((shards, tiles * tile), bf16)
                for index, block in enumerate(blocks):
                    row = index % per_tile * piece_rows
                    col = main + index // per_tile * tile
                    target[at, row : row + piece_rows, col : col + tile] = block

    vmem = pl.BlockSpec(memory_space=pltpu.VMEM)
    return pl.pallas_call(
        kernel,
        in_specs=[pl.BlockSpec(memory_space=pltpu.SMEM)] + [vmem] * 9,
        out_shape=(shape_of((count // 2, shards, main + tiles * tile), bf16),) * 2,
        scratch_shapes=[pltpu.VMEM((width, main), f32)],
        compiler_params=params(),
        cost_estimate=cost(5 * seq * width * part, 10 * seq * width),
        name="first_grads",
    )(me, dq, dk, dv, normed_t, context_low, branch, grad_router, grad_gain, table)


def first_smalls(columns, experts, heads, buckets, width, shards):
    piece_rows = -(-(experts + 1) // 16) * 16
    pieces = width // tile + 1
    _, per_tile = small_tiles(pieces, piece_rows, shards)
    found = []
    for index in range(pieces):
        row, col = index % per_tile * piece_rows, index // per_tile * tile
        found.append(columns[row : row + piece_rows, col : col + tile])
    wide = jnp.concatenate(found[:-1], axis=1)
    return wide[:experts], wide[experts], found[-1][:heads, :buckets]


def second_grads_call(me, dq, dk, dv, normed_t, table, count):
    tokens, part = dq.shape
    width, seq = normed_t.shape
    shards = width // count
    heads, _, buckets = table.shape
    main = 3 * part

    def kernel(me_ref, dq_ref, dk_ref, dv_ref, normed_ref, table_ref, give_ref, keep_ref, full_ref):
        own = pl.ds(pl.multiple_of(me_ref[0] * tokens, tokens), tokens)
        full_ref[:, :part] = mm(normed_ref[:, own], dq_ref[...])
        full_ref[:, part : 2 * part] = mm(normed_ref[...], dk_ref[...])
        full_ref[:, 2 * part :] = mm(normed_ref[...], dv_ref[...])
        split_rows(full_ref, me_ref[0], count, shards, main, give_ref, keep_ref)
        rows = [table_ref[head] for head in range(heads)]
        rows = jnp.concatenate(rows + [jnp.zeros((16 - heads, buckets), f32)], axis=0)
        rows = jnp.concatenate([rows, jnp.zeros((16, tile - buckets), f32)], axis=1).astype(bf16)
        for target in (give_ref, keep_ref):
            for at in range(count // 2):
                target[at, :, main:] = jnp.zeros((shards, tile), bf16)
                target[at, :16, main:] = rows

    vmem = pl.BlockSpec(memory_space=pltpu.VMEM)
    return pl.pallas_call(
        kernel,
        in_specs=[pl.BlockSpec(memory_space=pltpu.SMEM)] + [vmem] * 5,
        out_shape=(shape_of((count // 2, shards, main + tile), bf16),) * 2,
        scratch_shapes=[pltpu.VMEM((width, main), f32)],
        compiler_params=params(),
        cost_estimate=cost(5 * seq * width * part, 10 * seq * width),
        name="second_grads",
    )(me, dq, dk, dv, normed_t, table)


def rows_back_call(me, first, second, weights, count):
    tokens, part = first[0].shape
    width = weights[0].shape[0]

    def kernel(
        me_ref, dq1_ref, dk1_ref, dv1_ref, dq2_ref, dk2_ref, dv2_ref, wq_ref, wk_ref, wv_ref, give_ref, keep_ref,
    ):
        for offset in range(count):
            place = lax.bitwise_xor(me_ref[0], offset)
            at = pl.ds(pl.multiple_of(place * tokens, tokens), tokens)
            total = mm_t(dk1_ref[at, :], wk_ref[:, :part]) + mm_t(dk2_ref[at, :], wk_ref[:, part:])
            total = total + mm_t(dv1_ref[at, :], wv_ref[:, :part]) + mm_t(dv2_ref[at, :], wv_ref[:, part:])
            if offset == 0:
                total = total + mm_t(dq1_ref[...], wq_ref[:, :part]) + mm_t(dq2_ref[...], wq_ref[:, part:])
            target = give_ref if offset & 1 else keep_ref
            target[offset // 2] = total.astype(bf16)

    vmem = pl.BlockSpec(memory_space=pltpu.VMEM)
    return pl.pallas_call(
        kernel,
        in_specs=[pl.BlockSpec(memory_space=pltpu.SMEM)] + [vmem] * 9,
        out_shape=(shape_of((count // 2, tokens, width), bf16),) * 2,
        compiler_params=params(),
        cost_estimate=cost(10 * count * tokens * width * width, 10 * count * tokens * width),
        name="rows_back",
    )(me, *first, *second, *weights)


def finish_call(chain1, chain2, weights, gain, half_cols):
    shards, width = weights[0].shape
    rest = width - half_cols

    def kernel(c1_ref, c2_ref, wq_ref, wk_ref, wv_ref, gain_ref, gq_ref, gk_ref, gv_ref, go_ref, out_ref):
        total = jnp.zeros((shards, 1), f32)
        go_ref[...] = c1_ref[:, :width].astype(f32)
        for part, (weight_ref, grad_ref) in enumerate(((wq_ref, gq_ref), (wk_ref, gk_ref), (wv_ref, gv_ref))):
            left = c1_ref[:, width + part * half_cols : width + (part + 1) * half_cols].astype(f32)
            right = c2_ref[:, part * rest : (part + 1) * rest].astype(f32)
            grad_ref[:, :half_cols] = left
            grad_ref[:, half_cols:] = right
            weight = weight_ref[...].astype(f32)
            total = total + jnp.sum(left * weight[:, :half_cols], axis=1, keepdims=True)
            total = total + jnp.sum(right * weight[:, half_cols:], axis=1, keepdims=True)
        out_ref[...] = jnp.broadcast_to(total, (shards, tile)).T[0:1, :] / gain_ref[...].astype(f32)

    return pl.pallas_call(
        kernel,
        out_shape=(shape_of((shards, width), f32),) * 4 + (shape_of((1, shards), f32),),
        compiler_params=params(),
        cost_estimate=cost(6 * shards * width, 30 * shards * width),
        name="finish",
    )(chain1, chain2, *weights, gain[None, :])


def gather_blocks(value, axis_size, late=None):
    blocks = {0: value}
    bit = 2
    while bit < axis_size:
        for offset in sorted(blocks):
            blocks[offset | bit] = swap(blocks[offset], "fsdp", axis_size, bit)
            if late is not None:
                blocks[offset | bit] = ordered(blocks[offset | bit], late)[0]
        bit *= 2
    for offset in sorted(blocks):
        blocks[offset | 1] = swap(blocks[offset], "fsdp", axis_size, 1)
    return [blocks[offset] for offset in range(axis_size)]


def scatter_bits(axis_size):
    bits, bit = [1], axis_size // 2
    while bit > 1:
        bits.append(bit)
        bit //= 2
    return [bit for bit in bits if bit < axis_size]


def added(left_side, right_side):
    return left_side.astype(f32) + right_side.astype(f32)


def core_sum(given, kept, axis_size):
    arrived = swap(given, "fsdp", axis_size, 1)
    return {2 * at: added(kept[at], arrived[at]).astype(bf16) for at in range(axis_size // 2)}


def far_sum(pieces, axis_size, early=None, late=None, cuts=1):
    for bit in scatter_bits(axis_size):
        if bit == 1:
            continue
        left = {}
        for offset in sorted(pieces):
            if offset & bit:
                continue
            found = []
            for leaving in jnp.split(pieces[offset | bit].astype(bf16), cuts, axis=0):
                if early is not None:
                    leaving = ordered(leaving, early)[0]
                found.append(swap(leaving, "fsdp", axis_size, bit))
                early = found[-1]
            if late is not None:
                found[-1] = ordered(found[-1], late)[0]
            left[offset] = added(pieces[offset], jnp.concatenate(found, axis=0))
        pieces = left
    return pieces[0]


def far_steps(pieces, axis_size, fractions, early=None):
    bits = [bit for bit in scatter_bits(axis_size) if bit > 1]
    for bit in bits[:-1]:
        pieces = {
            offset: added(
                pieces[offset], swap(pieces[offset | bit].astype(bf16), "fsdp", axis_size, bit)
            )
            for offset in sorted(pieces)
            if not offset & bit
        }
    bit = bits[-1]
    rows = pieces[0].shape[0]
    leaving = pieces[bit].astype(bf16)
    found, begin = [], 0
    for step, fraction in enumerate(fractions):
        end = rows if step == len(fractions) - 1 else begin + rows * fraction // 12
        part = leaving[begin:end]
        if early is not None:
            part = ordered(part, early)[0]
        early = yield swap(part, "fsdp", axis_size, bit)
        found.append(early)
        begin = end
    yield added(pieces[0], jnp.concatenate(found, axis=0))


def all_sum_expert(value, axis_size, index, before_last=None):
    rows = value.shape[0]
    parts = jnp.pad(value.astype(bf16), ((0, -rows % (axis_size // 2)), (0, 0)))
    bit, bits = 1, []
    while bit < axis_size:
        bits.append(bit)
        bit *= 2
    inner = bits.pop()
    first_arrived = None
    for bit in bits:
        low_half, high_half = jnp.split(parts, 2, axis=0)
        upper = (index & bit) != 0
        keep = jnp.where(upper, high_half, low_half)
        give = jnp.where(upper, low_half, high_half)
        arrived = swap(give, "expert", axis_size, bit)
        first_arrived = arrived if first_arrived is None else first_arrived
        parts = added(keep, arrived).astype(bf16)
    parts = added(parts, swap(parts, "expert", axis_size, inner)).astype(bf16)
    for bit in reversed(bits):
        if bit == 1 and before_last is not None:
            parts = ordered(parts, before_last)[0]
        other = swap(parts, "expert", axis_size, bit)
        upper = (index & bit) != 0
        parts = jnp.concatenate(
            [jnp.where(upper, other, parts), jnp.where(upper, parts, other)], axis=0
        )
    return parts[:rows], first_arrived


def ordered(*values):
    return lax.optimization_barrier(values)


def build(count, expert_ranks):
    def per_device(
        tokens_in,
        seg_ids,
        routes,
        buckets,
        attn_gain,
        w_query,
        w_key,
        w_value,
        w_output,
        bias_table,
        ffn_gain,
        w_router,
        w_in,
        w_out,
        cotangent,
    ):
        tokens, width = tokens_in.shape
        shards, experts = w_router.shape
        bucket_rows, heads = bias_table.shape
        bucket_count = bucket_rows * count
        head_dim = width // heads
        seq = buckets.shape[0]
        top_count = routes.shape[1]
        capacity = 3 * top_count * tokens // (2 * experts)
        slots = experts * capacity
        fsdp_index = lax.axis_index("fsdp")
        expert_index = lax.axis_index("expert")
        me = jnp.stack([fsdp_index, expert_index]).astype(jnp.int32)

        used = experts + heads + 3
        small_rows = -(-used // 16) * 16
        packed = pack_call(
            me, (w_query, w_key, w_value), tokens_in, seg_ids[None, :],
            jnp.stack([attn_gain, ffn_gain]), bias_table, w_router.T, small_rows, width,
        )
        blocks = gather_blocks(packed, count)
        leaving_output = ordered(w_output, blocks[-2])[0]
        routes, blocks[1] = ordered(routes, blocks[1])
        padded_buckets = jnp.concatenate([jnp.full((seq,), -1, jnp.int32), buckets])
        bucket_window = lax.dynamic_slice_in_dim(
            padded_buckets, fsdp_index * tokens, seq + tokens, 0
        )[None, :]

        slot_map, back0, back1, grad_rows_out, places = route_call(routes, cotangent, capacity, experts)
        grad_rows_in = lax.all_to_all(
            grad_rows_out, "expert", split_axis=0, concat_axis=0, tiled=True
        )
        others = grad_rows_in[:, capacity, :capacity].reshape(1, slots)
        grad_rows_in = grad_rows_in[:, :capacity, :].reshape(slots, width)

        (queries, keys, values, normed, sequence, wq, wk, wv, smalls, bias, mask) = project_call(
            me, blocks, shards, small_rows, bucket_window, heads, bucket_count, experts
        )
        out_blocks = gather_blocks(leaving_output, count, queries)
        queries, grad_rows_in, others = ordered(queries, grad_rows_in, others)
        context, lse = attend_call(queries, keys, values, bias, mask, head_dim)
        wo, context_low, residual, ffn_low, gates, rows_out = dispatch_call(
            me, context, out_blocks, tokens_in, smalls, routes, slot_map, heads
        )(experts)
        normed_t = ordered(normed, rows_out)[0].T
        upstream = upstream_call(ordered(grad_rows_in, rows_out)[0], w_out[0])
        rows_in = lax.all_to_all(
            rows_out.reshape(experts, capacity, width),
            "expert",
            split_axis=0,
            concat_axis=0,
            tiled=True,
        ).reshape(slots, width)
        rows_in, normed_t, upstream = ordered(rows_in, normed_t, upstream)
        active, grad_hidden, made, row_grads = expert_call(
            rows_in, grad_rows_in, upstream, w_in[0], w_out[0], experts
        )
        row_grads_back = lax.all_to_all(
            row_grads, "expert", split_axis=0, concat_axis=0, tiled=True
        )

        rows_t = rows_in.T
        give = [offset for offset in range(count) if offset & 1]
        keep = [offset for offset in range(count) if not offset & 1]
        router = smalls[:experts]
        in_give, in_keep, out_give, out_keep = expert_grads_call(
            me, rows_t, rows_in, grad_rows_in, active, grad_hidden, router, others, give + keep
        )
        in_give, out_give, row_grads_back = ordered(in_give, out_give, row_grads_back)
        in_pieces = core_sum(in_give, in_keep, count)
        out_pieces = core_sum(out_give, out_keep, count)

        grad_residual, branch, grad_context, grad_router, grad_gain_ffn = combine_call(
            experts, heads, row_grads_back, places, gates, routes, cotangent,
            residual, ffn_low, smalls, wo,
        )
        pairs = width // tile
        near = pairs // 2
        last = max(in_pieces)
        grad_context, in_pieces[last] = ordered(grad_context, in_pieces[last])
        *part1, table1 = attend_back_call(
            queries, keys, values, bias, mask, lse, context, grad_context, bucket_window,
            bucket_count, head_dim, 0, near,
        )
        in_steps = far_steps(in_pieces, count, (5, 3, 4))
        arrived = next(in_steps)
        part1[0], arrived = ordered(part1[0], arrived)
        give1, keep1 = first_grads_call(
            me, *part1, normed_t, context_low, branch, grad_router, grad_gain_ffn, table1, count
        )
        arrived = in_steps.send(arrived)
        made = ordered(made, give1)[0]
        made_back = lax.all_to_all(
            made.reshape(experts, capacity, width),
            "expert",
            split_axis=0,
            concat_axis=0,
            tiled=True,
        ).reshape(slots, width)
        pieces1 = core_sum(give1, keep1, count)
        last = max(pieces1)
        grad_context, pieces1[last], arrived = ordered(grad_context, pieces1[last], arrived)
        *part2, table2 = attend_back_call(
            queries, keys, values, bias, mask, lse, context, grad_context, bucket_window,
            bucket_count, head_dim, near, pairs - near,
        )
        give2, keep2 = second_grads_call(me, *part2, normed_t, table2, count)
        sum1 = far_sum(pieces1, count, None, give2)
        rows_give, rows_keep = rows_back_call(me, part1, part2, (wq, wk, wv), count)
        sum2 = far_sum(core_sum(give2, keep2, count), count)
        arrived = in_steps.send(ordered(arrived, sum1)[0])
        in_sum = in_steps.send(arrived)
        out_steps = far_steps(out_pieces, count, (6, 6), arrived)
        arrived = out_steps.send(ordered(next(out_steps), sum2)[0])
        out_sum = out_steps.send(arrived)
        grad_shards = [in_sum, out_sum]
        chain1, _ = all_sum_expert(sum1, expert_ranks, expert_index)
        chain2, first_arrived = all_sum_expert(sum2, expert_ranks, expert_index)
        half_cols = near * tile

        grad_normed = far_sum(core_sum(rows_give, rows_keep, count), count, sum2)
        inputs = tokens_in.astype(f32)
        inverse = lax.rsqrt(jnp.mean(inputs * inputs, axis=-1, keepdims=True) + eps)
        gain_attn = smalls[experts + heads]
        scaled = grad_normed * gain_attn
        inner = jnp.mean(scaled * inputs, axis=-1, keepdims=True)
        grad_tokens = grad_residual + inverse * scaled - inputs * inverse**3 * inner

        made_back = ordered(made_back, sum2)[0]
        picked0 = mm(back0, made_back)
        picked1 = mm(back1, made_back)
        block_out = (residual + gates[:, 0:1] * picked0 + gates[:, 1:2] * picked1).astype(bf16)

        rest = width - half_cols
        *shards_out, grad_gain_attn = finish_call(
            chain1, chain2, (w_query, w_key, w_value), attn_gain, half_cols
        )
        router_sum, gain_sum, table_left = first_smalls(
            chain1[:, width + 3 * half_cols :].astype(f32), experts, 2 * near, bucket_count, width, shards
        )
        table_right = chain2[: heads - 2 * near, 3 * rest : 3 * rest + bucket_count].astype(f32)
        table_cols = lax.dynamic_slice_in_dim(
            jnp.concatenate([table_left, table_right], axis=0), fsdp_index * bucket_rows, bucket_rows, 1
        )
        return (
            block_out,
            grad_tokens,
            grad_gain_attn[0],
            shards_out[0],
            shards_out[1],
            shards_out[2],
            shards_out[3],
            table_cols.T,
            lax.dynamic_slice_in_dim(gain_sum, fsdp_index * shards, shards, 0),
            lax.dynamic_slice_in_dim(router_sum, fsdp_index * shards, shards, 1).T,
            grad_shards[0][None],
            grad_shards[1][None],
        )

    return per_device


def solution(mesh):
    return jax.shard_map(
        build(mesh.shape["fsdp"], mesh.shape["expert"]),
        mesh=mesh,
        in_specs=(
            P(("expert", "fsdp"), None),
            P(("expert", "fsdp")),
            P(("expert", "fsdp"), None),
            P(),
            P("fsdp"),
            P("fsdp", None),
            P("fsdp", None),
            P("fsdp", None),
            P("fsdp", None),
            P("fsdp", None),
            P("fsdp"),
            P("fsdp", None),
            P("expert", None, None),
            P("expert", None, None),
            P(("expert", "fsdp"), None),
        ),
        out_specs=(
            P(("expert", "fsdp"), None),
            P(("expert", "fsdp"), None),
            P("fsdp"),
            P("fsdp", None),
            P("fsdp", None),
            P("fsdp", None),
            P("fsdp", None),
            P("fsdp", None),
            P("fsdp"),
            P("fsdp", None),
            P("expert", "fsdp", None),
            P("expert", "fsdp", None),
        ),
        check_vma=False,
    )
```
